32 devices in a mesh: row: 8 (over z, y), col: 4 (over x, core).
Axes of the slice: x: 2, y: 2, z: 4, core: 2. Of those that a mesh axis runs over, the one named last changes fastest.
Arguments:
- orbitals: bfloat16 [32, 64000], P(('row', 'col')), may hold values from -6 to 6
- pair_list: int32 [32, 8, 2], P(('row', 'col')), may hold values from 0 to 7, as said below
- pair_count: int32 [32], P(('row', 'col')), may hold values from 1 to 8
Outputs:
- exchange_fields: float32 [32, 64000], P(('row', 'col'))
The draws below stay inside these ranges and needn't reach their ends.
Inputs may be any that keep to these rules, and one draw needn't show every extreme that they name: pair_list[., ., 0] is below 4 and pair_list[., ., 1] below 8.
All inputs are finite; a program needn't handle non-finite values.
Results may differ from the reference program's by a relative error of at most 0.0004.
Values may be sent and summed in bfloat16 or wider, within the bound.
No kernel may reach another device: no remote copies, remote signals or barrier semaphores. Data moves between devices by JAX's collectives and lax.ppermute only.
A program may use at most 64 MiB of HBM per device.

```python
import jax
import jax.numpy as jnp
from jax import lax

GX = 40
GRID = 64000
BAND_DEV = 1
PAIRS_DEV = 8
BANDS = 32
BLOCK_R = 4
BLOCK_C = 8
N_COL = 4


def draw_pair_list(key, part):
    key = jax.random.fold_in(key, 11)
    devices = BANDS // BAND_DEV
    key_first, key_second = jax.random.split(key)
    firsts = jax.random.randint(key_first, (devices, PAIRS_DEV), 0, BLOCK_R)
    seconds = jax.random.randint(key_second, (devices, PAIRS_DEV), 0, BLOCK_C)
    firsts = firsts.at[0, 0].set(BLOCK_R - 1).at[0, 1].set(0)
    seconds = seconds.at[0, 0].set(BLOCK_C - 1).at[0, 1].set(0)
    return jnp.stack([firsts, seconds], axis=-1).astype(jnp.int32)


def draw_pair_count(key, part):
    key = jax.random.fold_in(key, 23)
    devices = BANDS // BAND_DEV
    row_total = BANDS // BLOCK_R
    row_numbers = jnp.arange(devices, dtype=jnp.int32) // (BLOCK_R // BAND_DEV)
    jitter = jax.random.randint(key, (devices,), 0, 2)
    counts = jnp.maximum(1, PAIRS_DEV - row_numbers * PAIRS_DEV // row_total - jitter)
    counts = counts.at[0].set(PAIRS_DEV).at[devices - 1].set(1)
    return counts.astype(jnp.int32)


def block_scale(own_key, extent, shards, least, high):
    loudness = 1.0
    for axis_at, parts in shards:
        heights = jax.random.uniform(jax.random.fold_in(jax.random.fold_in(own_key, 6), axis_at), (parts,), jnp.float32, least / len(shards), high / len(shards))
        loudness = loudness * jnp.repeat(jnp.exp(heights), extent[axis_at] // parts).reshape((-1,) + (1,) * (len(extent) - 1 - axis_at))
    return loudness


def centred(key, extent, width, reach, cuts=(), kind=jnp.bfloat16):
    factor_of = block_scale(key, extent, cuts, -0.22, 0.18) if cuts else 1.0
    array = jax.random.normal(key, extent, jnp.float32) * width * factor_of
    return jnp.minimum(jnp.maximum(array, -reach), reach).astype(kind)


def setup_inputs(seed: int = 0) -> dict:
    arg_keys = jax.random.split(jax.random.key(seed), 4)
    return {
        "orbitals": centred(arg_keys[0], (BANDS, GRID), 1.0, 6.0, ((0, 32),)),
        "pair_list": draw_pair_list(jax.random.fold_in(arg_keys[3], 71), 0),
        "pair_count": draw_pair_count(jax.random.fold_in(arg_keys[3], 71), 0),
    }


screen_width = 0.9


def kernel_grid():
    frequency = jnp.fft.fftfreq(GX) * (2.0 * jnp.pi)
    squared = frequency * frequency
    squared_sum = squared[:, None, None] + squared[None, :, None] + squared[None, None, :]
    safe_sum = jnp.where(squared_sum > 0, squared_sum, 1.0)
    screened = 4.0 * jnp.pi * (1.0 - jnp.exp(-safe_sum / (4.0 * screen_width ** 2))) / safe_sum
    return jnp.where(squared_sum > 0, screened, jnp.pi / screen_width ** 2).astype(jnp.float32)


def reference(orbitals, pair_list, pair_count):
    device_ids = jnp.arange(BANDS // BAND_DEV, dtype=jnp.int32)
    row_ids = device_ids // N_COL
    col_ids = device_ids % N_COL
    first_index = row_ids[:, None] * BLOCK_R + pair_list[:, :, 0]
    second_local = pair_list[:, :, 1]
    second_index = ((second_local // BAND_DEV) * N_COL + col_ids[:, None]) * BAND_DEV + second_local % BAND_DEV
    active = (jnp.arange(PAIRS_DEV, dtype=jnp.int32)[None, :] < pair_count[:, None]).astype(jnp.float32)
    mirrored = jnp.where(first_index != second_index, 1.0, 0.0).astype(jnp.float32) * active
    wavefunctions = orbitals.astype(jnp.float32)
    kernel = kernel_grid()

    def add_pair(fields, pair_item):
        first_band, second_band, first_weight, second_weight = pair_item
        first_wave = lax.dynamic_index_in_dim(wavefunctions, first_band, 0, keepdims=False)
        second_wave = lax.dynamic_index_in_dim(wavefunctions, second_band, 0, keepdims=False)
        density = (first_wave * second_wave).reshape(GX, GX, GX)
        spectrum = jnp.fft.fftn(density)
        potential = jnp.real(jnp.fft.ifftn(spectrum * kernel)).reshape(-1).astype(jnp.float32)
        fields = fields.at[first_band].add(first_weight * potential * second_wave)
        fields = fields.at[second_band].add(second_weight * potential * first_wave)
        return fields, None

    fields = jnp.zeros((BANDS, GRID), jnp.float32)
    fields = lax.scan(add_pair, fields, (first_index.reshape(-1), second_index.reshape(-1), active.reshape(-1), mirrored.reshape(-1)))[0]
    return fields
```

```python
import functools

import jax
import jax.numpy as jnp
import ml_dtypes
import numpy as np
from jax import lax
from jax.experimental import pallas as pl
from jax.experimental.pallas import tpu as pltpu
from jax.sharding import PartitionSpec as P

GX = 40
LANES = 128
SIDE = 3
THIRD = -(-GX // SIDE)
PACK = THIRD * GX
ROWS = SIDE * PACK
LIVE = GX * GX
SPARE = SIDE * GX
DUO = 2 * GX
QUAD = 4 * GX
GROUP = 5
VMEM_LIMIT = 48 * 1024 * 1024
screen_width = 0.9
F32 = jnp.float32
BF16 = jnp.bfloat16


def real_basis():
    half = GX // 2
    point = np.arange(GX)
    rows = [np.cos(2 * np.pi * (k * point % GX) / GX) for k in range(half + 1)]
    rows += [np.sin(2 * np.pi * (k * point % GX) / GX) for k in range(1, half)]
    frequency = np.concatenate([np.arange(half + 1), np.arange(1, half)])
    norm = np.where((frequency == 0) | (frequency == half), 1.0, 2.0) / GX
    return np.stack(rows), frequency, norm


def halves(table):
    high = table.astype(ml_dtypes.bfloat16)
    low = (table - high.astype(np.float64)).astype(ml_dtypes.bfloat16)
    return high, low


def left_table(table):
    high, low = halves(np.kron(np.eye(2), table))
    return np.concatenate([high, low, high], axis=1)


def right_table(table):
    wide = np.zeros((LANES, LANES))
    for p in range(SIDE):
        wide[p * GX : (p + 1) * GX, p * GX : (p + 1) * GX] = table
    high, low = halves(wide)
    both = np.concatenate([high, low], axis=1)
    return np.concatenate([both, both], axis=0)


def kernel_table():
    _, frequency, norm = real_basis()
    wave = frequency * (2.0 * np.pi / GX)
    squared = wave * wave
    total = squared[:, None, None] + squared[None, :, None] + squared[None, None, :]
    safe = np.where(total > 0, total, 1.0)
    screened = 4.0 * np.pi * (1.0 - np.exp(-safe / (4.0 * screen_width**2))) / safe
    kernel = np.where(total > 0, screened, np.pi / screen_width**2)
    kernel = kernel * norm[:, None, None] * norm[None, :, None] * norm[None, None, :]
    rows = np.swapaxes(kernel, 0, 1).reshape(LIVE, GX)
    out = np.zeros((LIVE, LANES), np.float32)
    for p in range(SIDE):
        out[:, p * GX : (p + 1) * GX] = rows
    return out


def place(out, row, col):
    for z in range(GX):
        out[row + z, col + z] = 1.0


def pack_table():
    out = np.zeros((SIDE, GX, LANES), np.float32)
    for third in range(SIDE):
        place(out[third], 0, third * GX)
    return out.astype(ml_dtypes.bfloat16)


def spread_table():
    out = np.zeros((SIDE * LANES, SIDE * LANES), np.float32)
    for third in range(SIDE):
        for p in range(SIDE):
            place(out, p * LANES + third * GX, third * LANES + p * GX)
    return out.astype(ml_dtypes.bfloat16)


def repeat_table():
    out = np.zeros((LANES, SIDE * LANES), np.float32)
    for third in range(SIDE):
        for p in range(SIDE):
            place(out, third * GX, third * LANES + p * GX)
    return out.astype(ml_dtypes.bfloat16)


def dot(a, b):
    return jnp.dot(a, b, preferred_element_type=F32)


def split(values):
    high = values.astype(BF16)
    return high, (values - high.astype(F32)).astype(BF16)


def contract_rows(table, values):
    high, low = split(values)
    return dot(table, jnp.concatenate([high, high, low], axis=0))


def contract_lanes(values, table):
    both = dot(jnp.concatenate(split(values), axis=1), table)
    return both[:, :LANES] + both[:, LANES:]


def fold(values):
    return jnp.concatenate([values[:DUO], values[DUO:]], axis=1)


def unfold(values):
    return jnp.concatenate([values[:, :LANES], values[:, LANES:]], axis=0)


def in_groups(body):
    def group(outer, carry):
        body([outer * GROUP + inner for inner in range(GROUP)])
        return carry

    lax.fori_loop(0, GX // 4 // GROUP, group, 0)


def quad(step):
    return pl.ds(step * QUAD, QUAD)


def load_planes(ref, step):
    planes = [ref[pl.ds(step * 4 + i, GX, stride=GX), :] for i in range(4)]
    left = jnp.concatenate(planes[:2], axis=0)
    return jnp.concatenate([left, jnp.concatenate(planes[2:], axis=0)], axis=1)


def store_planes(ref, step, values):
    for i in range(4):
        rows, lanes = i % 2 * GX, i // 2 * LANES
        ref[pl.ds(step * 4 + i, GX, stride=GX), :] = values[rows : rows + GX, lanes : lanes + LANES]


def count_vector(list_ref, count_ref, first_row):
    row = lax.broadcasted_iota(jnp.int32, (8, LANES), 0) - first_row
    lane = lax.broadcasted_iota(jnp.int32, (8, LANES), 1) - SPARE
    counts = jnp.zeros((8, LANES), F32)
    for p in range(list_ref.shape[1]):
        here = (row == list_ref[0, p, 0]) & (lane == list_ref[0, p, 1])
        live = jnp.where(p < count_ref[0], 1.0, 0.0)
        counts = counts + jnp.where(here, live, 0.0)
    return counts


def pack_kernel(col_total, band_ref, table_ref, *rest):
    out_ref = rest[-1]
    total = None
    for third in range(SIDE):
        rows = min(PACK, LIVE - third * PACK)
        piece = dot(band_ref[pl.ds(third * PACK, rows), :], table_ref[third])
        if rows < PACK:
            piece = jnp.concatenate([piece, jnp.zeros((PACK - rows, LANES), F32)], axis=0)
        total = piece if total is None else total + piece
    if len(rest) > 1:
        counts = count_vector(rest[0], rest[1], 0) + count_vector(rest[2], rest[3], col_total)
        empty = jnp.zeros((PACK - counts.shape[0], LANES), F32)
        total = total + jnp.concatenate([counts, empty], axis=0)
    out_ref[...] = total.astype(BF16)


def spread_waves(own_bands, repeat_ref, wave_refs):
    for band, wave_ref in zip(own_bands, wave_refs):
        wide = dot(band, repeat_ref[...])
        for third in range(SIDE):
            wave_ref[pl.ds(third * PACK, PACK), :] = wide[:, third * LANES : (third + 1) * LANES]


def solve_pairs(total, lists, load_band, tables, out_refs, scratch):
    spread_ref, repeat_ref, z_ref, z_back_ref, row_ref, row_back_ref, kernel_ref = tables
    trio_ref, *wave_refs, partner_ref, work_ref, work2_ref, sum0_ref, sum1_ref = scratch
    sum_refs = (sum0_ref, sum1_ref)
    slot_list, band_list, weight_list = lists
    for sum_ref in sum_refs:
        sum_ref[...] = jnp.zeros_like(sum_ref)
    side = lax.broadcasted_iota(jnp.int32, (1, LANES), 1) // GX

    def by_side(values):
        row = jnp.zeros((1, LANES), F32)
        for p in range(SIDE):
            row = jnp.where(side == p, values[p].astype(F32), row)
        return row

    def trio(at, carry):
        places = [at * SIDE + p for p in range(SIDE)]
        for p, place in enumerate(places):
            load_band(slot_list[place], trio_ref, p)
        bands = [band_list[place] for place in places]
        weights = [weight_list[place] for place in places]
        is_mate = by_side(bands) > 0.5
        scales = [
            by_side([jnp.where(bands[p] == which, weights[p], 0) for p in range(SIDE)])
            for which in range(2)
        ]
        wide = dot(trio_ref[...], spread_ref[...])
        for third in range(SIDE):
            partner_ref[pl.ds(third * PACK, PACK), :] = wide[:, third * LANES : (third + 1) * LANES]

        def forward(steps):
            values = []
            for step in steps:
                wave = jnp.where(is_mate, wave_refs[1][quad(step), :], wave_refs[0][quad(step), :])
                values.append(partner_ref[quad(step), :] * wave)
            values = [contract_lanes(v, z_ref[...]) for v in values]
            values = [contract_rows(row_ref[...], fold(v)) for v in values]
            for step, v in zip(steps, values):
                work_ref[quad(step), :] = unfold(v)

        def across(steps):
            values = [load_planes(work_ref, step) for step in steps]
            values = [contract_rows(row_ref[...], v) for v in values]
            values = [v * fold(kernel_ref[quad(step), :]) for step, v in zip(steps, values)]
            values = [contract_rows(row_back_ref[...], v) for v in values]
            for step, v in zip(steps, values):
                store_planes(work2_ref, step, v)

        def back(steps):
            values = [fold(work2_ref[quad(step), :]) for step in steps]
            values = [unfold(contract_rows(row_back_ref[...], v)) for v in values]
            values = [contract_lanes(v, z_back_ref[...]) for v in values]
            for step, v in zip(steps, values):
                v = v * partner_ref[quad(step), :]
                for sum_ref, scale in zip(sum_refs, scales):
                    sum_ref[quad(step), :] = sum_ref[quad(step), :] + v * scale

        for phase in (forward, across, back):
            in_groups(phase)
        return carry

    lax.fori_loop(0, (total + SIDE - 1) // SIDE, trio, 0)

    def pack_sums(step, carry):
        for out_ref, sum_ref in zip(out_refs, sum_refs):
            packed = jnp.zeros((GX, LANES), F32)
            for third in range(SIDE):
                values = sum_ref[pl.ds(third * PACK + step * GX, GX), :]
                field = jnp.zeros((GX, LANES), F32)
                for p in range(SIDE):
                    shift = (third - p) * GX % LANES
                    field = field + (pltpu.roll(values, shift, 1) if shift else values)
                packed = jnp.where(side == third, field, packed)
            out_ref[pl.ds(step * GX, GX), :] = packed
        return carry

    lax.fori_loop(0, THIRD, pack_sums, 0)


def near_kernel(row_total, col_total, *refs):
    pairs_wide = col_total // 2
    slots = row_total * pairs_wide
    band_refs, refs = refs[:slots], refs[slots:]
    mate_ref, tables, out_refs, refs = refs[0], refs[1:8], refs[8:10], refs[10:]
    (count_vmem, count_smem, slot_list, band_list, weight_list), refs = refs[:5], refs[5:]
    scratch, sem = refs[:-1], refs[-1]

    lane = lax.broadcasted_iota(jnp.int32, (8, LANES), 1)
    counts = jnp.zeros((8, LANES), F32)
    for s in range(slots):
        spare = band_refs[s][0:16, :].astype(F32)[0:8]
        shift = (s * row_total - SPARE) % LANES
        moved = pltpu.roll(spare, shift, 1) if shift else spare
        counts = jnp.where(lane // row_total == s, moved, counts)
    count_vmem[...] = counts.astype(jnp.int32)
    copy = pltpu.make_async_copy(count_vmem, count_smem, sem)
    copy.start()
    spread_waves((band_refs[0][...], mate_ref[...]), tables[1], scratch[1:3])
    copy.wait()
    row = lax.axis_index("row")
    col = lax.axis_index("col")
    total = jnp.int32(0)
    for which in range(2):
        mine = col ^ which
        for slot in range(slots):
            row_flip, x_flip = slot // pairs_wide, slot % pairs_wide
            other_row = row ^ row_flip
            other_col = col ^ (2 * x_flip)
            weight = count_smem[mine, x_flip * row_total + other_row]
            if which or slot:
                mirror_lane = row_flip * pairs_wide * row_total + row
                weight = weight + count_smem[which * col_total + other_col, mirror_lane]
            slot_list[total] = slot
            band_list[total] = which
            weight_list[total] = weight
            total = total + jnp.where(weight > 0, 1, 0)
    lists = (slot_list, band_list, weight_list)
    for p in range(SIDE - 1):
        slot_list[total + p] = 0
        band_list[total + p] = 0
        weight_list[total + p] = 0

    def load_band(place, target, p):
        for s in range(slots):

            @pl.when(place == s)
            def _():
                target[:, p * LANES : (p + 1) * LANES] = band_refs[s][...]

    solve_pairs(total, lists, load_band, tables, out_refs, scratch)


def far_kernel(total_ref, slot_list, band_list, weight_list, bands_ref, own_ref, mate_ref, *refs):
    tables, out_refs, refs = refs[:7], refs[7:9], refs[9:]
    buffer, scratch = refs[0], refs[1:]
    spread_waves((own_ref[...], mate_ref[...]), tables[1], scratch[1:3])

    def load_band(place, target, p):
        pltpu.sync_copy(bands_ref.at[place], buffer)
        target[:, p * LANES : (p + 1) * LANES] = buffer[...]

    lists = (slot_list, band_list, weight_list)
    solve_pairs(total_ref[0], lists, load_band, tables, out_refs, scratch)


def finish_kernel(own_ref, part_ref, out_ref):
    for third in range(SIDE):
        rows = min(PACK, LIVE - third * PACK)
        values = own_ref[pl.ds(0, rows), :] + part_ref[pl.ds(0, rows), :]
        if third:
            values = pltpu.roll(values, LANES - third * GX, 1)
        out_ref[pl.ds(third * PACK, rows), :] = values[:, :GX]


VMEM_SPEC = pl.BlockSpec(memory_space=pltpu.VMEM)
SMEM_SPEC = pl.BlockSpec(memory_space=pltpu.SMEM)
ANY_SPEC = pl.BlockSpec(memory_space=pl.ANY)
PARAMS = pltpu.CompilerParams(vmem_limit_bytes=VMEM_LIMIT)


def solve_tables():
    basis, _, _ = real_basis()
    return [
        spread_table(),
        repeat_table(),
        right_table(basis.T),
        right_table(basis),
        left_table(basis),
        left_table(basis.T),
        kernel_table(),
    ]


def solve_scratch():
    wide = pltpu.VMEM((ROWS, LANES), F32)
    return [pltpu.VMEM((PACK, SIDE * LANES), BF16)] + [wide] * 7


def field_shapes():
    return [jax.ShapeDtypeStruct((PACK, LANES), F32)] * 2


def swap(values, axis, size, flip):
    return lax.ppermute(values, axis, [(i, i ^ flip) for i in range(size)])


def count_pairs(pair_list, pair_count, row_total, col_total):
    slots = pair_list.shape[1]
    live = lax.iota(jnp.int32, slots) < pair_count[0]
    first = pair_list[0, :, 0][:, None, None] == lax.iota(jnp.int32, col_total)[None, :, None]
    second = pair_list[0, :, 1][:, None, None] == lax.iota(jnp.int32, row_total)[None, None, :]
    return jnp.sum((first & second & live[:, None, None]).astype(F32), axis=0)


def pack_band(orbitals, col_total, extras):
    return pl.pallas_call(
        functools.partial(pack_kernel, col_total),
        out_shape=jax.ShapeDtypeStruct((PACK, LANES), BF16),
        in_specs=[VMEM_SPEC] * 2 + [SMEM_SPEC] * len(extras),
        out_specs=VMEM_SPEC,
        compiler_params=PARAMS,
        name="pack_band",
    )(orbitals.reshape(LIVE, GX), jnp.asarray(pack_table()), *extras)


def finish(own, part):
    field = pl.pallas_call(
        finish_kernel,
        out_shape=jax.ShapeDtypeStruct((LIVE, GX), F32),
        in_specs=[VMEM_SPEC] * 2,
        out_specs=VMEM_SPEC,
        compiler_params=PARAMS,
        name="add_parts",
    )(own, part)
    return field.reshape(1, LIVE * GX)


def near_shards(row_total, col_total, orbitals, pair_list, pair_count):
    row_swap = lambda values, flip: swap(values, "row", row_total, flip)
    col_swap = lambda values, flip: swap(values, "col", col_total, flip)
    extras = (pair_list, pair_count, col_swap(pair_list, 1), col_swap(pair_count, 1))
    own = pack_band(orbitals, col_total, extras)
    wide = col_total // 2
    bands = {(0, 0, 0): own}
    for z in range(1, row_total // 2):
        bands[z, 0, 0] = row_swap(own, 2 * z)
    for z in range(row_total // 2):
        for x in range(1, wide):
            bands[z, 0, x] = col_swap(bands[z, 0, 0], 2 * x)
        bands[z, 1, 0] = row_swap(bands[z, 0, 0], 1)
    for z in range(row_total // 2):
        for x in range(1, wide):
            if z % 2:
                bands[z, 1, x] = col_swap(bands[z, 1, 0], 2 * x)
            else:
                bands[z, 1, x] = row_swap(bands[z, 0, x], 1)
    mate = col_swap(own, 1)
    slots = row_total * wide
    ordered = [
        bands[s // wide // 2, s // wide % 2, s % wide] for s in range(slots)
    ]
    places = 2 * slots + SIDE
    fields = pl.pallas_call(
        functools.partial(near_kernel, row_total, col_total),
        out_shape=field_shapes(),
        in_specs=[VMEM_SPEC] * (slots + 8),
        out_specs=[VMEM_SPEC] * 2,
        scratch_shapes=[
            pltpu.VMEM((8, LANES), jnp.int32),
            pltpu.SMEM((8, LANES), jnp.int32),
            pltpu.SMEM((places,), jnp.int32),
            pltpu.SMEM((places,), jnp.int32),
            pltpu.SMEM((places,), jnp.int32),
        ]
        + solve_scratch()
        + [pltpu.SemaphoreType.DMA],
        compiler_params=PARAMS,
        name="solve_pairs",
    )(*ordered, mate, *map(jnp.asarray, solve_tables()))
    return finish(fields[0], col_swap(fields[1], 1))


def far_shards(row_total, col_total, orbitals, pair_list, pair_count):
    counts = count_pairs(pair_list, pair_count, row_total, col_total)
    own = pack_band(orbitals, col_total, ())
    axes = ("row", "col")
    table = lax.all_gather(counts.reshape(-1), axes)
    table = table.reshape(row_total, col_total, col_total, row_total)
    wide = col_total // 2
    column = lax.all_gather(own, "row")
    columns = [column] + [swap(column, "col", col_total, 2 * x) for x in range(1, wide)]
    bands = jnp.concatenate(columns, axis=0)
    row = lax.axis_index("row")
    col = lax.axis_index("col")
    mine = jnp.stack([col, col ^ 1])
    other_col = ((col // 2) ^ lax.iota(jnp.int32, wide)) * 2 + col % 2
    other_row = lax.iota(jnp.int32, row_total)
    direct = table[row][other_col][:, mine]
    direct = jnp.transpose(direct, (1, 2, 0))
    mirror = table[:, :, :, row][:, mine][:, :, other_col]
    mirror = jnp.transpose(mirror, (1, 0, 2))
    same = (mine[:, None, None] == other_col[None, None, :]) & (other_row == row)[None, :, None]
    weights = (direct + jnp.where(same, 0.0, mirror)).astype(jnp.int32).reshape(-1)
    index = lax.iota(jnp.int32, weights.shape[0])
    order = jnp.argsort(jnp.where(weights > 0, 0, 1), stable=True)
    pad = lambda values: jnp.pad(values.astype(jnp.int32), (0, SIDE))
    slots = row_total * wide
    slot = order % slots
    band = (slot % wide) * row_total + slot // wide
    total = jnp.sum((weights > 0).astype(jnp.int32)).reshape(1)
    fields = pl.pallas_call(
        far_kernel,
        out_shape=field_shapes(),
        in_specs=[SMEM_SPEC] * 4 + [ANY_SPEC] + [VMEM_SPEC] * 9,
        out_specs=[VMEM_SPEC] * 2,
        scratch_shapes=[pltpu.VMEM((PACK, LANES), BF16)] + solve_scratch(),
        compiler_params=PARAMS,
        name="solve_pairs",
    )(
        total,
        pad(band),
        pad(order // slots),
        pad(weights[order]),
        bands,
        own,
        swap(own, "col", col_total, 1),
        *map(jnp.asarray, solve_tables()),
    )
    return finish(fields[0], swap(fields[1], "col", col_total, 1))


def solution(mesh):
    row_total, col_total = mesh.shape["row"], mesh.shape["col"]
    near = 2 * col_total <= 8 and row_total <= 8 and row_total * row_total * col_total <= 2 * LANES
    shards = near_shards if near else far_shards
    return jax.shard_map(
        functools.partial(shards, row_total, col_total),
        mesh=mesh,
        in_specs=(P(("row", "col"), None), P(("row", "col"), None, None), P(("row", "col"))),
        out_specs=P(("row", "col"), None),
        check_vma=False,
    )
```

```python
import functools
import itertools

import jax
import jax.numpy as jnp
import ml_dtypes
import numpy as np
from jax import lax
from jax.experimental import pallas as pl
from jax.experimental.pallas import tpu as pltpu
from jax.sharding import PartitionSpec as P

GX = 40
LANES = 128
SIDE = 3
THIRD = -(-GX // SIDE)
PACK = THIRD * GX
ROWS = SIDE * PACK
LIVE = GX * GX
SPARE = SIDE * GX
DUO = 2 * GX
QUAD = 4 * GX
GROUP = 10
VMEM_LIMIT = 20 * 1024 * 1024
screen_width = 0.9
F32 = jnp.float32
BF16 = jnp.bfloat16


def real_basis():
    half = GX // 2
    point = np.arange(GX)
    rows = [np.cos(2 * np.pi * (k * point % GX) / GX) for k in range(half + 1)]
    rows += [np.sin(2 * np.pi * (k * point % GX) / GX) for k in range(1, half)]
    frequency = np.concatenate([np.arange(half + 1), np.arange(1, half)])
    norm = np.where((frequency == 0) | (frequency == half), 1.0, 2.0) / GX
    return np.stack(rows), frequency, norm


def halves(table):
    high = table.astype(ml_dtypes.bfloat16)
    low = (table - high.astype(np.float64)).astype(ml_dtypes.bfloat16)
    return high, low


def left_table(table):
    high, low = halves(np.kron(np.eye(2), table))
    return np.concatenate([high, low, high], axis=1)


def right_table(table):
    wide = np.zeros((LANES, LANES))
    for p in range(SIDE):
        wide[p * GX : (p + 1) * GX, p * GX : (p + 1) * GX] = table
    high, low = halves(wide)
    both = np.concatenate([high, low], axis=1)
    return np.concatenate([both, both], axis=0)


def kernel_table():
    _, frequency, norm = real_basis()
    wave = frequency * (2.0 * np.pi / GX)
    squared = wave * wave
    total = squared[:, None, None] + squared[None, :, None] + squared[None, None, :]
    safe = np.where(total > 0, total, 1.0)
    screened = 4.0 * np.pi * (1.0 - np.exp(-safe / (4.0 * screen_width**2))) / safe
    kernel = np.where(total > 0, screened, np.pi / screen_width**2)
    kernel = kernel * norm[:, None, None] * norm[None, :, None] * norm[None, None, :]
    rows = np.swapaxes(kernel, 0, 1).reshape(LIVE, GX)
    out = np.zeros((LIVE, LANES), np.float32)
    for p in range(SIDE):
        out[:, p * GX : (p + 1) * GX] = rows
    return out


def place(out, row, col):
    for z in range(GX):
        out[row + z, col + z] = 1.0


def pack_table():
    out = np.zeros((SIDE, GX, LANES), np.float32)
    for third in range(SIDE):
        place(out[third], 0, third * GX)
    return out.astype(ml_dtypes.bfloat16)


def spread_table():
    out = np.zeros((SIDE * LANES, SIDE * LANES), np.float32)
    for third in range(SIDE):
        for p in range(SIDE):
            place(out, p * LANES + third * GX, third * LANES + p * GX)
    return out.astype(ml_dtypes.bfloat16)


def repeat_table():
    out = np.zeros((LANES, SIDE * LANES), np.float32)
    for third in range(SIDE):
        for p in range(SIDE):
            place(out, third * GX, third * LANES + p * GX)
    return out.astype(ml_dtypes.bfloat16)


def dot(a, b):
    return jnp.dot(a, b, preferred_element_type=F32)


def split(values):
    high = values.astype(BF16)
    return high, (values - high.astype(F32)).astype(BF16)


def contract_rows(table, values):
    high, low = split(values)
    return dot(table, jnp.concatenate([high, high, low], axis=0))


def contract_lanes(values, table):
    both = dot(jnp.concatenate(split(values), axis=1), table)
    return both[:, :LANES] + both[:, LANES:]


def fold(values):
    return jnp.concatenate([values[:DUO], values[DUO:]], axis=1)


def unfold(values):
    return jnp.concatenate([values[:, :LANES], values[:, LANES:]], axis=0)


def in_groups(body):
    def group(outer, carry):
        body([outer * GROUP + inner for inner in range(GROUP)])
        return carry

    lax.fori_loop(0, GX // 4 // GROUP, group, 0)


def quad(step):
    return pl.ds(step * QUAD, QUAD)


def load_planes(ref, step):
    planes = [ref[pl.ds(step * 4 + i, GX, stride=GX), :] for i in range(4)]
    left = jnp.concatenate(planes[:2], axis=0)
    return jnp.concatenate([left, jnp.concatenate(planes[2:], axis=0)], axis=1)


def store_planes(ref, step, values):
    for i in range(4):
        rows, lanes = i % 2 * GX, i // 2 * LANES
        ref[pl.ds(step * 4 + i, GX, stride=GX), :] = values[rows : rows + GX, lanes : lanes + LANES]


def count_vector(list_ref, first_row):
    pairs = list_ref[0]
    slots = pairs.shape[0]
    row = lax.broadcasted_iota(jnp.int32, (slots, LANES), 1) - first_row
    lane = lax.broadcasted_iota(jnp.int32, (slots, LANES), 1) - SPARE
    first = jnp.where(pairs[:, 0:1] == row, 1.0, 0.0)
    second = jnp.where(pairs[:, 1:2] == lane, 1.0, 0.0)
    return lax.dot_general(first, second, (((0,), (0,)), ((), ())), preferred_element_type=F32)


def pack_kernel(col_total, band_ref, table_ref, *rest):
    out_ref = rest[-1]
    total = None
    for third in range(SIDE):
        rows = min(PACK, LIVE - third * PACK)
        piece = dot(band_ref[pl.ds(third * PACK, rows), :], table_ref[third])
        if rows < PACK:
            piece = jnp.concatenate([piece, jnp.zeros((PACK - rows, LANES), F32)], axis=0)
        total = piece if total is None else total + piece
    if len(rest) > 1:
        counts = sum(count_vector(ref, k * col_total) for k, ref in enumerate(rest[:-1]))
        counts = counts[:16]
        empty = jnp.zeros((PACK - counts.shape[0], LANES), F32)
        total = total + jnp.concatenate([counts, empty], axis=0)
    out_ref[0] = total.astype(BF16)


def spread_waves(own_bands, repeat_ref, wave_refs):
    for band, wave_ref in zip(own_bands, wave_refs):
        wide = dot(band, repeat_ref[...])
        for third in range(SIDE):
            wave_ref[pl.ds(third * PACK, PACK), :] = wide[:, third * LANES : (third + 1) * LANES]


def clear(sum_refs):
    for sum_ref in sum_refs:
        sum_ref[...] = jnp.zeros_like(sum_ref)


def lane_side():
    return lax.broadcasted_iota(jnp.int32, (1, LANES), 1) // GX


def solve_trios(first, count, lists, load_band, tables, wave_refs, sum_refs, scratch):
    spread_ref, _, z_ref, z_back_ref, row_ref, row_back_ref, kernel_ref = tables
    trio_ref, partner_ref, work_ref, work2_ref = scratch
    slot_list, band_list, weight_list = lists
    side = lane_side()

    def by_side(values):
        row = jnp.zeros((1, LANES), F32)
        for p in range(SIDE):
            row = jnp.where(side == p, values[p].astype(F32), row)
        return row

    def trio(at, carry):
        places = [first + at * SIDE + p for p in range(SIDE)]
        for p, place in enumerate(places):
            load_band(slot_list[place], trio_ref, p)
        bands = [band_list[place] for place in places]
        weights = [weight_list[place] for place in places]
        is_mate = by_side(bands) > 0.5
        scales = [
            by_side([jnp.where(bands[p] == which, weights[p], 0) for p in range(SIDE)])
            for which in range(2)
        ]
        wide = dot(trio_ref[...], spread_ref[...])
        for third in range(SIDE):
            partner_ref[pl.ds(third * PACK, PACK), :] = wide[:, third * LANES : (third + 1) * LANES]

        def forward(steps):
            values = []
            for step in steps:
                wave = jnp.where(is_mate, wave_refs[1][quad(step), :], wave_refs[0][quad(step), :])
                values.append(partner_ref[quad(step), :] * wave)
            values = [contract_lanes(v, z_ref[...]) for v in values]
            values = [contract_rows(row_ref[...], fold(v)) for v in values]
            for step, v in zip(steps, values):
                work_ref[quad(step), :] = unfold(v)

        def across(steps):
            values = [load_planes(work_ref, step) for step in steps]
            values = [contract_rows(row_ref[...], v) for v in values]
            values = [v * fold(kernel_ref[quad(step), :]) for step, v in zip(steps, values)]
            values = [contract_rows(row_back_ref[...], v) for v in values]
            for step, v in zip(steps, values):
                store_planes(work2_ref, step, v)

        def back(steps):
            values = [fold(work2_ref[quad(step), :]) for step in steps]
            values = [unfold(contract_rows(row_back_ref[...], v)) for v in values]
            values = [contract_lanes(v, z_back_ref[...]) for v in values]
            for step, v in zip(steps, values):
                v = v * partner_ref[quad(step), :]
                for sum_ref, scale in zip(sum_refs, scales):
                    sum_ref[quad(step), :] = sum_ref[quad(step), :] + v * scale

        for phase in (forward, across, back):
            in_groups(phase)
        return carry

    lax.fori_loop(0, count, trio, 0)


def pack_fields(sum_refs, out_refs):
    side = lane_side()

    def pack_sums(step, carry):
        for out_ref, sum_ref in zip(out_refs, sum_refs):
            packed = jnp.zeros((GX, LANES), F32)
            for third in range(SIDE):
                values = sum_ref[pl.ds(third * PACK + step * GX, GX), :]
                field = jnp.zeros((GX, LANES), F32)
                for p in range(SIDE):
                    shift = (third - p) * GX % LANES
                    field = field + (pltpu.roll(values, shift, 1) if shift else values)
                packed = jnp.where(side == third, field, packed)
            out_ref[pl.ds(step * GX, GX), :] = packed
        return carry

    lax.fori_loop(0, THIRD, pack_sums, 0)


def near_kernel(row_total, col_total, part, *refs):
    stages = STAGES[: part + 1]
    blocks = [block for stage in stages for block in stage]
    band_refs, refs = refs[: len(blocks)], refs[len(blocks) :]
    bands = [(ref, at) for ref, block in zip(band_refs, blocks) for at in range(len(block))]
    flips = [flip for block in blocks for flip in block]
    mate_ref, tables, refs = refs[0], refs[1:8], refs[8:]
    if part:
        wave_refs, given_refs, out_refs, refs = refs[:2], refs[2:4], refs[4:6], refs[6:]
    else:
        wave_refs, out_refs, refs = refs[:2], refs[2:4], refs[4:]
    (count_vmem, count_smem, slot_list, band_list, weight_list), refs = refs[:5], refs[5:]
    scratch, sem = refs[:4], refs[4]
    sum_refs = refs[5:] if part == 2 else out_refs

    lane = lax.broadcasted_iota(jnp.int32, (8, LANES), 1)
    counts = jnp.zeros((8, LANES), F32)
    for s, (ref, at) in enumerate(bands):
        spare = ref[at, 0:16, :].astype(F32)[0:8]
        shift = (s * row_total - SPARE) % LANES
        moved = pltpu.roll(spare, shift, 1) if shift else spare
        counts = jnp.where(lane // row_total == s, moved, counts)
    count_vmem[...] = counts.astype(jnp.int32)
    copy = pltpu.make_async_copy(count_vmem, count_smem, sem)
    copy.start()
    if part:
        for sum_ref, given_ref in zip(sum_refs, given_refs):
            sum_ref[...] = given_ref[...]
    else:
        clear(sum_refs)
        spread_waves((band_refs[0][0], mate_ref[0]), tables[1], wave_refs)
    copy.wait()
    row = lax.axis_index("row")
    col = lax.axis_index("col")
    total = jnp.int32(0)
    done = jnp.int32(0)
    place = 0
    for step, stage in enumerate(stages):
        here = range(place, place + sum(len(block) for block in stage))
        place = here.stop
        for which, at in itertools.product(range(2), here):
            row_flip, col_flip = flips[at]
            row_place = flips.index((0, col_flip)) * row_total
            col_place = flips.index((row_flip, 0)) * row_total
            weight = count_smem[col ^ which, row_place + (row ^ row_flip)]
            if at or which:
                mirror = which * col_total + (col ^ col_flip)
                weight = weight + count_smem[mirror, col_place + row]
            slot_list[total] = at
            band_list[total] = which
            weight_list[total] = weight
            total = total + jnp.where(weight > 0, 1, 0)
        if step < 2:
            trios = jnp.minimum((total - done) // SIDE, CAPS[step])
            if step < part:
                done = done + trios * SIDE
    if part == 2:
        trios = (total - done + SIDE - 1) // SIDE
        for p in range(SIDE - 1):
            slot_list[total + p] = 0
            band_list[total + p] = 0
            weight_list[total + p] = 0

    def load_band(wanted, target, p):
        for place, (ref, at) in enumerate(bands):

            @pl.when(wanted == place)
            def _():
                target[:, p * LANES : (p + 1) * LANES] = ref[at]

    lists = (slot_list, band_list, weight_list)
    solve_trios(done, trios, lists, load_band, tables, wave_refs, sum_refs, scratch)
    if part == 2:
        pack_fields(sum_refs, out_refs)


def far_kernel(total_ref, slot_list, band_list, weight_list, bands_ref, own_ref, mate_ref, *refs):
    tables, out_refs, refs = refs[:7], refs[7:9], refs[9:]
    buffer, wave_refs, sum_refs, scratch = refs[0], refs[1:3], refs[3:5], refs[5:]
    spread_waves((own_ref[0], mate_ref[0]), tables[1], wave_refs)
    clear(sum_refs)

    def load_band(place, target, p):
        pltpu.sync_copy(bands_ref.at[place], buffer)
        target[:, p * LANES : (p + 1) * LANES] = buffer[...]

    lists = (slot_list, band_list, weight_list)
    trios = (total_ref[0] + SIDE - 1) // SIDE
    solve_trios(0, trios, lists, load_band, tables, wave_refs, sum_refs, scratch)
    pack_fields(sum_refs, out_refs)


def finish_kernel(own_ref, part_ref, out_ref):
    for third in range(SIDE):
        rows = min(PACK, LIVE - third * PACK)
        values = own_ref[pl.ds(0, rows), :] + part_ref[pl.ds(0, rows), :]
        if third:
            values = pltpu.roll(values, LANES - third * GX, 1)
        out_ref[pl.ds(third * PACK, rows), :] = values[:, :GX]


VMEM_SPEC = pl.BlockSpec(memory_space=pltpu.VMEM)
SMEM_SPEC = pl.BlockSpec(memory_space=pltpu.SMEM)
ANY_SPEC = pl.BlockSpec(memory_space=pl.ANY)
PARAMS = pltpu.CompilerParams(vmem_limit_bytes=VMEM_LIMIT)


def solve_tables():
    basis, _, _ = real_basis()
    return [
        spread_table(),
        repeat_table(),
        right_table(basis.T),
        right_table(basis),
        left_table(basis),
        left_table(basis.T),
        kernel_table(),
    ]


def solve_scratch():
    return [pltpu.VMEM((PACK, SIDE * LANES), BF16)] + [pltpu.VMEM((ROWS, LANES), F32)] * 3


def pair_of(rows):
    return [jax.ShapeDtypeStruct((rows, LANES), F32)] * 2


def swap(values, axis, size, flip):
    return lax.ppermute(values, axis, [(i, i ^ flip) for i in range(size)])


def count_pairs(pair_list, pair_count, row_total, col_total):
    slots = pair_list.shape[1]
    live = lax.iota(jnp.int32, slots) < pair_count[0]
    first = pair_list[0, :, 0][:, None, None] == lax.iota(jnp.int32, col_total)[None, :, None]
    second = pair_list[0, :, 1][:, None, None] == lax.iota(jnp.int32, row_total)[None, None, :]
    return jnp.sum((first & second & live[:, None, None]).astype(F32), axis=0)


def pack_band(orbitals, col_total, extras):
    return pl.pallas_call(
        functools.partial(pack_kernel, col_total),
        out_shape=jax.ShapeDtypeStruct((1, PACK, LANES), BF16),
        in_specs=[VMEM_SPEC] * (2 + len(extras)),
        out_specs=VMEM_SPEC,
        compiler_params=PARAMS,
        name="pack_band",
    )(orbitals.reshape(LIVE, GX), jnp.asarray(pack_table()), *extras)


def finish(own, part):
    field = pl.pallas_call(
        finish_kernel,
        out_shape=jax.ShapeDtypeStruct((LIVE, GX), F32),
        in_specs=[VMEM_SPEC] * 2,
        out_specs=VMEM_SPEC,
        compiler_params=PARAMS,
        name="add_parts",
    )(own, part)
    return field.reshape(1, LIVE * GX)


NEAR = (8, 4)
STAGES = (
    (((0, 0),), ((4, 0),), ((2, 0),), ((1, 0),), ((0, 2),)),
    (((4, 2), (2, 2)), ((5, 0), (1, 2)), ((6, 0), (3, 0))),
    (((6, 2),), ((5, 2),), ((7, 0), (3, 2)), ((7, 2),)),
)
CAPS = (2, 2)


def near_part(row_total, col_total, part, operands):
    places = 2 * row_total * (col_total // 2) + SIDE
    out_shape = pair_of(ROWS)
    if part == 0:
        out_shape = out_shape * 2
    if part == 2:
        out_shape = pair_of(PACK)
    operands = list(operands)
    cost = pl.CostEstimate(flops=4 * 10**9, bytes_accessed=2 * 10**7, transcendentals=0)
    return pl.pallas_call(
        functools.partial(near_kernel, row_total, col_total, part),
        out_shape=out_shape,
        in_specs=[VMEM_SPEC] * len(operands),
        out_specs=[VMEM_SPEC] * len(out_shape),
        scratch_shapes=[
            pltpu.VMEM((8, LANES), jnp.int32),
            pltpu.SMEM((8, LANES), jnp.int32),
            pltpu.SMEM((places,), jnp.int32),
            pltpu.SMEM((places,), jnp.int32),
            pltpu.SMEM((places,), jnp.int32),
        ]
        + solve_scratch()
        + [pltpu.SemaphoreType.DMA]
        + [pltpu.VMEM((ROWS, LANES), F32)] * (2 if part == 2 else 0),
        compiler_params=PARAMS,
        cost_estimate=cost,
        name="solve_part",
    )(*operands)


def near_shards(row_total, col_total, orbitals, pair_list, pair_count):
    row_swap = lambda values, flip: swap(values, "row", row_total, flip)
    col_swap = lambda values, flip: swap(values, "col", col_total, flip)
    both = lambda a, b: jnp.concatenate([a, b], axis=0)
    live = lax.iota(jnp.int32, pair_list.shape[1])[None, :, None] < pair_count[0]
    pairs = jnp.where(live, pair_list, -row_total * col_total)
    own = pack_band(orbitals, col_total, [pairs, col_swap(pairs, 1)])
    w, z, y, x = row_swap(own, 4), row_swap(own, 2), row_swap(own, 1), col_swap(own, 2)
    mate = col_swap(own, 1)
    over_x, over_y, over_z = col_swap(both(w, z), 2), row_swap(both(w, x), 1), row_swap(both(w, y), 2)
    tables = [jnp.asarray(table) for table in solve_tables()]
    blocks = [own, w, z, y, x]
    *waves, sum0, sum1 = near_part(row_total, col_total, 0, [*blocks, mate, *tables])
    held = lax.optimization_barrier((sum0, sum1, over_x, over_y, over_z))
    sum0, sum1, over_x, over_y, over_z = held
    wzx = col_swap(over_z[:1], 2)
    wxy = row_swap(over_x[:1], 1)
    wyz_xyz = row_swap(over_y, 2)
    wzxy = row_swap(wzx, 1)
    arrivals = ((over_x, over_y, over_z), (wzx, wxy, wyz_xyz, wzxy))
    for part, arrived in enumerate(arrivals, 1):
        blocks += arrived
        operands = [*blocks, mate, *tables, *waves, sum0, sum1]
        sum0, sum1 = near_part(row_total, col_total, part, operands)
    return finish(sum0, col_swap(sum1, 1))


def far_shards(row_total, col_total, orbitals, pair_list, pair_count):
    counts = count_pairs(pair_list, pair_count, row_total, col_total)
    own = pack_band(orbitals, col_total, ())
    axes = ("row", "col")
    table = lax.all_gather(counts.reshape(-1), axes)
    table = table.reshape(row_total, col_total, col_total, row_total)
    wide = col_total // 2
    column = lax.all_gather(own[0], "row")
    columns = [column] + [swap(column, "col", col_total, 2 * x) for x in range(1, wide)]
    bands = jnp.concatenate(columns, axis=0)
    row = lax.axis_index("row")
    col = lax.axis_index("col")
    mine = jnp.stack([col, col ^ 1])
    other_col = ((col // 2) ^ lax.iota(jnp.int32, wide)) * 2 + col % 2
    other_row = lax.iota(jnp.int32, row_total)
    direct = table[row][other_col][:, mine]
    direct = jnp.transpose(direct, (1, 2, 0))
    mirror = table[:, :, :, row][:, mine][:, :, other_col]
    mirror = jnp.transpose(mirror, (1, 0, 2))
    same = (mine[:, None, None] == other_col[None, None, :]) & (other_row == row)[None, :, None]
    weights = (direct + jnp.where(same, 0.0, mirror)).astype(jnp.int32).reshape(-1)
    index = lax.iota(jnp.int32, weights.shape[0])
    order = jnp.argsort(jnp.where(weights > 0, 0, 1), stable=True)
    pad = lambda values: jnp.pad(values.astype(jnp.int32), (0, SIDE))
    slots = row_total * wide
    slot = order % slots
    band = (slot % wide) * row_total + slot // wide
    total = jnp.sum((weights > 0).astype(jnp.int32)).reshape(1)
    fields = pl.pallas_call(
        far_kernel,
        out_shape=pair_of(PACK),
        in_specs=[SMEM_SPEC] * 4 + [ANY_SPEC] + [VMEM_SPEC] * 9,
        out_specs=[VMEM_SPEC] * 2,
        scratch_shapes=[pltpu.VMEM((PACK, LANES), BF16)]
        + [pltpu.VMEM((ROWS, LANES), F32)] * 4
        + solve_scratch(),
        compiler_params=PARAMS,
        name="solve_pairs",
    )(
        total,
        pad(band),
        pad(order // slots),
        pad(weights[order]),
        bands,
        own,
        swap(own, "col", col_total, 1),
        *map(jnp.asarray, solve_tables()),
    )
    return finish(fields[0], swap(fields[1], "col", col_total, 1))


def solution(mesh):
    row_total, col_total = mesh.shape["row"], mesh.shape["col"]
    near = (row_total, col_total) == NEAR
    shards = near_shards if near else far_shards
    return jax.shard_map(
        functools.partial(shards, row_total, col_total),
        mesh=mesh,
        in_specs=(P(("row", "col"), None), P(("row", "col"), None, None), P(("row", "col"))),
        out_specs=P(("row", "col"), None),
        check_vma=False,
    )
```

```python
import functools
import itertools

import jax
import jax.numpy as jnp
import ml_dtypes
import numpy as np
from jax import lax
from jax.experimental import pallas as pl
from jax.experimental.pallas import tpu as pltpu
from jax.sharding import PartitionSpec as P

GX = 40
LANES = 128
SIDE = 3
THIRD = -(-GX // SIDE)
PACK = THIRD * GX
ROWS = SIDE * PACK
LIVE = GX * GX
SPARE = SIDE * GX
FLAT = LIVE * GX // LANES
CHUNK = PACK // 16
FLAT_ROWS = SIDE * CHUNK * 5 + 8
DUO = 2 * GX
QUAD = 4 * GX
GROUP = 10
VMEM_LIMIT = 20 * 1024 * 1024
screen_width = 0.9
F32 = jnp.float32
BF16 = jnp.bfloat16


def real_basis():
    half = GX // 2
    point = np.arange(GX)
    rows = [np.cos(2 * np.pi * (k * point % GX) / GX) for k in range(half + 1)]
    rows += [np.sin(2 * np.pi * (k * point % GX) / GX) for k in range(1, half)]
    frequency = np.concatenate([np.arange(half + 1), np.arange(1, half)])
    norm = np.where((frequency == 0) | (frequency == half), 1.0, 2.0) / GX
    return np.stack(rows), frequency, norm


def halves(table):
    high = table.astype(ml_dtypes.bfloat16)
    low = (table - high.astype(np.float64)).astype(ml_dtypes.bfloat16)
    return high, low


def left_table(table):
    high, low = halves(np.kron(np.eye(2), table))
    return np.concatenate([high, low, high], axis=1)


def right_table(table):
    wide = np.zeros((LANES, LANES))
    for p in range(SIDE):
        wide[p * GX : (p + 1) * GX, p * GX : (p + 1) * GX] = table
    high, low = halves(wide)
    both = np.concatenate([high, low], axis=1)
    return np.concatenate([both, both], axis=0)


def kernel_table():
    _, frequency, norm = real_basis()
    wave = frequency * (2.0 * np.pi / GX)
    squared = wave * wave
    total = squared[:, None, None] + squared[None, :, None] + squared[None, None, :]
    safe = np.where(total > 0, total, 1.0)
    screened = 4.0 * np.pi * (1.0 - np.exp(-safe / (4.0 * screen_width**2))) / safe
    kernel = np.where(total > 0, screened, np.pi / screen_width**2)
    kernel = kernel * norm[:, None, None] * norm[None, :, None] * norm[None, None, :]
    rows = np.swapaxes(kernel, 0, 1).reshape(LIVE, GX)
    out = np.zeros((LIVE, LANES), np.float32)
    for p in range(SIDE):
        out[:, p * GX : (p + 1) * GX] = rows
    return out


def place(out, row, col):
    for z in range(GX):
        out[row + z, col + z] = 1.0


def spread_table():
    out = np.zeros((SIDE * LANES, SIDE * LANES), np.float32)
    for third in range(SIDE):
        for p in range(SIDE):
            place(out, p * LANES + third * GX, third * LANES + p * GX)
    return out.astype(ml_dtypes.bfloat16)


def repeat_table():
    out = np.zeros((LANES, SIDE * LANES), np.float32)
    for third in range(SIDE):
        for p in range(SIDE):
            place(out, third * GX, third * LANES + p * GX)
    return out.astype(ml_dtypes.bfloat16)


def dot(a, b):
    return jnp.dot(a, b, preferred_element_type=F32)


def split(values):
    high = values.astype(BF16)
    return high, (values - high.astype(F32)).astype(BF16)


def contract_rows(table, values):
    high, low = split(values)
    return dot(table, jnp.concatenate([high, high, low], axis=0))


def contract_lanes(values, table):
    both = dot(jnp.concatenate(split(values), axis=1), table)
    return both[:, :LANES] + both[:, LANES:]


def fold(values):
    return jnp.concatenate([values[:DUO], values[DUO:]], axis=1)


def unfold(values):
    return jnp.concatenate([values[:, :LANES], values[:, LANES:]], axis=0)


def in_groups(body):
    def group(outer, carry):
        body([outer * GROUP + inner for inner in range(GROUP)])
        return carry

    lax.fori_loop(0, GX // 4 // GROUP, group, 0)


def quad(step):
    return pl.ds(step * QUAD, QUAD)


def load_planes(ref, step):
    planes = [ref[pl.ds(step * 4 + i, GX, stride=GX), :] for i in range(4)]
    left = jnp.concatenate(planes[:2], axis=0)
    return jnp.concatenate([left, jnp.concatenate(planes[2:], axis=0)], axis=1)


def store_planes(ref, step, values):
    for i in range(4):
        rows, lanes = i % 2 * GX, i // 2 * LANES
        ref[pl.ds(step * 4 + i, GX, stride=GX), :] = values[rows : rows + GX, lanes : lanes + LANES]


def count_vector(list_ref, first_row):
    pairs = list_ref[0]
    slots = pairs.shape[0]
    row = lax.broadcasted_iota(jnp.int32, (slots, LANES), 1) - first_row
    lane = lax.broadcasted_iota(jnp.int32, (slots, LANES), 1) - SPARE
    first = jnp.where(pairs[:, 0:1] == row, 1.0, 0.0)
    second = jnp.where(pairs[:, 1:2] == lane, 1.0, 0.0)
    return lax.dot_general(first, second, (((0,), (0,)), ((), ())), preferred_element_type=F32)


def unroll_rows(copy):
    for k in range(FLAT):
        copy(k, slice(k * LANES, (k + 1) * LANES))


def pack_kernel(col_total, band_ref, *rest):
    *list_refs, out_ref, flat_ref, wide_ref = rest

    def to_rows(k, lanes):
        flat_ref[k : k + 1, :] = band_ref[0:1, lanes].astype(F32)

    unroll_rows(to_rows)
    unused = FLAT_ROWS - FLAT
    flat_ref[FLAT:FLAT_ROWS, :] = jnp.zeros((unused, LANES), F32)
    lane = lax.broadcasted_iota(jnp.int32, (1, LANES), 1)
    for q in range(16):
        row, offset = divmod(q * GX, LANES)
        packed = jnp.zeros((CHUNK, LANES), F32)
        for third in range(SIDE):
            start = third * CHUNK * 5 + row
            values = flat_ref[pl.ds(start, CHUNK, stride=5), :]
            if offset + GX > LANES:
                after = flat_ref[pl.ds(start + 1, CHUNK, stride=5), :]
                values = jnp.where(lane >= offset, values, after)
            shift = (third * GX - offset) % LANES
            values = pltpu.roll(values, shift, 1) if shift else values
            packed = jnp.where(lane // GX == third, values, packed)
        wide_ref[pl.ds(q, CHUNK, stride=16), :] = packed
    if list_refs:
        counts = sum(count_vector(ref, k * col_total) for k, ref in enumerate(list_refs))
        wide_ref[0:16, :] = wide_ref[0:16, :] + counts[:16]
    out_ref[0] = wide_ref[...].astype(BF16)


def spread_waves(own_bands, repeat_ref, wave_refs):
    for band, wave_ref in zip(own_bands, wave_refs):
        wide = dot(band, repeat_ref[...])
        for third in range(SIDE):
            wave_ref[pl.ds(third * PACK, PACK), :] = wide[:, third * LANES : (third + 1) * LANES]


def clear(sum_refs):
    for sum_ref in sum_refs:
        sum_ref[...] = jnp.zeros_like(sum_ref)


def lane_side():
    return lax.broadcasted_iota(jnp.int32, (1, LANES), 1) // GX


def solve_trios(first, count, lists, load_band, tables, wave_refs, sum_refs, scratch):
    spread_ref, _, z_ref, z_back_ref, row_ref, row_back_ref, kernel_ref = tables
    trio_ref, partner_ref, work_ref, work2_ref = scratch
    slot_list, band_list, weight_list = lists
    side = lane_side()

    def by_side(values):
        row = jnp.zeros((1, LANES), F32)
        for p in range(SIDE):
            row = jnp.where(side == p, values[p].astype(F32), row)
        return row

    def trio(at, carry):
        places = [first + at * SIDE + p for p in range(SIDE)]
        for p, place in enumerate(places):
            load_band(slot_list[place], trio_ref, p)
        bands = [band_list[place] for place in places]
        weights = [weight_list[place] for place in places]
        is_mate = by_side(bands) > 0.5
        scales = [
            by_side([jnp.where(bands[p] == which, weights[p], 0) for p in range(SIDE)])
            for which in range(2)
        ]
        wide = dot(trio_ref[...], spread_ref[...])
        for third in range(SIDE):
            partner_ref[pl.ds(third * PACK, PACK), :] = wide[:, third * LANES : (third + 1) * LANES]

        def forward(steps):
            values = []
            for step in steps:
                wave = jnp.where(is_mate, wave_refs[1][quad(step), :], wave_refs[0][quad(step), :])
                values.append(partner_ref[quad(step), :] * wave)
            values = [contract_lanes(v, z_ref[...]) for v in values]
            values = [contract_rows(row_ref[...], fold(v)) for v in values]
            for step, v in zip(steps, values):
                work_ref[quad(step), :] = unfold(v)

        def across(steps):
            values = [load_planes(work_ref, step) for step in steps]
            values = [contract_rows(row_ref[...], v) for v in values]
            values = [v * fold(kernel_ref[quad(step), :]) for step, v in zip(steps, values)]
            values = [contract_rows(row_back_ref[...], v) for v in values]
            for step, v in zip(steps, values):
                store_planes(work2_ref, step, v)

        def back(steps):
            values = [fold(work2_ref[quad(step), :]) for step in steps]
            values = [unfold(contract_rows(row_back_ref[...], v)) for v in values]
            values = [contract_lanes(v, z_back_ref[...]) for v in values]
            for step, v in zip(steps, values):
                v = v * partner_ref[quad(step), :]
                for sum_ref, scale in zip(sum_refs, scales):
                    sum_ref[quad(step), :] = sum_ref[quad(step), :] + v * scale

        for phase in (forward, across, back):
            in_groups(phase)
        return carry

    lax.fori_loop(0, count, trio, 0)


def pack_fields(sum_refs, out_refs):
    side = lane_side()

    def pack_sums(step, carry):
        for out_ref, sum_ref in zip(out_refs, sum_refs):
            packed = jnp.zeros((GX, LANES), F32)
            for third in range(SIDE):
                values = sum_ref[pl.ds(third * PACK + step * GX, GX), :]
                field = jnp.zeros((GX, LANES), F32)
                for p in range(SIDE):
                    shift = (third - p) * GX % LANES
                    field = field + (pltpu.roll(values, shift, 1) if shift else values)
                packed = jnp.where(side == third, field, packed)
            out_ref[pl.ds(step * GX, GX), :] = packed
        return carry

    lax.fori_loop(0, THIRD, pack_sums, 0)


def near_kernel(row_total, col_total, part, *refs):
    stages = STAGES[: part + 1]
    blocks = [block for stage in stages for block in stage]
    band_refs, refs = refs[: len(blocks)], refs[len(blocks) :]
    bands = [(ref, at) for ref, block in zip(band_refs, blocks) for at in range(len(block))]
    flips = [flip for block in blocks for flip in block]
    mate_ref, tables, refs = refs[0], refs[1:8], refs[8:]
    if part:
        wave_refs, given_refs, out_refs, refs = refs[:2], refs[2:4], refs[4:6], refs[6:]
    else:
        wave_refs, out_refs, refs = refs[:2], refs[2:4], refs[4:]
    (count_vmem, count_smem, slot_list, band_list, weight_list), refs = refs[:5], refs[5:]
    scratch, sem = refs[:4], refs[4]
    sum_refs = refs[5:] if part == 2 else out_refs

    lane = lax.broadcasted_iota(jnp.int32, (8, LANES), 1)
    counts = jnp.zeros((8, LANES), F32)
    for s, (ref, at) in enumerate(bands):
        spare = ref[at, 0:16, :].astype(F32)[0:8]
        shift = (s * row_total - SPARE) % LANES
        moved = pltpu.roll(spare, shift, 1) if shift else spare
        counts = jnp.where(lane // row_total == s, moved, counts)
    count_vmem[...] = counts.astype(jnp.int32)
    copy = pltpu.make_async_copy(count_vmem, count_smem, sem)
    copy.start()
    if part:
        for sum_ref, given_ref in zip(sum_refs, given_refs):
            sum_ref[...] = given_ref[...]
    else:
        clear(sum_refs)
        spread_waves((band_refs[0][0], mate_ref[0]), tables[1], wave_refs)
    copy.wait()
    row = lax.axis_index("row")
    col = lax.axis_index("col")
    total = jnp.int32(0)
    done = jnp.int32(0)
    place = 0
    for step, stage in enumerate(stages):
        here = range(place, place + sum(len(block) for block in stage))
        place = here.stop
        for which, at in itertools.product(range(2), here):
            row_flip, col_flip = flips[at]
            row_place = flips.index((0, col_flip)) * row_total
            col_place = flips.index((row_flip, 0)) * row_total
            weight = count_smem[col ^ which, row_place + (row ^ row_flip)]
            if at or which:
                mirror = which * col_total + (col ^ col_flip)
                weight = weight + count_smem[mirror, col_place + row]
            slot_list[total] = at
            band_list[total] = which
            weight_list[total] = weight
            total = total + jnp.where(weight > 0, 1, 0)
        if step < 2:
            trios = jnp.minimum((total - done) // SIDE, CAPS[step])
            if step < part:
                done = done + trios * SIDE
    if part == 2:
        trios = (total - done + SIDE - 1) // SIDE
        for p in range(SIDE - 1):
            slot_list[total + p] = 0
            band_list[total + p] = 0
            weight_list[total + p] = 0

    def load_band(wanted, target, p):
        for place, (ref, at) in enumerate(bands):

            @pl.when(wanted == place)
            def _():
                target[:, p * LANES : (p + 1) * LANES] = ref[at]

    lists = (slot_list, band_list, weight_list)
    solve_trios(done, trios, lists, load_band, tables, wave_refs, sum_refs, scratch)
    if part == 2:
        pack_fields(sum_refs, out_refs)


def far_kernel(total_ref, slot_list, band_list, weight_list, bands_ref, own_ref, mate_ref, *refs):
    tables, out_refs, refs = refs[:7], refs[7:9], refs[9:]
    buffer, wave_refs, sum_refs, scratch = refs[0], refs[1:3], refs[3:5], refs[5:]
    spread_waves((own_ref[0], mate_ref[0]), tables[1], wave_refs)
    clear(sum_refs)

    def load_band(place, target, p):
        pltpu.sync_copy(bands_ref.at[place], buffer)
        target[:, p * LANES : (p + 1) * LANES] = buffer[...]

    lists = (slot_list, band_list, weight_list)
    trios = (total_ref[0] + SIDE - 1) // SIDE
    solve_trios(0, trios, lists, load_band, tables, wave_refs, sum_refs, scratch)
    pack_fields(sum_refs, out_refs)


def finish_kernel(own_ref, part_ref, out_ref, wide_ref, flat_ref):
    wide_ref[...] = own_ref[...] + part_ref[...]
    lane = lax.broadcasted_iota(jnp.int32, (1, LANES), 1)
    for third in range(SIDE):
        rows = min(CHUNK, LIVE // 16 - third * CHUNK)
        flat = [jnp.zeros((rows, LANES), F32)] * 5
        for q in range(16):
            row, offset = divmod(q * GX, LANES)
            shift = (offset - third * GX) % LANES
            values = wide_ref[pl.ds(q, rows, stride=16), :]
            values = pltpu.roll(values, shift, 1) if shift else values
            flat[row] = jnp.where(lane >= offset, values, flat[row])
            if offset + GX > LANES:
                flat[row + 1] = jnp.where(lane < offset + GX - LANES, values, flat[row + 1])
        for row in range(5):
            flat_ref[pl.ds(third * CHUNK * 5 + row, rows, stride=5), :] = flat[row]

    def to_lanes(k, lanes):
        out_ref[0:1, lanes] = flat_ref[k : k + 1, :]

    unroll_rows(to_lanes)


VMEM_SPEC = pl.BlockSpec(memory_space=pltpu.VMEM)
SMEM_SPEC = pl.BlockSpec(memory_space=pltpu.SMEM)
ANY_SPEC = pl.BlockSpec(memory_space=pl.ANY)
PARAMS = pltpu.CompilerParams(vmem_limit_bytes=VMEM_LIMIT)


def solve_tables():
    basis, _, _ = real_basis()
    return [
        spread_table(),
        repeat_table(),
        right_table(basis.T),
        right_table(basis),
        left_table(basis),
        left_table(basis.T),
        kernel_table(),
    ]


def solve_scratch():
    return [pltpu.VMEM((PACK, SIDE * LANES), BF16)] + [pltpu.VMEM((ROWS, LANES), F32)] * 3


def pair_of(rows):
    return [jax.ShapeDtypeStruct((rows, LANES), F32)] * 2


def swap(values, axis, size, flip):
    return lax.ppermute(values, axis, [(i, i ^ flip) for i in range(size)])


def count_pairs(pair_list, pair_count, row_total, col_total):
    slots = pair_list.shape[1]
    live = lax.iota(jnp.int32, slots) < pair_count[0]
    first = pair_list[0, :, 0][:, None, None] == lax.iota(jnp.int32, col_total)[None, :, None]
    second = pair_list[0, :, 1][:, None, None] == lax.iota(jnp.int32, row_total)[None, None, :]
    return jnp.sum((first & second & live[:, None, None]).astype(F32), axis=0)


def pack_band(orbitals, col_total, lists):
    return pl.pallas_call(
        functools.partial(pack_kernel, col_total),
        out_shape=jax.ShapeDtypeStruct((1, PACK, LANES), BF16),
        in_specs=[VMEM_SPEC] * (1 + len(lists)),
        out_specs=VMEM_SPEC,
        scratch_shapes=[pltpu.VMEM((FLAT_ROWS, LANES), F32), pltpu.VMEM((PACK, LANES), F32)],
        compiler_params=PARAMS,
        name="pack_band",
    )(orbitals, *lists)


def finish(own, part):
    return pl.pallas_call(
        finish_kernel,
        out_shape=jax.ShapeDtypeStruct((1, LIVE * GX), F32),
        in_specs=[VMEM_SPEC] * 2,
        out_specs=VMEM_SPEC,
        scratch_shapes=[pltpu.VMEM((PACK, LANES), F32), pltpu.VMEM((FLAT_ROWS, LANES), F32)],
        compiler_params=PARAMS,
        name="add_parts",
    )(own, part)


NEAR = (8, 4)
STAGES = (
    (((0, 0),), ((4, 0),), ((2, 0),), ((1, 0),), ((0, 2),)),
    (((4, 2), (2, 2)), ((5, 0), (1, 2)), ((6, 0), (3, 0)), ((6, 2),), ((5, 2),)),
    (((7, 0), (3, 2)), ((7, 2),)),
)
CAPS = (2, 2)


def near_part(row_total, col_total, part, operands):
    places = 2 * row_total * (col_total // 2) + SIDE
    out_shape = pair_of(ROWS)
    if part == 0:
        out_shape = out_shape * 2
    if part == 2:
        out_shape = pair_of(PACK)
    operands = list(operands)
    cost = pl.CostEstimate(flops=4 * 10**9, bytes_accessed=2 * 10**7, transcendentals=0)
    return pl.pallas_call(
        functools.partial(near_kernel, row_total, col_total, part),
        out_shape=out_shape,
        in_specs=[VMEM_SPEC] * len(operands),
        out_specs=[VMEM_SPEC] * len(out_shape),
        scratch_shapes=[
            pltpu.VMEM((8, LANES), jnp.int32),
            pltpu.SMEM((8, LANES), jnp.int32),
            pltpu.SMEM((places,), jnp.int32),
            pltpu.SMEM((places,), jnp.int32),
            pltpu.SMEM((places,), jnp.int32),
        ]
        + solve_scratch()
        + [pltpu.SemaphoreType.DMA]
        + [pltpu.VMEM((ROWS, LANES), F32)] * (2 if part == 2 else 0),
        compiler_params=PARAMS,
        cost_estimate=cost,
        name="solve_part",
    )(*operands)


def near_shards(row_total, col_total, orbitals, pair_list, pair_count):
    row_swap = lambda values, flip: swap(values, "row", row_total, flip)
    col_swap = lambda values, flip: swap(values, "col", col_total, flip)
    both = lambda a, b: jnp.concatenate([a, b], axis=0)
    live = lax.iota(jnp.int32, pair_list.shape[1])[None, :, None] < pair_count[0]
    pairs = jnp.where(live, pair_list, -row_total * col_total)
    own = pack_band(orbitals, col_total, [pairs, col_swap(pairs, 1)])
    x, y, z, w = col_swap(own, 2), row_swap(own, 1), row_swap(own, 2), row_swap(own, 4)
    mate = col_swap(own, 1)
    over_x, over_y, over_z = col_swap(both(w, z), 2), row_swap(both(w, x), 1), row_swap(both(w, y), 2)
    tables = [jnp.asarray(table) for table in solve_tables()]
    blocks = [own, w, z, y, x]
    *waves, sum0, sum1 = near_part(row_total, col_total, 0, [*blocks, mate, *tables])
    held = lax.optimization_barrier((sum0, sum1, over_x, over_y, over_z))
    sum0, sum1, over_x, over_y, over_z = held
    wzx = col_swap(over_z[:1], 2)
    wxy = row_swap(over_x[:1], 1)
    wyz_xyz = row_swap(over_y, 2)
    wzxy = row_swap(wzx, 1)
    arrivals = ((over_x, over_y, over_z, wzx, wxy), (wyz_xyz, wzxy))
    for part, arrived in enumerate(arrivals, 1):
        blocks += arrived
        operands = [*blocks, mate, *tables, *waves, sum0, sum1]
        sum0, sum1 = near_part(row_total, col_total, part, operands)
    return finish(sum0, col_swap(sum1, 1))


def far_shards(row_total, col_total, orbitals, pair_list, pair_count):
    counts = count_pairs(pair_list, pair_count, row_total, col_total)
    own = pack_band(orbitals, col_total, ())
    axes = ("row", "col")
    table = lax.all_gather(counts.reshape(-1), axes)
    table = table.reshape(row_total, col_total, col_total, row_total)
    wide = col_total // 2
    column = lax.all_gather(own[0], "row")
    columns = [column] + [swap(column, "col", col_total, 2 * x) for x in range(1, wide)]
    bands = jnp.concatenate(columns, axis=0)
    row = lax.axis_index("row")
    col = lax.axis_index("col")
    mine = jnp.stack([col, col ^ 1])
    other_col = ((col // 2) ^ lax.iota(jnp.int32, wide)) * 2 + col % 2
    other_row = lax.iota(jnp.int32, row_total)
    direct = table[row][other_col][:, mine]
    direct = jnp.transpose(direct, (1, 2, 0))
    mirror = table[:, :, :, row][:, mine][:, :, other_col]
    mirror = jnp.transpose(mirror, (1, 0, 2))
    same = (mine[:, None, None] == other_col[None, None, :]) & (other_row == row)[None, :, None]
    weights = (direct + jnp.where(same, 0.0, mirror)).astype(jnp.int32).reshape(-1)
    index = lax.iota(jnp.int32, weights.shape[0])
    order = jnp.argsort(jnp.where(weights > 0, 0, 1), stable=True)
    pad = lambda values: jnp.pad(values.astype(jnp.int32), (0, SIDE))
    slots = row_total * wide
    slot = order % slots
    band = (slot % wide) * row_total + slot // wide
    total = jnp.sum((weights > 0).astype(jnp.int32)).reshape(1)
    fields = pl.pallas_call(
        far_kernel,
        out_shape=pair_of(PACK),
        in_specs=[SMEM_SPEC] * 4 + [ANY_SPEC] + [VMEM_SPEC] * 9,
        out_specs=[VMEM_SPEC] * 2,
        scratch_shapes=[pltpu.VMEM((PACK, LANES), BF16)]
        + [pltpu.VMEM((ROWS, LANES), F32)] * 4
        + solve_scratch(),
        compiler_params=PARAMS,
        name="solve_pairs",
    )(
        total,
        pad(band),
        pad(order // slots),
        pad(weights[order]),
        bands,
        own,
        swap(own, "col", col_total, 1),
        *map(jnp.asarray, solve_tables()),
    )
    return finish(fields[0], swap(fields[1], "col", col_total, 1))


def solution(mesh):
    row_total, col_total = mesh.shape["row"], mesh.shape["col"]
    near = (row_total, col_total) == NEAR
    shards = near_shards if near else far_shards
    return jax.shard_map(
        functools.partial(shards, row_total, col_total),
        mesh=mesh,
        in_specs=(P(("row", "col"), None), P(("row", "col"), None, None), P(("row", "col"))),
        out_specs=P(("row", "col"), None),
        check_vma=False,
    )
```

```python
import functools
import itertools

import jax
import jax.numpy as jnp
import ml_dtypes
import numpy as np
from jax import lax
from jax.experimental import pallas as pl
from jax.experimental.pallas import tpu as pltpu
from jax.sharding import PartitionSpec as P

GX = 40
LANES = 128
SIDE = 3
THIRD = -(-GX // SIDE)
PACK = THIRD * GX
ROWS = SIDE * PACK
LIVE = GX * GX
SPARE = SIDE * GX
FLAT = LIVE * GX // LANES
CHUNK = PACK // 16
FLAT_ROWS = SIDE * CHUNK * 5 + 8
DUO = 2 * GX
QUAD = 4 * GX
GROUP = 10
VMEM_LIMIT = 20 * 1024 * 1024
screen_width = 0.9
F32 = jnp.float32
BF16 = jnp.bfloat16


def real_basis():
    half = GX // 2
    point = np.arange(GX)
    rows = [np.cos(2 * np.pi * (k * point % GX) / GX) for k in range(half + 1)]
    rows += [np.sin(2 * np.pi * (k * point % GX) / GX) for k in range(1, half)]
    frequency = np.concatenate([np.arange(half + 1), np.arange(1, half)])
    norm = np.where((frequency == 0) | (frequency == half), 1.0, 2.0) / GX
    return np.stack(rows), frequency, norm


def halves(table):
    high = table.astype(ml_dtypes.bfloat16)
    low = (table - high.astype(np.float64)).astype(ml_dtypes.bfloat16)
    return high, low


def left_table(table):
    high, low = halves(np.kron(np.eye(2), table))
    rows = [np.concatenate([part, part], axis=1) for part in (high, low)]
    return np.concatenate(rows, axis=0)


def right_table(table):
    wide = np.zeros((LANES, LANES))
    for p in range(SIDE):
        wide[p * GX : (p + 1) * GX, p * GX : (p + 1) * GX] = table
    high, low = halves(wide)
    both = np.concatenate([high, low], axis=1)
    return np.concatenate([both, both], axis=0)


def kernel_table():
    _, frequency, norm = real_basis()
    wave = frequency * (2.0 * np.pi / GX)
    squared = wave * wave
    total = squared[:, None, None] + squared[None, :, None] + squared[None, None, :]
    safe = np.where(total > 0, total, 1.0)
    screened = 4.0 * np.pi * (1.0 - np.exp(-safe / (4.0 * screen_width**2))) / safe
    kernel = np.where(total > 0, screened, np.pi / screen_width**2)
    kernel = kernel * norm[:, None, None] * norm[None, :, None] * norm[None, None, :]
    rows = np.swapaxes(kernel, 0, 1).reshape(LIVE, GX)
    out = np.zeros((LIVE, LANES), np.float32)
    for p in range(SIDE):
        out[:, p * GX : (p + 1) * GX] = rows
    return out


def place(out, row, col):
    for z in range(GX):
        out[row + z, col + z] = 1.0


def spread_table():
    out = np.zeros((SIDE * LANES, SIDE * LANES), np.float32)
    for third in range(SIDE):
        for p in range(SIDE):
            place(out, p * LANES + third * GX, third * LANES + p * GX)
    return out.astype(ml_dtypes.bfloat16)


def repeat_table():
    out = np.zeros((LANES, SIDE * LANES), np.float32)
    for third in range(SIDE):
        for p in range(SIDE):
            place(out, third * GX, third * LANES + p * GX)
    return out.astype(ml_dtypes.bfloat16)


def dot(a, b):
    return jnp.dot(a, b, preferred_element_type=F32)


def split(values):
    high = values.astype(BF16)
    return high, (values - high.astype(F32)).astype(BF16)


def contract_rows(table, values):
    both = dot(table, jnp.concatenate(split(values), axis=0))
    return both[:DUO] + both[DUO:]


def contract_lanes(values, table):
    both = dot(jnp.concatenate(split(values), axis=1), table)
    return both[:, :LANES] + both[:, LANES:]


def fold(values):
    return jnp.concatenate([values[:DUO], values[DUO:]], axis=1)


def unfold(values):
    return jnp.concatenate([values[:, :LANES], values[:, LANES:]], axis=0)


def in_groups(body):
    def group(outer, carry):
        body([outer * GROUP + inner for inner in range(GROUP)])
        return carry

    lax.fori_loop(0, GX // 4 // GROUP, group, 0)


def quad(step):
    return pl.ds(step * QUAD, QUAD)


def load_planes(ref, step):
    planes = [ref[pl.ds(step * 4 + i, GX, stride=GX), :] for i in range(4)]
    left = jnp.concatenate(planes[:2], axis=0)
    return jnp.concatenate([left, jnp.concatenate(planes[2:], axis=0)], axis=1)


def store_planes(ref, step, values):
    for i in range(4):
        rows, lanes = i % 2 * GX, i // 2 * LANES
        ref[pl.ds(step * 4 + i, GX, stride=GX), :] = values[rows : rows + GX, lanes : lanes + LANES]


def count_vector(list_ref, live_ref, first_row):
    pairs = list_ref[0]
    slots = pairs.shape[1]
    row = lax.broadcasted_iota(jnp.int32, (16, slots), 0) - first_row
    lane = lax.broadcasted_iota(jnp.int32, (LANES, slots), 0) - SPARE
    live = lax.broadcasted_iota(jnp.int32, (16, slots), 1) < live_ref[...]
    first = jnp.where((pairs[0:1] == row) & live, 1.0, 0.0)
    second = jnp.where(pairs[1:2] == lane, 1.0, 0.0)
    return lax.dot_general(first, second, (((1,), (1,)), ((), ())), preferred_element_type=F32)


def unroll_rows(copy):
    for k in range(FLAT):
        copy(k, slice(k * LANES, (k + 1) * LANES))


def pack_kernel(band_hbm, out_ref, band_ref, flat_ref, wide_ref, sem):
    copy = pltpu.make_async_copy(band_hbm, band_ref, sem)
    copy.start()
    copy.wait()

    def to_rows(k, lanes):
        flat_ref[k : k + 1, :] = band_ref[0:1, lanes].astype(F32)

    unroll_rows(to_rows)
    unused = FLAT_ROWS - FLAT
    flat_ref[FLAT:FLAT_ROWS, :] = jnp.zeros((unused, LANES), F32)
    lane = lax.broadcasted_iota(jnp.int32, (1, LANES), 1)
    for q in range(16):
        row, offset = divmod(q * GX, LANES)
        packed = jnp.zeros((CHUNK, LANES), F32)
        for third in range(SIDE):
            start = third * CHUNK * 5 + row
            values = flat_ref[pl.ds(start, CHUNK, stride=5), :]
            if offset + GX > LANES:
                after = flat_ref[pl.ds(start + 1, CHUNK, stride=5), :]
                values = jnp.where(lane >= offset, values, after)
            shift = (third * GX - offset) % LANES
            values = pltpu.roll(values, shift, 1) if shift else values
            packed = jnp.where(lane // GX == third, values, packed)
        wide_ref[pl.ds(q, CHUNK, stride=16), :] = packed
    out_ref[0] = wide_ref[...].astype(BF16)


def count_kernel(col_total, packed_ref, own_ref, own_live_ref, mate_ref, mate_live_ref, out_ref):
    out_ref[...] = packed_ref[...]
    counts = count_vector(own_ref, own_live_ref, 0)
    counts = counts + count_vector(mate_ref, mate_live_ref, col_total)
    out_ref[0, 0:16, :] = (packed_ref[0, 0:16, :].astype(F32) + counts).astype(BF16)


def spread_waves(own_bands, repeat_ref, wave_refs):
    for band, wave_ref in zip(own_bands, wave_refs):
        wide = dot(band, repeat_ref[...])
        for third in range(SIDE):
            wave_ref[pl.ds(third * PACK, PACK), :] = wide[:, third * LANES : (third + 1) * LANES]


def clear(sum_refs):
    for sum_ref in sum_refs:
        sum_ref[...] = jnp.zeros_like(sum_ref)


def lane_side():
    return lax.broadcasted_iota(jnp.int32, (1, LANES), 1) // GX


def solve_trios(first, count, lists, load_band, tables, wave_refs, sum_refs, scratch):
    spread_ref, _, z_ref, z_back_ref, row_ref, row_back_ref, kernel_ref = tables
    trio_ref, partner_ref, work_ref, work2_ref = scratch
    slot_list, band_list, weight_list = lists
    side = lane_side()

    def by_side(values):
        row = jnp.zeros((1, LANES), F32)
        for p in range(SIDE):
            row = jnp.where(side == p, values[p].astype(F32), row)
        return row

    def trio(at, carry):
        places = [first + at * SIDE + p for p in range(SIDE)]
        for p, place in enumerate(places):
            load_band(slot_list[place], trio_ref, p)
        bands = [band_list[place] for place in places]
        weights = [weight_list[place] for place in places]
        is_mate = by_side(bands) > 0.5
        scales = [
            by_side([jnp.where(bands[p] == which, weights[p], 0) for p in range(SIDE)])
            for which in range(2)
        ]
        wide = dot(trio_ref[...], spread_ref[...])
        for third in range(SIDE):
            partner_ref[pl.ds(third * PACK, PACK), :] = wide[:, third * LANES : (third + 1) * LANES]

        def forward(steps):
            values = []
            for step in steps:
                wave = jnp.where(is_mate, wave_refs[1][quad(step), :], wave_refs[0][quad(step), :])
                values.append(partner_ref[quad(step), :] * wave)
            values = [contract_lanes(v, z_ref[...]) for v in values]
            values = [contract_rows(row_ref[...], fold(v)) for v in values]
            for step, v in zip(steps, values):
                work_ref[quad(step), :] = unfold(v)

        def across(steps):
            values = [load_planes(work_ref, step) for step in steps]
            values = [contract_rows(row_ref[...], v) for v in values]
            values = [v * fold(kernel_ref[quad(step), :]) for step, v in zip(steps, values)]
            values = [contract_rows(row_back_ref[...], v) for v in values]
            for step, v in zip(steps, values):
                store_planes(work2_ref, step, v)

        def back(steps):
            values = [fold(work2_ref[quad(step), :]) for step in steps]
            values = [unfold(contract_rows(row_back_ref[...], v)) for v in values]
            values = [contract_lanes(v, z_back_ref[...]) for v in values]
            for step, v in zip(steps, values):
                v = v * partner_ref[quad(step), :]
                for sum_ref, scale in zip(sum_refs, scales):
                    sum_ref[quad(step), :] = sum_ref[quad(step), :] + v * scale

        for phase in (forward, across, back):
            in_groups(phase)
        return carry

    lax.fori_loop(0, count, trio, 0)


def flat_fields(sum_refs, out_refs):
    lane = lax.broadcasted_iota(jnp.int32, (1, LANES), 1)
    rows = LIVE // 16
    for sum_ref, out_ref in zip(sum_refs, out_refs):
        flat = [jnp.zeros((rows, LANES), F32)] * 5
        for q in range(16):
            row, offset = divmod(q * GX, LANES)
            values = sum_ref[pl.ds(q, rows, stride=16), :]
            moved = jnp.zeros((rows, LANES), F32)
            for p in range(SIDE):
                shift = (offset - p * GX) % LANES
                moved = moved + (pltpu.roll(values, shift, 1) if shift else values)
            flat[row] = jnp.where(lane >= offset, moved, flat[row])
            if offset + GX > LANES:
                flat[row + 1] = jnp.where(lane < offset + GX - LANES, moved, flat[row + 1])
        for row in range(5):
            out_ref[pl.ds(row, rows, stride=5), :] = flat[row]


def near_kernel(row_total, col_total, part, *refs):
    stages = STAGES[: part + 1]
    blocks = [block for stage in stages for block in stage]
    band_refs, refs = refs[: len(blocks)], refs[len(blocks) :]
    bands = [(ref, at) for ref, block in zip(band_refs, blocks) for at in range(len(block))]
    flips = [flip for block in blocks for flip in block]
    mate_ref, tables, refs = refs[0], refs[1:8], refs[8:]
    if part:
        wave_refs, given_refs, out_refs, refs = refs[:2], refs[2:4], refs[4:6], refs[6:]
    else:
        wave_refs, out_refs, refs = refs[:2], refs[2:4], refs[4:]
    (count_vmem, count_smem, slot_list, band_list, weight_list), refs = refs[:5], refs[5:]
    scratch, sem = refs[:4], refs[4]
    sum_refs = refs[5:] if part == 2 else out_refs

    lane = lax.broadcasted_iota(jnp.int32, (8, LANES), 1)
    counts = jnp.zeros((8, LANES), F32)
    for s, (ref, at) in enumerate(bands):
        spare = ref[at, 0:16, :].astype(F32)[0:8]
        shift = (s * row_total - SPARE) % LANES
        moved = pltpu.roll(spare, shift, 1) if shift else spare
        counts = jnp.where(lane // row_total == s, moved, counts)
    count_vmem[...] = counts.astype(jnp.int32)
    copy = pltpu.make_async_copy(count_vmem, count_smem, sem)
    copy.start()
    if part:
        for sum_ref, given_ref in zip(sum_refs, given_refs):
            sum_ref[...] = given_ref[...]
    else:
        clear(sum_refs)
        spread_waves((band_refs[0][0], mate_ref[0]), tables[1], wave_refs)
    copy.wait()
    row = lax.axis_index("row")
    col = lax.axis_index("col")
    total = jnp.int32(0)
    done = jnp.int32(0)
    place = 0
    for step, stage in enumerate(stages):
        here = range(place, place + sum(len(block) for block in stage))
        place = here.stop
        for which, at in itertools.product(range(2), here):
            row_flip, col_flip = flips[at]
            row_place = flips.index((0, col_flip)) * row_total
            col_place = flips.index((row_flip, 0)) * row_total
            weight = count_smem[col ^ which, row_place + (row ^ row_flip)]
            if at or which:
                mirror = which * col_total + (col ^ col_flip)
                weight = weight + count_smem[mirror, col_place + row]
            slot_list[total] = at
            band_list[total] = which
            weight_list[total] = weight
            total = total + jnp.where(weight > 0, 1, 0)
        if step < 2:
            trios = jnp.minimum((total - done) // SIDE, CAPS[step])
            if step < part:
                done = done + trios * SIDE
    if part == 2:
        trios = (total - done + SIDE - 1) // SIDE
        for p in range(SIDE - 1):
            slot_list[total + p] = 0
            band_list[total + p] = 0
            weight_list[total + p] = 0

    def load_band(wanted, target, p):
        for place, (ref, at) in enumerate(bands):

            @pl.when(wanted == place)
            def _():
                target[:, p * LANES : (p + 1) * LANES] = ref[at]

    lists = (slot_list, band_list, weight_list)
    solve_trios(done, trios, lists, load_band, tables, wave_refs, sum_refs, scratch)
    if part == 2:
        flat_fields(sum_refs, out_refs)


def far_kernel(total_ref, slot_list, band_list, weight_list, bands_ref, own_ref, mate_ref, *refs):
    tables, out_refs, refs = refs[:7], refs[7:9], refs[9:]
    buffer, wave_refs, sum_refs, scratch = refs[0], refs[1:3], refs[3:5], refs[5:]
    spread_waves((own_ref[0], mate_ref[0]), tables[1], wave_refs)
    clear(sum_refs)

    def load_band(place, target, p):
        pltpu.sync_copy(bands_ref.at[place], buffer)
        target[:, p * LANES : (p + 1) * LANES] = buffer[...]

    lists = (slot_list, band_list, weight_list)
    trios = (total_ref[0] + SIDE - 1) // SIDE
    solve_trios(0, trios, lists, load_band, tables, wave_refs, sum_refs, scratch)
    flat_fields(sum_refs, out_refs)


def finish_kernel(own_ref, part_ref, out_ref):
    def to_lanes(k, lanes):
        out_ref[0:1, lanes] = own_ref[k : k + 1, :] + part_ref[k : k + 1, :]

    unroll_rows(to_lanes)


VMEM_SPEC = pl.BlockSpec(memory_space=pltpu.VMEM)
SMEM_SPEC = pl.BlockSpec(memory_space=pltpu.SMEM)
ANY_SPEC = pl.BlockSpec(memory_space=pl.ANY)
PARAMS = pltpu.CompilerParams(vmem_limit_bytes=VMEM_LIMIT)


def solve_tables():
    basis, _, _ = real_basis()
    return [
        spread_table(),
        repeat_table(),
        right_table(basis.T),
        right_table(basis),
        left_table(basis),
        left_table(basis.T),
        kernel_table(),
    ]


def solve_scratch():
    return [pltpu.VMEM((PACK, SIDE * LANES), BF16)] + [pltpu.VMEM((ROWS, LANES), F32)] * 3


def pair_of(rows):
    return [jax.ShapeDtypeStruct((rows, LANES), F32)] * 2


def swap(values, axis, size, flip):
    return lax.ppermute(values, axis, [(i, i ^ flip) for i in range(size)])


def count_pairs(pair_list, pair_count, row_total, col_total):
    slots = pair_list.shape[1]
    live = lax.iota(jnp.int32, slots) < pair_count[0]
    first = pair_list[0, :, 0][:, None, None] == lax.iota(jnp.int32, col_total)[None, :, None]
    second = pair_list[0, :, 1][:, None, None] == lax.iota(jnp.int32, row_total)[None, None, :]
    return jnp.sum((first & second & live[:, None, None]).astype(F32), axis=0)


def pack_band(orbitals):
    return pl.pallas_call(
        pack_kernel,
        out_shape=jax.ShapeDtypeStruct((1, PACK, LANES), BF16),
        in_specs=[ANY_SPEC],
        out_specs=VMEM_SPEC,
        scratch_shapes=[
            pltpu.VMEM(orbitals.shape, BF16),
            pltpu.VMEM((FLAT_ROWS, LANES), F32),
            pltpu.VMEM((PACK, LANES), F32),
            pltpu.SemaphoreType.DMA,
        ],
        compiler_params=PARAMS,
        name="pack_band",
    )(orbitals)


def add_counts(packed, col_total, lists):
    return pl.pallas_call(
        functools.partial(count_kernel, col_total),
        out_shape=jax.ShapeDtypeStruct(packed.shape, BF16),
        in_specs=[VMEM_SPEC] * 5,
        out_specs=VMEM_SPEC,
        compiler_params=PARAMS,
        name="add_counts",
    )(packed, *lists)


def finish(own, part):
    return pl.pallas_call(
        finish_kernel,
        out_shape=jax.ShapeDtypeStruct((1, LIVE * GX), F32),
        in_specs=[VMEM_SPEC] * 2,
        out_specs=VMEM_SPEC,
        compiler_params=PARAMS,
        name="add_parts",
    )(own, part)


NEAR = (8, 4)
STAGES = (
    (((0, 0),), ((4, 0),), ((2, 0),), ((1, 0),), ((0, 2),)),
    (((4, 2), (2, 2)), ((5, 0), (1, 2)), ((6, 0), (3, 0)), ((6, 2),), ((5, 2),)),
    (((7, 0), (3, 2)), ((7, 2),)),
)
CAPS = (2, 2)


def near_part(row_total, col_total, part, operands):
    places = 2 * row_total * (col_total // 2) + SIDE
    out_shape = pair_of(ROWS)
    if part == 0:
        out_shape = out_shape * 2
    if part == 2:
        out_shape = pair_of(FLAT)
    operands = list(operands)
    cost = pl.CostEstimate(flops=4 * 10**9, bytes_accessed=2 * 10**7, transcendentals=0)
    return pl.pallas_call(
        functools.partial(near_kernel, row_total, col_total, part),
        out_shape=out_shape,
        in_specs=[VMEM_SPEC] * len(operands),
        out_specs=[VMEM_SPEC] * len(out_shape),
        scratch_shapes=[
            pltpu.VMEM((8, LANES), jnp.int32),
            pltpu.SMEM((8, LANES), jnp.int32),
            pltpu.SMEM((places,), jnp.int32),
            pltpu.SMEM((places,), jnp.int32),
            pltpu.SMEM((places,), jnp.int32),
        ]
        + solve_scratch()
        + [pltpu.SemaphoreType.DMA]
        + [pltpu.VMEM((ROWS, LANES), F32)] * (2 if part == 2 else 0),
        compiler_params=PARAMS,
        cost_estimate=cost,
        name="solve_part",
    )(*operands)


def near_shards(row_total, col_total, orbitals, pair_list, pair_count):
    row_swap = lambda values, flip: swap(values, "row", row_total, flip)
    col_swap = lambda values, flip: swap(values, "col", col_total, flip)
    both = lambda a, b: jnp.concatenate([a, b], axis=0)
    pairs = jnp.swapaxes(pair_list, 1, 2)
    lists = (pairs, pair_count.reshape(1, 1), col_swap(pairs, 1), col_swap(pair_count, 1).reshape(1, 1))
    own = add_counts(pack_band(orbitals), col_total, lists)
    x, y, z, w = col_swap(own, 2), row_swap(own, 1), row_swap(own, 2), row_swap(own, 4)
    mate = col_swap(own, 1)
    over_x, over_y, over_z = col_swap(both(w, z), 2), row_swap(both(w, x), 1), row_swap(both(w, y), 2)
    tables = [jnp.asarray(table) for table in solve_tables()]
    blocks = [own, w, z, y, x]
    *waves, sum0, sum1 = near_part(row_total, col_total, 0, [*blocks, mate, *tables])
    held = lax.optimization_barrier((sum0, sum1, over_x, over_y, over_z))
    sum0, sum1, over_x, over_y, over_z = held
    wzx = col_swap(over_z[:1], 2)
    wxy = row_swap(over_x[:1], 1)
    wyz_xyz = row_swap(over_y, 2)
    wzxy = row_swap(wzx, 1)
    arrivals = ((over_x, over_y, over_z, wzx, wxy), (wyz_xyz, wzxy))
    for part, arrived in enumerate(arrivals, 1):
        blocks += arrived
        operands = [*blocks, mate, *tables, *waves, sum0, sum1]
        sum0, sum1 = near_part(row_total, col_total, part, operands)
    return finish(sum0, col_swap(sum1, 1))


def far_shards(row_total, col_total, orbitals, pair_list, pair_count):
    counts = count_pairs(pair_list, pair_count, row_total, col_total)
    own = pack_band(orbitals)
    axes = ("row", "col")
    table = lax.all_gather(counts.reshape(-1), axes)
    table = table.reshape(row_total, col_total, col_total, row_total)
    wide = col_total // 2
    column = lax.all_gather(own[0], "row")
    columns = [column] + [swap(column, "col", col_total, 2 * x) for x in range(1, wide)]
    bands = jnp.concatenate(columns, axis=0)
    row = lax.axis_index("row")
    col = lax.axis_index("col")
    mine = jnp.stack([col, col ^ 1])
    other_col = ((col // 2) ^ lax.iota(jnp.int32, wide)) * 2 + col % 2
    other_row = lax.iota(jnp.int32, row_total)
    direct = table[row][other_col][:, mine]
    direct = jnp.transpose(direct, (1, 2, 0))
    mirror = table[:, :, :, row][:, mine][:, :, other_col]
    mirror = jnp.transpose(mirror, (1, 0, 2))
    same = (mine[:, None, None] == other_col[None, None, :]) & (other_row == row)[None, :, None]
    weights = (direct + jnp.where(same, 0.0, mirror)).astype(jnp.int32).reshape(-1)
    index = lax.iota(jnp.int32, weights.shape[0])
    order = jnp.argsort(jnp.where(weights > 0, 0, 1), stable=True)
    pad = lambda values: jnp.pad(values.astype(jnp.int32), (0, SIDE))
    slots = row_total * wide
    slot = order % slots
    band = (slot % wide) * row_total + slot // wide
    total = jnp.sum((weights > 0).astype(jnp.int32)).reshape(1)
    fields = pl.pallas_call(
        far_kernel,
        out_shape=pair_of(FLAT),
        in_specs=[SMEM_SPEC] * 4 + [ANY_SPEC] + [VMEM_SPEC] * 9,
        out_specs=[VMEM_SPEC] * 2,
        scratch_shapes=[pltpu.VMEM((PACK, LANES), BF16)]
        + [pltpu.VMEM((ROWS, LANES), F32)] * 4
        + solve_scratch(),
        compiler_params=PARAMS,
        name="solve_pairs",
    )(
        total,
        pad(band),
        pad(order // slots),
        pad(weights[order]),
        bands,
        own,
        swap(own, "col", col_total, 1),
        *map(jnp.asarray, solve_tables()),
    )
    return finish(fields[0], swap(fields[1], "col", col_total, 1))


def solution(mesh):
    row_total, col_total = mesh.shape["row"], mesh.shape["col"]
    near = (row_total, col_total) == NEAR
    shards = near_shards if near else far_shards
    return jax.shard_map(
        functools.partial(shards, row_total, col_total),
        mesh=mesh,
        in_specs=(P(("row", "col"), None), P(("row", "col"), None, None), P(("row", "col"))),
        out_specs=P(("row", "col"), None),
        check_vma=False,
    )
```

```python
import functools
import itertools

import jax
import jax.numpy as jnp
import ml_dtypes
import numpy as np
from jax import lax
from jax.experimental import pallas as pl
from jax.experimental.pallas import tpu as pltpu
from jax.sharding import PartitionSpec as P

GX = 40
LANES = 128
SIDE = 3
THIRD = -(-GX // SIDE)
PACK = THIRD * GX
ROWS = SIDE * PACK
LIVE = GX * GX
SPARE = SIDE * GX
FLAT = LIVE * GX // LANES
CHUNK = PACK // 16
FLAT_ROWS = SIDE * CHUNK * 5 + 8
DUO = 2 * GX
QUAD = 4 * GX
GROUP = 10
VMEM_LIMIT = 20 * 1024 * 1024
screen_width = 0.9
F32 = jnp.float32
BF16 = jnp.bfloat16


def real_basis():
    half = GX // 2
    point = np.arange(GX)
    rows = [np.cos(2 * np.pi * (k * point % GX) / GX) for k in range(half + 1)]
    rows += [np.sin(2 * np.pi * (k * point % GX) / GX) for k in range(1, half)]
    frequency = np.concatenate([np.arange(half + 1), np.arange(1, half)])
    norm = np.where((frequency == 0) | (frequency == half), 1.0, 2.0) / GX
    return np.stack(rows), frequency, norm


def halves(table):
    high = table.astype(ml_dtypes.bfloat16)
    low = (table - high.astype(np.float64)).astype(ml_dtypes.bfloat16)
    return high, low


def left_table(table):
    high, low = halves(np.kron(np.eye(2), table))
    return np.concatenate([high, low, high], axis=1)


def right_table(table):
    wide = np.zeros((LANES, LANES))
    for p in range(SIDE):
        wide[p * GX : (p + 1) * GX, p * GX : (p + 1) * GX] = table
    high, low = halves(wide)
    both = np.concatenate([high, low], axis=1)
    return np.concatenate([both, both], axis=0)


def kernel_table():
    _, frequency, norm = real_basis()
    wave = frequency * (2.0 * np.pi / GX)
    squared = wave * wave
    total = squared[:, None, None] + squared[None, :, None] + squared[None, None, :]
    safe = np.where(total > 0, total, 1.0)
    screened = 4.0 * np.pi * (1.0 - np.exp(-safe / (4.0 * screen_width**2))) / safe
    kernel = np.where(total > 0, screened, np.pi / screen_width**2)
    kernel = kernel * norm[:, None, None] * norm[None, :, None] * norm[None, None, :]
    rows = np.swapaxes(kernel, 0, 1).reshape(LIVE, GX)
    out = np.zeros((LIVE, LANES), np.float32)
    for p in range(SIDE):
        out[:, p * GX : (p + 1) * GX] = rows
    return out


def place(out, row, col):
    for z in range(GX):
        out[row + z, col + z] = 1.0


def spread_table():
    out = np.zeros((SIDE * LANES, SIDE * LANES), np.float32)
    for third in range(SIDE):
        for p in range(SIDE):
            place(out, p * LANES + third * GX, third * LANES + p * GX)
    return out.astype(ml_dtypes.bfloat16)


def repeat_table():
    out = np.zeros((LANES, SIDE * LANES), np.float32)
    for third in range(SIDE):
        for p in range(SIDE):
            place(out, third * GX, third * LANES + p * GX)
    return out.astype(ml_dtypes.bfloat16)


def dot(a, b):
    return jnp.dot(a, b, preferred_element_type=F32)


def split(values):
    high = values.astype(BF16)
    return high, (values - high.astype(F32)).astype(BF16)


def contract_rows(table, values):
    high, low = split(values)
    return dot(table, jnp.concatenate([high, high, low], axis=0))


def contract_lanes(values, table):
    both = dot(jnp.concatenate(split(values), axis=1), table)
    return both[:, :LANES] + both[:, LANES:]


def fold(values):
    return jnp.concatenate([values[:DUO], values[DUO:]], axis=1)


def unfold(values):
    return jnp.concatenate([values[:, :LANES], values[:, LANES:]], axis=0)


def in_groups(body):
    def group(outer, carry):
        body([outer * GROUP + inner for inner in range(GROUP)])
        return carry

    lax.fori_loop(0, GX // 4 // GROUP, group, 0)


def quad(step):
    return pl.ds(step * QUAD, QUAD)


def load_planes(ref, step):
    planes = [ref[pl.ds(step * 4 + i, GX, stride=GX), :] for i in range(4)]
    left = jnp.concatenate(planes[:2], axis=0)
    return jnp.concatenate([left, jnp.concatenate(planes[2:], axis=0)], axis=1)


def store_planes(ref, step, values):
    for i in range(4):
        rows, lanes = i % 2 * GX, i // 2 * LANES
        ref[pl.ds(step * 4 + i, GX, stride=GX), :] = values[rows : rows + GX, lanes : lanes + LANES]


def count_vector(pairs, live):
    slots = pairs.shape[1]
    row = lax.broadcasted_iota(jnp.int32, (16, slots), 0)
    lane = lax.broadcasted_iota(jnp.int32, (LANES, slots), 0) - SPARE
    first = (pairs[0:1] == row) & (lax.broadcasted_iota(jnp.int32, (16, slots), 1) < live)
    second = jnp.where(pairs[1:2] == lane, 1.0, 0.0)
    contract = (((1,), (1,)), ((), ()))
    return lax.dot_general(jnp.where(first, 1.0, 0.0), second, contract, preferred_element_type=F32)


def unroll_rows(copy):
    for k in range(FLAT):
        copy(k, slice(k * LANES, (k + 1) * LANES))


def pack_kernel(band_ref, out_ref, flat_ref, wide_ref):
    def to_rows(k, lanes):
        flat_ref[k : k + 1, :] = band_ref[0:1, lanes].astype(F32)

    unroll_rows(to_rows)
    unused = FLAT_ROWS - FLAT
    flat_ref[FLAT:FLAT_ROWS, :] = jnp.zeros((unused, LANES), F32)
    lane = lax.broadcasted_iota(jnp.int32, (1, LANES), 1)
    for q in range(16):
        row, offset = divmod(q * GX, LANES)
        packed = jnp.zeros((CHUNK, LANES), F32)
        for third in range(SIDE):
            start = third * CHUNK * 5 + row
            values = flat_ref[pl.ds(start, CHUNK, stride=5), :]
            if offset + GX > LANES:
                after = flat_ref[pl.ds(start + 1, CHUNK, stride=5), :]
                values = jnp.where(lane >= offset, values, after)
            shift = (third * GX - offset) % LANES
            values = pltpu.roll(values, shift, 1) if shift else values
            packed = jnp.where(lane // GX == third, values, packed)
        wide_ref[pl.ds(q, CHUNK, stride=16), :] = packed
    out_ref[0] = wide_ref[...].astype(BF16)


def list_kernel(pairs_ref, live_ref, out_ref):
    out_ref[...] = count_vector(pairs_ref[0], live_ref[...])


def count_kernel(col_total, packed_ref, own_ref, mate_ref, out_ref):
    out_ref[...] = packed_ref[...]
    counts = own_ref[...] + pltpu.roll(mate_ref[...], col_total, 0)
    out_ref[0, 0:16, :] = (packed_ref[0, 0:16, :].astype(F32) + counts).astype(BF16)


def spread_waves(own_bands, repeat_ref, wave_refs):
    for band, wave_ref in zip(own_bands, wave_refs):
        wide = dot(band, repeat_ref[...])
        for third in range(SIDE):
            wave_ref[pl.ds(third * PACK, PACK), :] = wide[:, third * LANES : (third + 1) * LANES]


def clear(sum_refs):
    for sum_ref in sum_refs:
        sum_ref[...] = jnp.zeros_like(sum_ref)


def lane_side():
    return lax.broadcasted_iota(jnp.int32, (1, LANES), 1) // GX


def solve_trios(first, count, lists, load_band, tables, wave_refs, sum_refs, scratch):
    spread_ref, _, z_ref, z_back_ref, row_ref, row_back_ref, kernel_ref = tables
    trio_ref, partner_ref, work_ref, work2_ref = scratch
    slot_list, band_list, weight_list = lists
    side = lane_side()

    def by_side(values):
        row = jnp.zeros((1, LANES), F32)
        for p in range(SIDE):
            row = jnp.where(side == p, values[p].astype(F32), row)
        return row

    def trio(at, carry):
        places = [first + at * SIDE + p for p in range(SIDE)]
        for p, place in enumerate(places):
            load_band(slot_list[place], trio_ref, p)
        bands = [band_list[place] for place in places]
        weights = [weight_list[place] for place in places]
        is_mate = by_side(bands) > 0.5
        scales = [
            by_side([jnp.where(bands[p] == which, weights[p], 0) for p in range(SIDE)])
            for which in range(2)
        ]
        wide = dot(trio_ref[...], spread_ref[...])
        for third in range(SIDE):
            partner_ref[pl.ds(third * PACK, PACK), :] = wide[:, third * LANES : (third + 1) * LANES]

        def forward(steps):
            values = []
            for step in steps:
                wave = jnp.where(is_mate, wave_refs[1][quad(step), :], wave_refs[0][quad(step), :])
                values.append(partner_ref[quad(step), :] * wave)
            values = [contract_lanes(v, z_ref[...]) for v in values]
            values = [contract_rows(row_ref[...], fold(v)) for v in values]
            for step, v in zip(steps, values):
                work_ref[quad(step), :] = unfold(v)

        def across(steps):
            values = [load_planes(work_ref, step) for step in steps]
            values = [contract_rows(row_ref[...], v) for v in values]
            values = [v * fold(kernel_ref[quad(step), :]) for step, v in zip(steps, values)]
            values = [contract_rows(row_back_ref[...], v) for v in values]
            for step, v in zip(steps, values):
                store_planes(work2_ref, step, v)

        def back(steps):
            values = [fold(work2_ref[quad(step), :]) for step in steps]
            values = [unfold(contract_rows(row_back_ref[...], v)) for v in values]
            values = [contract_lanes(v, z_back_ref[...]) for v in values]
            for step, v in zip(steps, values):
                v = v * partner_ref[quad(step), :]
                for sum_ref, scale in zip(sum_refs, scales):
                    sum_ref[quad(step), :] = sum_ref[quad(step), :] + v * scale

        for phase in (forward, across, back):
            in_groups(phase)
        return carry

    lax.fori_loop(0, count, trio, 0)


def flat_fields(sum_refs, out_refs):
    lane = lax.broadcasted_iota(jnp.int32, (1, LANES), 1)
    rows = LIVE // 16
    for sum_ref, out_ref in zip(sum_refs, out_refs):
        flat = [jnp.zeros((rows, LANES), F32)] * 5
        for q in range(16):
            row, offset = divmod(q * GX, LANES)
            values = sum_ref[pl.ds(q, rows, stride=16), :]
            moved = jnp.zeros((rows, LANES), F32)
            for p in range(SIDE):
                shift = (offset - p * GX) % LANES
                moved = moved + (pltpu.roll(values, shift, 1) if shift else values)
            flat[row] = jnp.where(lane >= offset, moved, flat[row])
            if offset + GX > LANES:
                flat[row + 1] = jnp.where(lane < offset + GX - LANES, moved, flat[row + 1])
        for row in range(5):
            out_ref[pl.ds(row, rows, stride=5), :] = flat[row]


def near_kernel(row_total, col_total, part, *refs):
    stages = STAGES[: part + 1]
    blocks = [block for stage in stages for block in stage]
    band_refs, refs = refs[: len(blocks)], refs[len(blocks) :]
    bands = [(ref, at) for ref, block in zip(band_refs, blocks) for at in range(len(block))]
    flips = [flip for block in blocks for flip in block]
    mate_ref, tables, refs = refs[0], refs[1:8], refs[8:]
    if part:
        wave_refs, given_refs, out_refs, refs = refs[:2], refs[2:4], refs[4:6], refs[6:]
    else:
        wave_refs, out_refs, refs = refs[:2], refs[2:4], refs[4:]
    (count_vmem, count_smem, slot_list, band_list, weight_list), refs = refs[:5], refs[5:]
    scratch, sem = refs[:4], refs[4]
    sum_refs = refs[5:] if part == 2 else out_refs

    lane = lax.broadcasted_iota(jnp.int32, (8, LANES), 1)
    counts = jnp.zeros((8, LANES), F32)
    for s, (ref, at) in enumerate(bands):
        spare = ref[at, 0:16, :].astype(F32)[0:8]
        shift = (s * row_total - SPARE) % LANES
        moved = pltpu.roll(spare, shift, 1) if shift else spare
        counts = jnp.where(lane // row_total == s, moved, counts)
    count_vmem[...] = counts.astype(jnp.int32)
    copy = pltpu.make_async_copy(count_vmem, count_smem, sem)
    copy.start()
    if part:
        for sum_ref, given_ref in zip(sum_refs, given_refs):
            sum_ref[...] = given_ref[...]
    else:
        clear(sum_refs)
        spread_waves((band_refs[0][0], mate_ref[0]), tables[1], wave_refs)
    copy.wait()
    row = lax.axis_index("row")
    col = lax.axis_index("col")
    total = jnp.int32(0)
    done = jnp.int32(0)
    place = 0
    for step, stage in enumerate(stages):
        here = range(place, place + sum(len(block) for block in stage))
        place = here.stop
        for which, at in itertools.product(range(2), here):
            row_flip, col_flip = flips[at]
            row_place = flips.index((0, col_flip)) * row_total
            col_place = flips.index((row_flip, 0)) * row_total
            weight = count_smem[col ^ which, row_place + (row ^ row_flip)]
            if at or which:
                mirror = which * col_total + (col ^ col_flip)
                weight = weight + count_smem[mirror, col_place + row]
            slot_list[total] = at
            band_list[total] = which
            weight_list[total] = weight
            total = total + jnp.where(weight > 0, 1, 0)
        if step < 2:
            trios = jnp.minimum((total - done) // SIDE, CAPS[step])
            if step < part:
                done = done + trios * SIDE
    if part == 2:
        trios = (total - done + SIDE - 1) // SIDE
        for p in range(SIDE - 1):
            slot_list[total + p] = 0
            band_list[total + p] = 0
            weight_list[total + p] = 0

    def load_band(wanted, target, p):
        for place, (ref, at) in enumerate(bands):

            @pl.when(wanted == place)
            def _():
                target[:, p * LANES : (p + 1) * LANES] = ref[at]

    lists = (slot_list, band_list, weight_list)
    solve_trios(done, trios, lists, load_band, tables, wave_refs, sum_refs, scratch)
    if part == 2:
        flat_fields(sum_refs, out_refs)


def far_kernel(total_ref, slot_list, band_list, weight_list, bands_ref, own_ref, mate_ref, *refs):
    tables, out_refs, refs = refs[:7], refs[7:9], refs[9:]
    buffer, wave_refs, sum_refs, scratch = refs[0], refs[1:3], refs[3:5], refs[5:]
    spread_waves((own_ref[0], mate_ref[0]), tables[1], wave_refs)
    clear(sum_refs)

    def load_band(place, target, p):
        pltpu.sync_copy(bands_ref.at[place], buffer)
        target[:, p * LANES : (p + 1) * LANES] = buffer[...]

    lists = (slot_list, band_list, weight_list)
    trios = (total_ref[0] + SIDE - 1) // SIDE
    solve_trios(0, trios, lists, load_band, tables, wave_refs, sum_refs, scratch)
    flat_fields(sum_refs, out_refs)


def finish_kernel(own_ref, part_ref, out_ref):
    def to_lanes(k, lanes):
        out_ref[0:1, lanes] = own_ref[k : k + 1, :] + part_ref[k : k + 1, :]

    unroll_rows(to_lanes)


VMEM_SPEC = pl.BlockSpec(memory_space=pltpu.VMEM)
SMEM_SPEC = pl.BlockSpec(memory_space=pltpu.SMEM)
ANY_SPEC = pl.BlockSpec(memory_space=pl.ANY)
PARAMS = pltpu.CompilerParams(vmem_limit_bytes=VMEM_LIMIT)


def solve_tables():
    basis, _, _ = real_basis()
    return [
        spread_table(),
        repeat_table(),
        right_table(basis.T),
        right_table(basis),
        left_table(basis),
        left_table(basis.T),
        kernel_table(),
    ]


def solve_scratch():
    return [pltpu.VMEM((PACK, SIDE * LANES), BF16)] + [pltpu.VMEM((ROWS, LANES), F32)] * 3


def pair_of(rows):
    return [jax.ShapeDtypeStruct((rows, LANES), F32)] * 2


def swap(values, axis, size, flip):
    return lax.ppermute(values, axis, [(i, i ^ flip) for i in range(size)])


def count_pairs(pair_list, pair_count, row_total, col_total):
    slots = pair_list.shape[1]
    live = lax.iota(jnp.int32, slots) < pair_count[0]
    first = pair_list[0, :, 0][:, None, None] == lax.iota(jnp.int32, col_total)[None, :, None]
    second = pair_list[0, :, 1][:, None, None] == lax.iota(jnp.int32, row_total)[None, None, :]
    return jnp.sum((first & second & live[:, None, None]).astype(F32), axis=0)


def pack_band(orbitals):
    return pl.pallas_call(
        pack_kernel,
        out_shape=jax.ShapeDtypeStruct((1, PACK, LANES), BF16),
        in_specs=[VMEM_SPEC],
        out_specs=VMEM_SPEC,
        scratch_shapes=[pltpu.VMEM((FLAT_ROWS, LANES), F32), pltpu.VMEM((PACK, LANES), F32)],
        compiler_params=PARAMS,
        name="pack_band",
    )(orbitals)


def list_counts(pair_list, pair_count):
    return pl.pallas_call(
        list_kernel,
        out_shape=jax.ShapeDtypeStruct((16, LANES), F32),
        in_specs=[VMEM_SPEC] * 2,
        out_specs=VMEM_SPEC,
        compiler_params=PARAMS,
        name="list_counts",
    )(jnp.swapaxes(pair_list, 1, 2), pair_count.reshape(1, 1))


def add_counts(packed, col_total, counts, mate_counts):
    return pl.pallas_call(
        functools.partial(count_kernel, col_total),
        out_shape=jax.ShapeDtypeStruct(packed.shape, BF16),
        in_specs=[VMEM_SPEC] * 3,
        out_specs=VMEM_SPEC,
        compiler_params=PARAMS,
        name="add_counts",
    )(packed, counts, mate_counts)


def finish(own, part):
    return pl.pallas_call(
        finish_kernel,
        out_shape=jax.ShapeDtypeStruct((1, LIVE * GX), F32),
        in_specs=[VMEM_SPEC] * 2,
        out_specs=VMEM_SPEC,
        compiler_params=PARAMS,
        name="add_parts",
    )(own, part)


NEAR = (8, 4)
STAGES = (
    (((0, 0),), ((4, 0),), ((2, 0),), ((1, 0),), ((0, 2),), ((1, 2),)),
    (((4, 2), (2, 2)), ((5, 0), (3, 0)), ((6, 0), (3, 2))),
    (((5, 2),), ((6, 2), (7, 0)), ((7, 2),)),
)
CAPS = (2, 2)


def near_part(row_total, col_total, part, operands):
    places = 2 * row_total * (col_total // 2) + SIDE
    out_shape = pair_of(ROWS)
    if part == 0:
        out_shape = out_shape * 2
    if part == 2:
        out_shape = pair_of(FLAT)
    operands = list(operands)
    cost = pl.CostEstimate(flops=4 * 10**9, bytes_accessed=2 * 10**7, transcendentals=0)
    return pl.pallas_call(
        functools.partial(near_kernel, row_total, col_total, part),
        out_shape=out_shape,
        in_specs=[VMEM_SPEC] * len(operands),
        out_specs=[VMEM_SPEC] * len(out_shape),
        scratch_shapes=[
            pltpu.VMEM((8, LANES), jnp.int32),
            pltpu.SMEM((8, LANES), jnp.int32),
            pltpu.SMEM((places,), jnp.int32),
            pltpu.SMEM((places,), jnp.int32),
            pltpu.SMEM((places,), jnp.int32),
        ]
        + solve_scratch()
        + [pltpu.SemaphoreType.DMA]
        + [pltpu.VMEM((ROWS, LANES), F32)] * (2 if part == 2 else 0),
        compiler_params=PARAMS,
        cost_estimate=cost,
        name="solve_part",
    )(*operands)


def near_shards(row_total, col_total, orbitals, pair_list, pair_count):
    row_swap = lambda values, flip: swap(values, "row", row_total, flip)
    col_swap = lambda values, flip: swap(values, "col", col_total, flip)
    both = lambda a, b: jnp.concatenate([a, b], axis=0)

    def corner_swap(values):
        places = list(itertools.product(range(row_total), range(col_total)))
        at = lambda row, col: row * col_total + col
        pairs = [(at(row, col), at(row ^ 1, col ^ 2)) for row, col in places]
        return lax.ppermute(values, ("row", "col"), pairs)

    counts = list_counts(pair_list, pair_count)
    own = add_counts(pack_band(orbitals), col_total, counts, col_swap(counts, 1))
    mate, x, y, z = col_swap(own, 1), col_swap(own, 2), row_swap(own, 1), row_swap(own, 2)
    xy, w = corner_swap(own), row_swap(own, 4)
    mate, x, y, z, xy, w = lax.optimization_barrier((mate, x, y, z, xy, w))
    over_x, over_y, over_z = (
        col_swap(both(w, z), 2),
        row_swap(both(w, z), 1),
        row_swap(both(w, xy), 2),
    )
    tables = [jnp.asarray(table) for table in solve_tables()]
    blocks = [own, w, z, y, x, xy]
    *waves, sum0, sum1 = near_part(row_total, col_total, 0, [*blocks, mate, *tables])
    held = lax.optimization_barrier((sum0, sum1, over_x, over_y, over_z))
    sum0, sum1, over_x, over_y, over_z = held
    last = (
        row_swap(over_x[:1], 1),
        row_swap(both(over_x[:1], over_y[:1]), 2),
        corner_swap(over_z[:1]),
    )
    for part, arrived in enumerate(((over_x, over_y, over_z), last), 1):
        blocks += arrived
        operands = [*blocks, mate, *tables, *waves, sum0, sum1]
        sum0, sum1 = near_part(row_total, col_total, part, operands)
    return finish(sum0, col_swap(sum1, 1))


def far_shards(row_total, col_total, orbitals, pair_list, pair_count):
    counts = count_pairs(pair_list, pair_count, row_total, col_total)
    own = pack_band(orbitals)
    axes = ("row", "col")
    table = lax.all_gather(counts.reshape(-1), axes)
    table = table.reshape(row_total, col_total, col_total, row_total)
    wide = col_total // 2
    column = lax.all_gather(own[0], "row")
    columns = [column] + [swap(column, "col", col_total, 2 * x) for x in range(1, wide)]
    bands = jnp.concatenate(columns, axis=0)
    row = lax.axis_index("row")
    col = lax.axis_index("col")
    mine = jnp.stack([col, col ^ 1])
    other_col = ((col // 2) ^ lax.iota(jnp.int32, wide)) * 2 + col % 2
    other_row = lax.iota(jnp.int32, row_total)
    direct = table[row][other_col][:, mine]
    direct = jnp.transpose(direct, (1, 2, 0))
    mirror = table[:, :, :, row][:, mine][:, :, other_col]
    mirror = jnp.transpose(mirror, (1, 0, 2))
    same = (mine[:, None, None] == other_col[None, None, :]) & (other_row == row)[None, :, None]
    weights = (direct + jnp.where(same, 0.0, mirror)).astype(jnp.int32).reshape(-1)
    index = lax.iota(jnp.int32, weights.shape[0])
    order = jnp.argsort(jnp.where(weights > 0, 0, 1), stable=True)
    pad = lambda values: jnp.pad(values.astype(jnp.int32), (0, SIDE))
    slots = row_total * wide
    slot = order % slots
    band = (slot % wide) * row_total + slot // wide
    total = jnp.sum((weights > 0).astype(jnp.int32)).reshape(1)
    fields = pl.pallas_call(
        far_kernel,
        out_shape=pair_of(FLAT),
        in_specs=[SMEM_SPEC] * 4 + [ANY_SPEC] + [VMEM_SPEC] * 9,
        out_specs=[VMEM_SPEC] * 2,
        scratch_shapes=[pltpu.VMEM((PACK, LANES), BF16)]
        + [pltpu.VMEM((ROWS, LANES), F32)] * 4
        + solve_scratch(),
        compiler_params=PARAMS,
        name="solve_pairs",
    )(
        total,
        pad(band),
        pad(order // slots),
        pad(weights[order]),
        bands,
        own,
        swap(own, "col", col_total, 1),
        *map(jnp.asarray, solve_tables()),
    )
    return finish(fields[0], swap(fields[1], "col", col_total, 1))


def solution(mesh):
    row_total, col_total = mesh.shape["row"], mesh.shape["col"]
    near = (row_total, col_total) == NEAR
    shards = near_shards if near else far_shards
    return jax.shard_map(
        functools.partial(shards, row_total, col_total),
        mesh=mesh,
        in_specs=(P(("row", "col"), None), P(("row", "col"), None, None), P(("row", "col"))),
        out_specs=P(("row", "col"), None),
        check_vma=False,
    )
```

```python
import functools
import itertools

import jax
import jax.numpy as jnp
import ml_dtypes
import numpy as np
from jax import lax
from jax.experimental import pallas as pl
from jax.experimental.pallas import tpu as pltpu
from jax.sharding import PartitionSpec as P

GX = 40
LANES = 128
SIDE = 3
THIRD = -(-GX // SIDE)
PACK = THIRD * GX
ROWS = SIDE * PACK
LIVE = GX * GX
SPARE = SIDE * GX
FLAT = LIVE * GX // LANES
CHUNK = PACK // 16
FLAT_ROWS = SIDE * CHUNK * 5 + 8
DUO = 2 * GX
QUAD = 4 * GX
VMEM_LIMIT = 20 * 1024 * 1024
screen_width = 0.9
F32 = jnp.float32
BF16 = jnp.bfloat16


def real_basis():
    half = GX // 2
    point = np.arange(GX)
    rows = [np.cos(2 * np.pi * (k * point % GX) / GX) for k in range(half + 1)]
    rows += [np.sin(2 * np.pi * (k * point % GX) / GX) for k in range(1, half)]
    frequency = np.concatenate([np.arange(half + 1), np.arange(1, half)])
    norm = np.where((frequency == 0) | (frequency == half), 1.0, 2.0) / GX
    return np.stack(rows), frequency, norm


def halves(table):
    high = table.astype(ml_dtypes.bfloat16)
    low = (table - high.astype(np.float64)).astype(ml_dtypes.bfloat16)
    return high, low


def left_table(table):
    high, low = halves(np.kron(np.eye(2), table))
    return np.concatenate([high, low, high], axis=1)


def right_table(table):
    wide = np.zeros((LANES, LANES))
    for p in range(SIDE):
        wide[p * GX : (p + 1) * GX, p * GX : (p + 1) * GX] = table
    high, low = halves(wide)
    both = np.concatenate([high, low], axis=1)
    return np.concatenate([both, both], axis=0)


def kernel_table():
    _, frequency, norm = real_basis()
    wave = frequency * (2.0 * np.pi / GX)
    squared = wave * wave
    total = squared[:, None, None] + squared[None, :, None] + squared[None, None, :]
    safe = np.where(total > 0, total, 1.0)
    screened = 4.0 * np.pi * (1.0 - np.exp(-safe / (4.0 * screen_width**2))) / safe
    kernel = np.where(total > 0, screened, np.pi / screen_width**2)
    kernel = kernel * norm[:, None, None] * norm[None, :, None] * norm[None, None, :]
    rows = np.swapaxes(kernel, 0, 1).reshape(LIVE, GX)
    out = np.zeros((LIVE, LANES), np.float32)
    for p in range(SIDE):
        out[:, p * GX : (p + 1) * GX] = rows
    return out


def place(out, row, col):
    for z in range(GX):
        out[row + z, col + z] = 1.0


def spread_table():
    out = np.zeros((SIDE * LANES, SIDE * LANES), np.float32)
    for third in range(SIDE):
        for p in range(SIDE):
            place(out, p * LANES + third * GX, third * LANES + p * GX)
    return out.astype(ml_dtypes.bfloat16)


def repeat_table():
    out = np.zeros((LANES, SIDE * LANES), np.float32)
    for third in range(SIDE):
        for p in range(SIDE):
            place(out, third * GX, third * LANES + p * GX)
    return out.astype(ml_dtypes.bfloat16)


def dot(a, b):
    return jnp.dot(a, b, preferred_element_type=F32)


def split(values):
    high = values.astype(BF16)
    return high, (values - high.astype(F32)).astype(BF16)


def contract_rows(table, values):
    high, low = split(values)
    return dot(table, jnp.concatenate([high, high, low], axis=0))


def contract_lanes(values, table):
    both = dot(jnp.concatenate(split(values), axis=1), table)
    return both[:, :LANES] + both[:, LANES:]


def fold(values):
    return jnp.concatenate([values[:DUO], values[DUO:]], axis=1)


def unfold(values):
    return jnp.concatenate([values[:, :LANES], values[:, LANES:]], axis=0)


def quad(step):
    return pl.ds(step * QUAD, QUAD)


def load_planes(ref, step):
    planes = [ref[pl.ds(step * 4 + i, GX, stride=GX), :] for i in range(4)]
    left = jnp.concatenate(planes[:2], axis=0)
    return jnp.concatenate([left, jnp.concatenate(planes[2:], axis=0)], axis=1)


def store_planes(ref, step, values):
    for i in range(4):
        rows, lanes = i % 2 * GX, i // 2 * LANES
        ref[pl.ds(step * 4 + i, GX, stride=GX), :] = values[rows : rows + GX, lanes : lanes + LANES]


def count_vector(pairs, live):
    slots = pairs.shape[1]
    row = lax.broadcasted_iota(jnp.int32, (16, slots), 0)
    lane = lax.broadcasted_iota(jnp.int32, (LANES, slots), 0) - SPARE
    first = (pairs[0:1] == row) & (lax.broadcasted_iota(jnp.int32, (16, slots), 1) < live)
    second = jnp.where(pairs[1:2] == lane, 1.0, 0.0)
    contract = (((1,), (1,)), ((), ()))
    return lax.dot_general(jnp.where(first, 1.0, 0.0), second, contract, preferred_element_type=F32)


def unroll_rows(copy):
    for k in range(FLAT):
        copy(k, slice(k * LANES, (k + 1) * LANES))


def pack_kernel(band_ref, out_ref, flat_ref, wide_ref):
    def to_rows(k, lanes):
        flat_ref[k : k + 1, :] = band_ref[0:1, lanes].astype(F32)

    unroll_rows(to_rows)
    unused = FLAT_ROWS - FLAT
    flat_ref[FLAT:FLAT_ROWS, :] = jnp.zeros((unused, LANES), F32)
    lane = lax.broadcasted_iota(jnp.int32, (1, LANES), 1)
    for q in range(16):
        row, offset = divmod(q * GX, LANES)
        packed = jnp.zeros((CHUNK, LANES), F32)
        for third in range(SIDE):
            start = third * CHUNK * 5 + row
            values = flat_ref[pl.ds(start, CHUNK, stride=5), :]
            if offset + GX > LANES:
                after = flat_ref[pl.ds(start + 1, CHUNK, stride=5), :]
                values = jnp.where(lane >= offset, values, after)
            shift = (third * GX - offset) % LANES
            values = pltpu.roll(values, shift, 1) if shift else values
            packed = jnp.where(lane // GX == third, values, packed)
        wide_ref[pl.ds(q, CHUNK, stride=16), :] = packed
    out_ref[0] = wide_ref[...].astype(BF16)


def list_kernel(pairs_ref, live_ref, out_ref):
    out_ref[...] = count_vector(pairs_ref[0], live_ref[...])


def count_kernel(col_total, packed_ref, own_ref, mate_ref, out_ref):
    out_ref[...] = packed_ref[...]
    counts = own_ref[...] + pltpu.roll(mate_ref[...], col_total, 0)
    out_ref[0, 0:16, :] = (packed_ref[0, 0:16, :].astype(F32) + counts).astype(BF16)


def spread_waves(own_bands, repeat_ref, wave_refs):
    for band, wave_ref in zip(own_bands, wave_refs):
        wide = dot(band, repeat_ref[...])
        for third in range(SIDE):
            wave_ref[pl.ds(third * PACK, PACK), :] = wide[:, third * LANES : (third + 1) * LANES]


def clear(sum_refs):
    for sum_ref in sum_refs:
        sum_ref[...] = jnp.zeros_like(sum_ref)


def lane_side():
    return lax.broadcasted_iota(jnp.int32, (1, LANES), 1) // GX


def solve_trios(first, count, lists, load_band, tables, wave_refs, sum_refs, scratch):
    spread_ref, _, z_ref, z_back_ref, row_ref, row_back_ref, kernel_ref = tables
    trio_ref, partner_ref, work_ref, work2_ref = scratch
    slot_list, band_list, weight_list = lists
    side = lane_side()

    def by_side(values):
        row = jnp.zeros((1, LANES), F32)
        for p in range(SIDE):
            row = jnp.where(side == p, values[p].astype(F32), row)
        return row

    def trio(at, carry):
        places = [first + at * SIDE + p for p in range(SIDE)]
        for p, place in enumerate(places):
            load_band(slot_list[place], trio_ref, p)
        bands = [band_list[place] for place in places]
        weights = [weight_list[place] for place in places]
        is_mate = by_side(bands) > 0.5
        scales = [
            by_side([jnp.where(bands[p] == which, weights[p], 0) for p in range(SIDE)])
            for which in range(2)
        ]
        wide = dot(trio_ref[...], spread_ref[...])
        for third in range(SIDE):
            partner_ref[pl.ds(third * PACK, PACK), :] = wide[:, third * LANES : (third + 1) * LANES]

        def forward(steps):
            planes = pl.ds(steps[0] * QUAD, len(steps) * QUAD)
            wave = jnp.where(is_mate, wave_refs[1][planes, :], wave_refs[0][planes, :])
            values = contract_lanes(partner_ref[planes, :] * wave, z_ref[...])
            values = [values[i * QUAD : (i + 1) * QUAD] for i in range(len(steps))]
            values = [contract_rows(row_ref[...], fold(v)) for v in values]
            for step, v in zip(steps, values):
                work_ref[quad(step), :] = unfold(v)

        def across(steps):
            values = [load_planes(work_ref, step) for step in steps]
            values = [contract_rows(row_ref[...], v) for v in values]
            values = [v * fold(kernel_ref[quad(step), :]) for step, v in zip(steps, values)]
            values = [contract_rows(row_back_ref[...], v) for v in values]
            for step, v in zip(steps, values):
                store_planes(work2_ref, step, v)

        def back(steps):
            planes = pl.ds(steps[0] * QUAD, len(steps) * QUAD)
            values = [fold(work2_ref[quad(step), :]) for step in steps]
            values = [unfold(contract_rows(row_back_ref[...], v)) for v in values]
            values = contract_lanes(jnp.concatenate(values, axis=0), z_back_ref[...])
            values = values * partner_ref[planes, :]
            for sum_ref, scale in zip(sum_refs, scales):
                sum_ref[planes, :] = sum_ref[planes, :] + values * scale

        for phase in (forward, across, back):
            phase(range(GX // 4))
        return carry

    lax.fori_loop(0, count, trio, 0)


def flat_fields(sum_refs, out_refs):
    lane = lax.broadcasted_iota(jnp.int32, (1, LANES), 1)
    rows = LIVE // 16
    for sum_ref, out_ref in zip(sum_refs, out_refs):
        flat = [jnp.zeros((rows, LANES), F32)] * 5
        for q in range(16):
            row, offset = divmod(q * GX, LANES)
            values = sum_ref[pl.ds(q, rows, stride=16), :]
            moved = jnp.zeros((rows, LANES), F32)
            for p in range(SIDE):
                shift = (offset - p * GX) % LANES
                moved = moved + (pltpu.roll(values, shift, 1) if shift else values)
            flat[row] = jnp.where(lane >= offset, moved, flat[row])
            if offset + GX > LANES:
                flat[row + 1] = jnp.where(lane < offset + GX - LANES, moved, flat[row + 1])
        for row in range(5):
            out_ref[pl.ds(row, rows, stride=5), :] = flat[row]


def near_kernel(row_total, col_total, part, *refs):
    stages = STAGES[: part + 1]
    blocks = [block for stage in stages for block in stage]
    band_refs, refs = refs[: len(blocks)], refs[len(blocks) :]
    bands = [(ref, at) for ref, block in zip(band_refs, blocks) for at in range(len(block))]
    flips = [flip for block in blocks for flip in block]
    mate_ref, tables, refs = refs[0], refs[1:8], refs[8:]
    if part:
        wave_refs, given_refs, out_refs, refs = refs[:2], refs[2:4], refs[4:6], refs[6:]
    else:
        wave_refs, out_refs, refs = refs[:2], refs[2:4], refs[4:]
    (count_vmem, count_smem, slot_list, band_list, weight_list), refs = refs[:5], refs[5:]
    scratch, sem = refs[:4], refs[4]
    sum_refs = refs[5:] if part == 2 else out_refs

    lane = lax.broadcasted_iota(jnp.int32, (8, LANES), 1)
    counts = jnp.zeros((8, LANES), F32)
    for s, (ref, at) in enumerate(bands):
        spare = ref[at, 0:16, :].astype(F32)[0:8]
        shift = (s * row_total - SPARE) % LANES
        moved = pltpu.roll(spare, shift, 1) if shift else spare
        counts = jnp.where(lane // row_total == s, moved, counts)
    count_vmem[...] = counts.astype(jnp.int32)
    copy = pltpu.make_async_copy(count_vmem, count_smem, sem)
    copy.start()
    if part:
        for sum_ref, given_ref in zip(sum_refs, given_refs):
            sum_ref[...] = given_ref[...]
    else:
        clear(sum_refs)
        spread_waves((band_refs[0][0], mate_ref[0]), tables[1], wave_refs)
    copy.wait()
    row = lax.axis_index("row")
    col = lax.axis_index("col")
    total = jnp.int32(0)
    done = jnp.int32(0)
    place = 0
    for step, stage in enumerate(stages):
        here = range(place, place + sum(len(block) for block in stage))
        place = here.stop
        for which, at in itertools.product(range(2), here):
            row_flip, col_flip = flips[at]
            row_place = flips.index((0, col_flip)) * row_total
            col_place = flips.index((row_flip, 0)) * row_total
            weight = count_smem[col ^ which, row_place + (row ^ row_flip)]
            if at or which:
                mirror = which * col_total + (col ^ col_flip)
                weight = weight + count_smem[mirror, col_place + row]
            slot_list[total] = at
            band_list[total] = which
            weight_list[total] = weight
            total = total + jnp.where(weight > 0, 1, 0)
        if step < 2:
            trios = jnp.minimum((total - done) // SIDE, CAPS[step])
            if step < part:
                done = done + trios * SIDE
    if part == 2:
        trios = (total - done + SIDE - 1) // SIDE
        for p in range(SIDE - 1):
            slot_list[total + p] = 0
            band_list[total + p] = 0
            weight_list[total + p] = 0

    def load_band(wanted, target, p):
        for place, (ref, at) in enumerate(bands):

            @pl.when(wanted == place)
            def _():
                target[:, p * LANES : (p + 1) * LANES] = ref[at]

    lists = (slot_list, band_list, weight_list)
    solve_trios(done, trios, lists, load_band, tables, wave_refs, sum_refs, scratch)
    if part == 2:
        flat_fields(sum_refs, out_refs)


def far_kernel(total_ref, slot_list, band_list, weight_list, bands_ref, own_ref, mate_ref, *refs):
    tables, out_refs, refs = refs[:7], refs[7:9], refs[9:]
    buffer, wave_refs, sum_refs, scratch = refs[0], refs[1:3], refs[3:5], refs[5:]
    spread_waves((own_ref[0], mate_ref[0]), tables[1], wave_refs)
    clear(sum_refs)

    def load_band(place, target, p):
        pltpu.sync_copy(bands_ref.at[place], buffer)
        target[:, p * LANES : (p + 1) * LANES] = buffer[...]

    lists = (slot_list, band_list, weight_list)
    trios = (total_ref[0] + SIDE - 1) // SIDE
    solve_trios(0, trios, lists, load_band, tables, wave_refs, sum_refs, scratch)
    flat_fields(sum_refs, out_refs)


def finish_kernel(own_ref, part_ref, out_ref):
    def to_lanes(k, lanes):
        out_ref[0:1, lanes] = own_ref[k : k + 1, :] + part_ref[k : k + 1, :]

    unroll_rows(to_lanes)


VMEM_SPEC = pl.BlockSpec(memory_space=pltpu.VMEM)
SMEM_SPEC = pl.BlockSpec(memory_space=pltpu.SMEM)
ANY_SPEC = pl.BlockSpec(memory_space=pl.ANY)
PARAMS = pltpu.CompilerParams(vmem_limit_bytes=VMEM_LIMIT)


def solve_tables():
    basis, _, _ = real_basis()
    return [
        spread_table(),
        repeat_table(),
        right_table(basis.T),
        right_table(basis),
        left_table(basis),
        left_table(basis.T),
        kernel_table(),
    ]


def solve_scratch():
    return [pltpu.VMEM((PACK, SIDE * LANES), BF16)] + [pltpu.VMEM((ROWS, LANES), F32)] * 3


def pair_of(rows):
    return [jax.ShapeDtypeStruct((rows, LANES), F32)] * 2


def swap(values, axis, size, flip):
    return lax.ppermute(values, axis, [(i, i ^ flip) for i in range(size)])


def count_pairs(pair_list, pair_count, row_total, col_total):
    slots = pair_list.shape[1]
    live = lax.iota(jnp.int32, slots) < pair_count[0]
    first = pair_list[0, :, 0][:, None, None] == lax.iota(jnp.int32, col_total)[None, :, None]
    second = pair_list[0, :, 1][:, None, None] == lax.iota(jnp.int32, row_total)[None, None, :]
    return jnp.sum((first & second & live[:, None, None]).astype(F32), axis=0)


def pack_band(orbitals):
    return pl.pallas_call(
        pack_kernel,
        out_shape=jax.ShapeDtypeStruct((1, PACK, LANES), BF16),
        in_specs=[VMEM_SPEC],
        out_specs=VMEM_SPEC,
        scratch_shapes=[pltpu.VMEM((FLAT_ROWS, LANES), F32), pltpu.VMEM((PACK, LANES), F32)],
        compiler_params=PARAMS,
        name="pack_band",
    )(orbitals)


def list_counts(pair_list, pair_count):
    return pl.pallas_call(
        list_kernel,
        out_shape=jax.ShapeDtypeStruct((16, LANES), F32),
        in_specs=[VMEM_SPEC] * 2,
        out_specs=VMEM_SPEC,
        compiler_params=PARAMS,
        name="list_counts",
    )(jnp.swapaxes(pair_list, 1, 2), pair_count.reshape(1, 1))


def add_counts(packed, col_total, counts, mate_counts):
    return pl.pallas_call(
        functools.partial(count_kernel, col_total),
        out_shape=jax.ShapeDtypeStruct(packed.shape, BF16),
        in_specs=[VMEM_SPEC] * 3,
        out_specs=VMEM_SPEC,
        compiler_params=PARAMS,
        name="add_counts",
    )(packed, counts, mate_counts)


def finish(own, part):
    return pl.pallas_call(
        finish_kernel,
        out_shape=jax.ShapeDtypeStruct((1, LIVE * GX), F32),
        in_specs=[VMEM_SPEC] * 2,
        out_specs=VMEM_SPEC,
        compiler_params=PARAMS,
        name="add_parts",
    )(own, part)


NEAR = (8, 4)
STAGES = (
    (((0, 0),), ((4, 0),), ((2, 0),), ((1, 0),), ((0, 2),), ((1, 2),)),
    (((4, 2), (2, 2)), ((5, 0), (3, 0)), ((6, 0), (3, 2))),
    (((5, 2),), ((6, 2), (7, 0)), ((7, 2),)),
)
CAPS = (2, 2)


def near_part(row_total, col_total, part, operands):
    places = 2 * row_total * (col_total // 2) + SIDE
    out_shape = pair_of(ROWS)
    if part == 0:
        out_shape = out_shape * 2
    if part == 2:
        out_shape = pair_of(FLAT)
    operands = list(operands)
    cost = pl.CostEstimate(flops=4 * 10**9, bytes_accessed=2 * 10**7, transcendentals=0)
    return pl.pallas_call(
        functools.partial(near_kernel, row_total, col_total, part),
        out_shape=out_shape,
        in_specs=[VMEM_SPEC] * len(operands),
        out_specs=[VMEM_SPEC] * len(out_shape),
        scratch_shapes=[
            pltpu.VMEM((8, LANES), jnp.int32),
            pltpu.SMEM((8, LANES), jnp.int32),
            pltpu.SMEM((places,), jnp.int32),
            pltpu.SMEM((places,), jnp.int32),
            pltpu.SMEM((places,), jnp.int32),
        ]
        + solve_scratch()
        + [pltpu.SemaphoreType.DMA]
        + [pltpu.VMEM((ROWS, LANES), F32)] * (2 if part == 2 else 0),
        compiler_params=PARAMS,
        cost_estimate=cost,
        name="solve_part",
    )(*operands)


def near_shards(row_total, col_total, orbitals, pair_list, pair_count):
    row_swap = lambda values, flip: swap(values, "row", row_total, flip)
    col_swap = lambda values, flip: swap(values, "col", col_total, flip)
    both = lambda a, b: jnp.concatenate([a, b], axis=0)

    def corner_swap(values):
        places = list(itertools.product(range(row_total), range(col_total)))
        at = lambda row, col: row * col_total + col
        pairs = [(at(row, col), at(row ^ 1, col ^ 2)) for row, col in places]
        return lax.ppermute(values, ("row", "col"), pairs)

    counts = list_counts(pair_list, pair_count)
    own = add_counts(pack_band(orbitals), col_total, counts, col_swap(counts, 1))
    in_order = lambda *values: lax.optimization_barrier(values)
    mate, x, y, xy, z, w = in_order(
        col_swap(own, 1),
        col_swap(own, 2),
        row_swap(own, 1),
        corner_swap(own),
        row_swap(own, 2),
        row_swap(own, 4),
    )
    w_z, w_xy = in_order(both(w, z), both(w, xy))
    over_x, over_y, over_z = col_swap(w_z, 2), row_swap(w_z, 1), row_swap(w_xy, 2)
    tables = [jnp.asarray(table) for table in solve_tables()]
    blocks = [own, w, z, y, x, xy]
    *waves, sum0, sum1 = near_part(row_total, col_total, 0, [*blocks, mate, *tables])
    sum0, sum1, over_x, over_y, over_z = in_order(sum0, sum1, over_x, over_y, over_z)
    wx, wz, wx_wy = in_order(over_x[:1], over_z[:1], both(over_x[:1], over_y[:1]))
    wxy, wzxy, over_z2 = in_order(row_swap(wx, 1), corner_swap(wz), row_swap(wx_wy, 2))
    last = (wxy, over_z2, wzxy)
    for part, arrived in enumerate(((over_x, over_y, over_z), last), 1):
        blocks += arrived
        operands = [*blocks, mate, *tables, *waves, sum0, sum1]
        sum0, sum1 = near_part(row_total, col_total, part, operands)
    return finish(sum0, col_swap(sum1, 1))


def far_shards(row_total, col_total, orbitals, pair_list, pair_count):
    counts = count_pairs(pair_list, pair_count, row_total, col_total)
    own = pack_band(orbitals)
    axes = ("row", "col")
    table = lax.all_gather(counts.reshape(-1), axes)
    table = table.reshape(row_total, col_total, col_total, row_total)
    wide = col_total // 2
    column = lax.all_gather(own[0], "row")
    columns = [column] + [swap(column, "col", col_total, 2 * x) for x in range(1, wide)]
    bands = jnp.concatenate(columns, axis=0)
    row = lax.axis_index("row")
    col = lax.axis_index("col")
    mine = jnp.stack([col, col ^ 1])
    other_col = ((col // 2) ^ lax.iota(jnp.int32, wide)) * 2 + col % 2
    other_row = lax.iota(jnp.int32, row_total)
    direct = table[row][other_col][:, mine]
    direct = jnp.transpose(direct, (1, 2, 0))
    mirror = table[:, :, :, row][:, mine][:, :, other_col]
    mirror = jnp.transpose(mirror, (1, 0, 2))
    same = (mine[:, None, None] == other_col[None, None, :]) & (other_row == row)[None, :, None]
    weights = (direct + jnp.where(same, 0.0, mirror)).astype(jnp.int32).reshape(-1)
    index = lax.iota(jnp.int32, weights.shape[0])
    order = jnp.argsort(jnp.where(weights > 0, 0, 1), stable=True)
    pad = lambda values: jnp.pad(values.astype(jnp.int32), (0, SIDE))
    slots = row_total * wide
    slot = order % slots
    band = (slot % wide) * row_total + slot // wide
    total = jnp.sum((weights > 0).astype(jnp.int32)).reshape(1)
    fields = pl.pallas_call(
        far_kernel,
        out_shape=pair_of(FLAT),
        in_specs=[SMEM_SPEC] * 4 + [ANY_SPEC] + [VMEM_SPEC] * 9,
        out_specs=[VMEM_SPEC] * 2,
        scratch_shapes=[pltpu.VMEM((PACK, LANES), BF16)]
        + [pltpu.VMEM((ROWS, LANES), F32)] * 4
        + solve_scratch(),
        compiler_params=PARAMS,
        name="solve_pairs",
    )(
        total,
        pad(band),
        pad(order // slots),
        pad(weights[order]),
        bands,
        own,
        swap(own, "col", col_total, 1),
        *map(jnp.asarray, solve_tables()),
    )
    return finish(fields[0], swap(fields[1], "col", col_total, 1))


def solution(mesh):
    row_total, col_total = mesh.shape["row"], mesh.shape["col"]
    near = (row_total, col_total) == NEAR
    shards = near_shards if near else far_shards
    return jax.shard_map(
        functools.partial(shards, row_total, col_total),
        mesh=mesh,
        in_specs=(P(("row", "col"), None), P(("row", "col"), None, None), P(("row", "col"))),
        out_specs=P(("row", "col"), None),
        check_vma=False,
    )
```

```python
import functools
import itertools

import jax
import jax.numpy as jnp
import ml_dtypes
import numpy as np
from jax import lax
from jax.experimental import pallas as pl
from jax.experimental.pallas import tpu as pltpu
from jax.sharding import PartitionSpec as P

GX = 40
LANES = 128
SIDE = 3
THIRD = -(-GX // SIDE)
PACK = THIRD * GX
ROWS = SIDE * PACK
LIVE = GX * GX
SPARE = SIDE * GX
FLAT = LIVE * GX // LANES
CHUNK = PACK // 16
FLAT_ROWS = SIDE * CHUNK * 5 + 8
DUO = 2 * GX
QUAD = 4 * GX
PITCH = GX + 1
VMEM_LIMIT = 16 * 1024 * 1024
screen_width = 0.9
F32 = jnp.float32
BF16 = jnp.bfloat16


def real_basis():
    half = GX // 2
    point = np.arange(GX)
    rows = [np.cos(2 * np.pi * (k * point % GX) / GX) for k in range(half + 1)]
    rows += [np.sin(2 * np.pi * (k * point % GX) / GX) for k in range(1, half)]
    frequency = np.concatenate([np.arange(half + 1), np.arange(1, half)])
    norm = np.where((frequency == 0) | (frequency == half), 1.0, 2.0) / GX
    return np.stack(rows), frequency, norm


def halves(table):
    high = table.astype(ml_dtypes.bfloat16)
    low = (table - high.astype(np.float64)).astype(ml_dtypes.bfloat16)
    return high, low


def left_table(table):
    high, low = halves(np.kron(np.eye(2), table))
    return np.concatenate([high, low, high], axis=1)


def right_table(table):
    wide = np.zeros((LANES, LANES))
    for p in range(SIDE):
        wide[p * GX : (p + 1) * GX, p * GX : (p + 1) * GX] = table
    high, low = halves(wide)
    both = np.concatenate([high, low], axis=1)
    return np.concatenate([both, both], axis=0)


def kernel_table():
    _, frequency, norm = real_basis()
    wave = frequency * (2.0 * np.pi / GX)
    squared = wave * wave
    total = squared[:, None, None] + squared[None, :, None] + squared[None, None, :]
    safe = np.where(total > 0, total, 1.0)
    screened = 4.0 * np.pi * (1.0 - np.exp(-safe / (4.0 * screen_width**2))) / safe
    kernel = np.where(total > 0, screened, np.pi / screen_width**2)
    kernel = kernel * norm[:, None, None] * norm[None, :, None] * norm[None, None, :]
    rows = np.swapaxes(kernel, 0, 1).reshape(LIVE, GX)
    out = np.zeros((LIVE, LANES), np.float32)
    for p in range(SIDE):
        out[:, p * GX : (p + 1) * GX] = rows
    return out


def place(out, row, col):
    for z in range(GX):
        out[row + z, col + z] = 1.0


def spread_table():
    out = np.zeros((SIDE * LANES, SIDE * LANES), np.float32)
    for third in range(SIDE):
        for p in range(SIDE):
            place(out, p * LANES + third * GX, third * LANES + p * GX)
    return out.astype(ml_dtypes.bfloat16)


def repeat_table():
    out = np.zeros((LANES, SIDE * LANES), np.float32)
    for third in range(SIDE):
        for p in range(SIDE):
            place(out, third * GX, third * LANES + p * GX)
    return out.astype(ml_dtypes.bfloat16)


def dot(a, b):
    return jnp.dot(a, b, preferred_element_type=F32)


def split(values):
    high = values.astype(BF16)
    return high, (values - high.astype(F32)).astype(BF16)


def contract_rows(table, values):
    high, low = split(values)
    return dot(table, jnp.concatenate([high, high, low], axis=0))


def contract_lanes(values, table):
    both = dot(jnp.concatenate(split(values), axis=1), table)
    return both[:, :LANES] + both[:, LANES:]


def fold(values):
    return jnp.concatenate([values[:DUO], values[DUO:]], axis=1)


def unfold(values):
    return jnp.concatenate([values[:, :LANES], values[:, LANES:]], axis=0)


def quad(step):
    return pl.ds(step * QUAD, QUAD)


def joined(planes):
    left = jnp.concatenate(planes[:2], axis=0)
    return jnp.concatenate([left, jnp.concatenate(planes[2:], axis=0)], axis=1)


def parted(values):
    return [
        values[i % 2 * GX : i % 2 * GX + GX, i // 2 * LANES : (i // 2 + 1) * LANES] for i in range(4)
    ]


def load_planes(ref, step):
    return joined([ref[pl.ds(step * 4 + i, GX, stride=PITCH), :] for i in range(4)])


def store_planes(ref, step, values):
    for i, plane in enumerate(parted(values)):
        ref[pl.ds(step * 4 + i, GX, stride=PITCH), :] = plane


def load_x_planes(ref, step):
    return joined([ref[pl.ds((step * 4 + i) * PITCH, GX), :] for i in range(4)])


def store_x_planes(ref, step, values):
    for i, plane in enumerate(parted(values)):
        ref[pl.ds((step * 4 + i) * PITCH, GX), :] = plane


def count_vector(pairs, live):
    slots = pairs.shape[1]
    row = lax.broadcasted_iota(jnp.int32, (16, slots), 0)
    lane = lax.broadcasted_iota(jnp.int32, (LANES, slots), 0) - SPARE
    first = (pairs[0:1] == row) & (lax.broadcasted_iota(jnp.int32, (16, slots), 1) < live)
    second = jnp.where(pairs[1:2] == lane, 1.0, 0.0)
    contract = (((1,), (1,)), ((), ()))
    return lax.dot_general(jnp.where(first, 1.0, 0.0), second, contract, preferred_element_type=F32)


def unroll_rows(copy):
    for k in range(FLAT):
        copy(k, slice(k * LANES, (k + 1) * LANES))


def pack_kernel(band_ref, out_ref, flat_ref, wide_ref):
    def to_rows(k, lanes):
        flat_ref[k : k + 1, :] = band_ref[0:1, lanes].astype(F32)

    unroll_rows(to_rows)
    unused = FLAT_ROWS - FLAT
    flat_ref[FLAT:FLAT_ROWS, :] = jnp.zeros((unused, LANES), F32)
    lane = lax.broadcasted_iota(jnp.int32, (1, LANES), 1)
    for q in range(16):
        row, offset = divmod(q * GX, LANES)
        packed = jnp.zeros((CHUNK, LANES), F32)
        for third in range(SIDE):
            start = third * CHUNK * 5 + row
            values = flat_ref[pl.ds(start, CHUNK, stride=5), :]
            if offset + GX > LANES:
                after = flat_ref[pl.ds(start + 1, CHUNK, stride=5), :]
                values = jnp.where(lane >= offset, values, after)
            shift = (third * GX - offset) % LANES
            values = pltpu.roll(values, shift, 1) if shift else values
            packed = jnp.where(lane // GX == third, values, packed)
        wide_ref[pl.ds(q, CHUNK, stride=16), :] = packed
    out_ref[0] = wide_ref[...].astype(BF16)


def list_kernel(pairs_ref, live_ref, out_ref):
    out_ref[...] = count_vector(pairs_ref[0], live_ref[...])


def count_kernel(col_total, packed_ref, own_ref, mate_ref, out_ref):
    out_ref[...] = packed_ref[...]
    counts = own_ref[...] + pltpu.roll(mate_ref[...], col_total, 0)
    out_ref[0, 0:16, :] = (packed_ref[0, 0:16, :].astype(F32) + counts).astype(BF16)


def spread_waves(own_bands, repeat_ref, wave_refs):
    for band, wave_ref in zip(own_bands, wave_refs):
        wide = dot(band, repeat_ref[...])
        for third in range(SIDE):
            wave_ref[pl.ds(third * PACK, PACK), :] = wide[:, third * LANES : (third + 1) * LANES]


def clear(sum_refs):
    for sum_ref in sum_refs:
        sum_ref[...] = jnp.zeros_like(sum_ref)


def lane_side():
    return lax.broadcasted_iota(jnp.int32, (1, LANES), 1) // GX


def solve_trios(first, count, lists, load_band, tables, wave_refs, sum_refs, scratch):
    spread_ref, _, z_ref, z_back_ref, row_ref, row_back_ref, kernel_ref = tables
    trio_ref, partner_ref, work_ref, work2_ref = scratch
    slot_list, band_list, weight_list = lists
    side = lane_side()

    def by_side(values):
        row = jnp.zeros((1, LANES), F32)
        for p in range(SIDE):
            row = jnp.where(side == p, values[p].astype(F32), row)
        return row

    def trio(at, carry):
        places = [first + at * SIDE + p for p in range(SIDE)]
        for p, place in enumerate(places):
            load_band(slot_list[place], trio_ref, p)
        bands = [band_list[place] for place in places]
        weights = [weight_list[place] for place in places]
        is_mate = by_side(bands) > 0.5
        scales = [
            by_side([jnp.where(bands[p] == which, weights[p], 0) for p in range(SIDE)])
            for which in range(2)
        ]
        wide = dot(trio_ref[...], spread_ref[...])
        for third in range(SIDE):
            partner_ref[pl.ds(third * PACK, PACK), :] = wide[:, third * LANES : (third + 1) * LANES]

        steps = range(GX // 4)

        def forward():
            values = []
            for step in steps:
                wave = jnp.where(is_mate, wave_refs[1][quad(step), :], wave_refs[0][quad(step), :])
                values.append(partner_ref[quad(step), :] * wave)
            values = [contract_lanes(v, z_ref[...]) for v in values]
            values = [contract_rows(row_ref[...], fold(v)) for v in values]
            for step, v in zip(steps, values):
                store_x_planes(work_ref, step, v)

        def across():
            values = [load_planes(work_ref, step) for step in steps]
            values = [contract_rows(row_ref[...], v) for v in values]
            values = [v * fold(kernel_ref[quad(step), :]) for step, v in zip(steps, values)]
            values = [contract_rows(row_back_ref[...], v) for v in values]
            for step, v in zip(steps, values):
                store_planes(work2_ref, step, v)

        def back():
            values = [load_x_planes(work2_ref, step) for step in steps]
            values = [unfold(contract_rows(row_back_ref[...], v)) for v in values]
            values = [contract_lanes(v, z_back_ref[...]) for v in values]
            for step, v in zip(steps, values):
                v = v * partner_ref[quad(step), :]
                for sum_ref, scale in zip(sum_refs, scales):
                    sum_ref[quad(step), :] = sum_ref[quad(step), :] + v * scale

        for phase in (forward, across, back):
            phase()
        return carry

    lax.fori_loop(0, count, trio, 0)


def flat_fields(sum_refs, out_refs):
    lane = lax.broadcasted_iota(jnp.int32, (1, LANES), 1)
    rows = LIVE // 16
    for sum_ref, out_ref in zip(sum_refs, out_refs):
        flat = [jnp.zeros((rows, LANES), F32)] * 5
        for q in range(16):
            row, offset = divmod(q * GX, LANES)
            values = sum_ref[pl.ds(q, rows, stride=16), :]
            moved = jnp.zeros((rows, LANES), F32)
            for p in range(SIDE):
                shift = (offset - p * GX) % LANES
                moved = moved + (pltpu.roll(values, shift, 1) if shift else values)
            flat[row] = jnp.where(lane >= offset, moved, flat[row])
            if offset + GX > LANES:
                flat[row + 1] = jnp.where(lane < offset + GX - LANES, moved, flat[row + 1])
        for row in range(5):
            out_ref[pl.ds(row, rows, stride=5), :] = flat[row]


def near_kernel(row_total, col_total, part, *refs):
    stages = STAGES[: part + 1]
    blocks = [block for stage in stages for block in stage]
    band_refs, refs = refs[: len(blocks)], refs[len(blocks) :]
    bands = [(ref, at) for ref, block in zip(band_refs, blocks) for at in range(len(block))]
    flips = [flip for block in blocks for flip in block]
    mate_ref, tables, refs = refs[0], refs[1:8], refs[8:]
    if part:
        wave_refs, given_refs, out_refs, refs = refs[:2], refs[2:4], refs[4:6], refs[6:]
    else:
        wave_refs, out_refs, refs = refs[:2], refs[2:4], refs[4:]
    (count_vmem, count_smem, slot_list, band_list, weight_list), refs = refs[:5], refs[5:]
    scratch, sem = refs[:4], refs[4]
    sum_refs = refs[5:] if part == 2 else out_refs

    lane = lax.broadcasted_iota(jnp.int32, (8, LANES), 1)
    counts = jnp.zeros((8, LANES), F32)
    for s, (ref, at) in enumerate(bands):
        spare = ref[at, 0:16, :].astype(F32)[0:8]
        shift = (s * row_total - SPARE) % LANES
        moved = pltpu.roll(spare, shift, 1) if shift else spare
        counts = jnp.where(lane // row_total == s, moved, counts)
    count_vmem[...] = counts.astype(jnp.int32)
    copy = pltpu.make_async_copy(count_vmem, count_smem, sem)
    copy.start()
    if part:
        for sum_ref, given_ref in zip(sum_refs, given_refs):
            sum_ref[...] = given_ref[...]
    else:
        clear(sum_refs)
        spread_waves((band_refs[0][0], mate_ref[0]), tables[1], wave_refs)
    copy.wait()
    row = lax.axis_index("row")
    col = lax.axis_index("col")
    total = jnp.int32(0)
    done = jnp.int32(0)
    place = 0
    for step, stage in enumerate(stages):
        here = range(place, place + sum(len(block) for block in stage))
        place = here.stop
        for which, at in itertools.product(range(2), here):
            row_flip, col_flip = flips[at]
            row_place = flips.index((0, col_flip)) * row_total
            col_place = flips.index((row_flip, 0)) * row_total
            weight = count_smem[col ^ which, row_place + (row ^ row_flip)]
            if at or which:
                mirror = which * col_total + (col ^ col_flip)
                weight = weight + count_smem[mirror, col_place + row]
            slot_list[total] = at
            band_list[total] = which
            weight_list[total] = weight
            total = total + jnp.where(weight > 0, 1, 0)
        if step < 2:
            trios = jnp.minimum((total - done) // SIDE, CAPS[step])
            if step < part:
                done = done + trios * SIDE
    if part == 2:
        trios = (total - done + SIDE - 1) // SIDE
        for p in range(SIDE - 1):
            slot_list[total + p] = 0
            band_list[total + p] = 0
            weight_list[total + p] = 0

    def load_band(wanted, target, p):
        for place, (ref, at) in enumerate(bands):

            @pl.when(wanted == place)
            def _():
                target[:, p * LANES : (p + 1) * LANES] = ref[at]

    lists = (slot_list, band_list, weight_list)
    solve_trios(done, trios, lists, load_band, tables, wave_refs, sum_refs, scratch)
    if part == 2:
        flat_fields(sum_refs, out_refs)


def far_kernel(total_ref, slot_list, band_list, weight_list, bands_ref, own_ref, mate_ref, *refs):
    tables, out_refs, refs = refs[:7], refs[7:9], refs[9:]
    buffer, wave_refs, sum_refs, scratch = refs[0], refs[1:3], refs[3:5], refs[5:]
    spread_waves((own_ref[0], mate_ref[0]), tables[1], wave_refs)
    clear(sum_refs)

    def load_band(place, target, p):
        pltpu.sync_copy(bands_ref.at[place], buffer)
        target[:, p * LANES : (p + 1) * LANES] = buffer[...]

    lists = (slot_list, band_list, weight_list)
    trios = (total_ref[0] + SIDE - 1) // SIDE
    solve_trios(0, trios, lists, load_band, tables, wave_refs, sum_refs, scratch)
    flat_fields(sum_refs, out_refs)


def finish_kernel(own_ref, part_ref, out_ref):
    def to_lanes(k, lanes):
        out_ref[0:1, lanes] = own_ref[k : k + 1, :] + part_ref[k : k + 1, :]

    unroll_rows(to_lanes)


VMEM_SPEC = pl.BlockSpec(memory_space=pltpu.VMEM)
SMEM_SPEC = pl.BlockSpec(memory_space=pltpu.SMEM)
ANY_SPEC = pl.BlockSpec(memory_space=pl.ANY)
PARAMS = pltpu.CompilerParams(vmem_limit_bytes=VMEM_LIMIT)


def solve_tables():
    basis, _, _ = real_basis()
    return [
        spread_table(),
        repeat_table(),
        right_table(basis.T),
        right_table(basis),
        left_table(basis),
        left_table(basis.T),
        kernel_table(),
    ]


def solve_scratch():
    return [pltpu.VMEM((PACK, SIDE * LANES), BF16)] + [pltpu.VMEM((ROWS, LANES), F32)] * 3


def pair_of(rows):
    return [jax.ShapeDtypeStruct((rows, LANES), F32)] * 2


def swap(values, axis, size, flip):
    return lax.ppermute(values, axis, [(i, i ^ flip) for i in range(size)])


def count_pairs(pair_list, pair_count, row_total, col_total):
    slots = pair_list.shape[1]
    live = lax.iota(jnp.int32, slots) < pair_count[0]
    first = pair_list[0, :, 0][:, None, None] == lax.iota(jnp.int32, col_total)[None, :, None]
    second = pair_list[0, :, 1][:, None, None] == lax.iota(jnp.int32, row_total)[None, None, :]
    return jnp.sum((first & second & live[:, None, None]).astype(F32), axis=0)


def pack_band(orbitals):
    return pl.pallas_call(
        pack_kernel,
        out_shape=jax.ShapeDtypeStruct((1, PACK, LANES), BF16),
        in_specs=[VMEM_SPEC],
        out_specs=VMEM_SPEC,
        scratch_shapes=[pltpu.VMEM((FLAT_ROWS, LANES), F32), pltpu.VMEM((PACK, LANES), F32)],
        compiler_params=PARAMS,
        name="pack_band",
    )(orbitals)


def list_counts(pair_list, pair_count):
    return pl.pallas_call(
        list_kernel,
        out_shape=jax.ShapeDtypeStruct((16, LANES), F32),
        in_specs=[VMEM_SPEC] * 2,
        out_specs=VMEM_SPEC,
        compiler_params=PARAMS,
        name="list_counts",
    )(jnp.swapaxes(pair_list, 1, 2), pair_count.reshape(1, 1))


def add_counts(packed, col_total, counts, mate_counts):
    return pl.pallas_call(
        functools.partial(count_kernel, col_total),
        out_shape=jax.ShapeDtypeStruct(packed.shape, BF16),
        in_specs=[VMEM_SPEC] * 3,
        out_specs=VMEM_SPEC,
        compiler_params=PARAMS,
        name="add_counts",
    )(packed, counts, mate_counts)


def finish(own, part):
    return pl.pallas_call(
        finish_kernel,
        out_shape=jax.ShapeDtypeStruct((1, LIVE * GX), F32),
        in_specs=[VMEM_SPEC] * 2,
        out_specs=VMEM_SPEC,
        compiler_params=PARAMS,
        name="add_parts",
    )(own, part)


NEAR = (8, 4)
STAGES = (
    (((0, 0),), ((4, 0),), ((2, 0),), ((1, 0),), ((0, 2),), ((1, 2),)),
    (((4, 2), (2, 2)), ((5, 0), (3, 0)), ((6, 0), (3, 2))),
    (((5, 2),), ((6, 2), (7, 0)), ((7, 2),)),
)
CAPS = (2, 2)


def near_part(row_total, col_total, part, operands):
    places = 2 * row_total * (col_total // 2) + SIDE
    out_shape = pair_of(ROWS)
    if part == 0:
        out_shape = out_shape * 2
    if part == 2:
        out_shape = pair_of(FLAT)
    operands = list(operands)
    cost = pl.CostEstimate(flops=4 * 10**9, bytes_accessed=2 * 10**7, transcendentals=0)
    return pl.pallas_call(
        functools.partial(near_kernel, row_total, col_total, part),
        out_shape=out_shape,
        in_specs=[VMEM_SPEC] * len(operands),
        out_specs=[VMEM_SPEC] * len(out_shape),
        scratch_shapes=[
            pltpu.VMEM((8, LANES), jnp.int32),
            pltpu.SMEM((8, LANES), jnp.int32),
            pltpu.SMEM((places,), jnp.int32),
            pltpu.SMEM((places,), jnp.int32),
            pltpu.SMEM((places,), jnp.int32),
        ]
        + solve_scratch()
        + [pltpu.SemaphoreType.DMA]
        + [pltpu.VMEM((ROWS, LANES), F32)] * (2 if part == 2 else 0),
        compiler_params=PARAMS,
        cost_estimate=cost,
        name="solve_part",
    )(*operands)


def near_shards(row_total, col_total, orbitals, pair_list, pair_count):
    row_swap = lambda values, flip: swap(values, "row", row_total, flip)
    col_swap = lambda values, flip: swap(values, "col", col_total, flip)
    both = lambda a, b: jnp.concatenate([a, b], axis=0)

    def corner_swap(values):
        places = list(itertools.product(range(row_total), range(col_total)))
        at = lambda row, col: row * col_total + col
        pairs = [(at(row, col), at(row ^ 1, col ^ 2)) for row, col in places]
        return lax.ppermute(values, ("row", "col"), pairs)

    counts = list_counts(pair_list, pair_count)
    own = add_counts(pack_band(orbitals), col_total, counts, col_swap(counts, 1))
    in_order = lambda *values: lax.optimization_barrier(values)
    mate, x, y, xy, z, w = in_order(
        col_swap(own, 1),
        col_swap(own, 2),
        row_swap(own, 1),
        corner_swap(own),
        row_swap(own, 2),
        row_swap(own, 4),
    )
    w_z, w_xy = in_order(both(w, z), both(w, xy))
    over_x, over_y, over_z = col_swap(w_z, 2), row_swap(w_z, 1), row_swap(w_xy, 2)
    tables = [jnp.asarray(table) for table in solve_tables()]
    blocks = [own, w, z, y, x, xy]
    *waves, sum0, sum1 = near_part(row_total, col_total, 0, [*blocks, mate, *tables])
    sum0, sum1, over_x, over_y, over_z = in_order(sum0, sum1, over_x, over_y, over_z)
    last = (
        row_swap(over_x[:1], 1),
        row_swap(both(over_x[:1], over_y[:1]), 2),
        corner_swap(over_z[:1]),
    )
    for part, arrived in enumerate(((over_x, over_y, over_z), last), 1):
        blocks += arrived
        operands = [*blocks, mate, *tables, *waves, sum0, sum1]
        sum0, sum1 = near_part(row_total, col_total, part, operands)
    return finish(sum0, col_swap(sum1, 1))


def far_shards(row_total, col_total, orbitals, pair_list, pair_count):
    counts = count_pairs(pair_list, pair_count, row_total, col_total)
    own = pack_band(orbitals)
    axes = ("row", "col")
    table = lax.all_gather(counts.reshape(-1), axes)
    table = table.reshape(row_total, col_total, col_total, row_total)
    wide = col_total // 2
    column = lax.all_gather(own[0], "row")
    columns = [column] + [swap(column, "col", col_total, 2 * x) for x in range(1, wide)]
    bands = jnp.concatenate(columns, axis=0)
    row = lax.axis_index("row")
    col = lax.axis_index("col")
    mine = jnp.stack([col, col ^ 1])
    other_col = ((col // 2) ^ lax.iota(jnp.int32, wide)) * 2 + col % 2
    other_row = lax.iota(jnp.int32, row_total)
    direct = table[row][other_col][:, mine]
    direct = jnp.transpose(direct, (1, 2, 0))
    mirror = table[:, :, :, row][:, mine][:, :, other_col]
    mirror = jnp.transpose(mirror, (1, 0, 2))
    same = (mine[:, None, None] == other_col[None, None, :]) & (other_row == row)[None, :, None]
    weights = (direct + jnp.where(same, 0.0, mirror)).astype(jnp.int32).reshape(-1)
    index = lax.iota(jnp.int32, weights.shape[0])
    order = jnp.argsort(jnp.where(weights > 0, 0, 1), stable=True)
    pad = lambda values: jnp.pad(values.astype(jnp.int32), (0, SIDE))
    slots = row_total * wide
    slot = order % slots
    band = (slot % wide) * row_total + slot // wide
    total = jnp.sum((weights > 0).astype(jnp.int32)).reshape(1)
    fields = pl.pallas_call(
        far_kernel,
        out_shape=pair_of(FLAT),
        in_specs=[SMEM_SPEC] * 4 + [ANY_SPEC] + [VMEM_SPEC] * 9,
        out_specs=[VMEM_SPEC] * 2,
        scratch_shapes=[pltpu.VMEM((PACK, LANES), BF16)]
        + [pltpu.VMEM((ROWS, LANES), F32)] * 4
        + solve_scratch(),
        compiler_params=PARAMS,
        name="solve_pairs",
    )(
        total,
        pad(band),
        pad(order // slots),
        pad(weights[order]),
        bands,
        own,
        swap(own, "col", col_total, 1),
        *map(jnp.asarray, solve_tables()),
    )
    return finish(fields[0], swap(fields[1], "col", col_total, 1))


def solution(mesh):
    row_total, col_total = mesh.shape["row"], mesh.shape["col"]
    near = (row_total, col_total) == NEAR
    shards = near_shards if near else far_shards
    return jax.shard_map(
        functools.partial(shards, row_total, col_total),
        mesh=mesh,
        in_specs=(P(("row", "col"), None), P(("row", "col"), None, None), P(("row", "col"))),
        out_specs=P(("row", "col"), None),
        check_vma=False,
    )
```

```python
import functools
import itertools

import jax
import jax.numpy as jnp
import ml_dtypes
import numpy as np
from jax import lax
from jax.experimental import pallas as pl
from jax.experimental.pallas import tpu as pltpu
from jax.sharding import PartitionSpec as P

GX = 40
LANES = 128
SIDE = 3
THIRD = -(-GX // SIDE)
PACK = THIRD * GX
ROWS = SIDE * PACK
LIVE = GX * GX
SPARE = SIDE * GX
FLAT = LIVE * GX // LANES
CHUNK = PACK // 16
FLAT_ROWS = SIDE * CHUNK * 5 + 8
DUO = 2 * GX
QUAD = 4 * GX
PITCH = GX + 1
VMEM_LIMIT = 16 * 1024 * 1024
screen_width = 0.9
F32 = jnp.float32
BF16 = jnp.bfloat16


def real_basis():
    half = GX // 2
    point = np.arange(GX)
    rows = [np.cos(2 * np.pi * (k * point % GX) / GX) for k in range(half + 1)]
    rows += [np.sin(2 * np.pi * (k * point % GX) / GX) for k in range(1, half)]
    frequency = np.concatenate([np.arange(half + 1), np.arange(1, half)])
    norm = np.where((frequency == 0) | (frequency == half), 1.0, 2.0) / GX
    return np.stack(rows), frequency, norm


def halves(table):
    high = table.astype(ml_dtypes.bfloat16)
    low = (table - high.astype(np.float64)).astype(ml_dtypes.bfloat16)
    return high, low


def left_table(table):
    high, low = halves(np.kron(np.eye(2), table))
    return np.concatenate([high, low, high], axis=1)


def right_table(table):
    wide = np.zeros((LANES, LANES))
    for p in range(SIDE):
        wide[p * GX : (p + 1) * GX, p * GX : (p + 1) * GX] = table
    high, low = halves(wide)
    both = np.concatenate([high, low], axis=1)
    return np.concatenate([both, both], axis=0)


def kernel_table():
    _, frequency, norm = real_basis()
    wave = frequency * (2.0 * np.pi / GX)
    squared = wave * wave
    total = squared[:, None, None] + squared[None, :, None] + squared[None, None, :]
    safe = np.where(total > 0, total, 1.0)
    screened = 4.0 * np.pi * (1.0 - np.exp(-safe / (4.0 * screen_width**2))) / safe
    kernel = np.where(total > 0, screened, np.pi / screen_width**2)
    kernel = kernel * norm[:, None, None] * norm[None, :, None] * norm[None, None, :]
    rows = np.swapaxes(kernel, 0, 1).reshape(LIVE, GX)
    out = np.zeros((LIVE, LANES), np.float32)
    for p in range(SIDE):
        out[:, p * GX : (p + 1) * GX] = rows
    return out


def place(out, row, col):
    for z in range(GX):
        out[row + z, col + z] = 1.0


def spread_table():
    out = np.zeros((SIDE * LANES, SIDE * LANES), np.float32)
    for third in range(SIDE):
        for p in range(SIDE):
            place(out, p * LANES + third * GX, third * LANES + p * GX)
    return out.astype(ml_dtypes.bfloat16)


def repeat_table():
    out = np.zeros((LANES, SIDE * LANES), np.float32)
    for third in range(SIDE):
        for p in range(SIDE):
            place(out, third * GX, third * LANES + p * GX)
    return out.astype(ml_dtypes.bfloat16)


def dot(a, b):
    return jnp.dot(a, b, preferred_element_type=F32)


def split(values):
    high = values.astype(BF16)
    return high, (values - high.astype(F32)).astype(BF16)


def contract_rows(table, values):
    high, low = split(values)
    return dot(table, jnp.concatenate([high, high, low], axis=0))


def contract_lanes(values, table):
    both = dot(jnp.concatenate(split(values), axis=1), table)
    return both[:, :LANES] + both[:, LANES:]


def fold(values):
    return jnp.concatenate([values[:DUO], values[DUO:]], axis=1)


def unfold(values):
    return jnp.concatenate([values[:, :LANES], values[:, LANES:]], axis=0)


def quad(step):
    return pl.ds(step * QUAD, QUAD)


def joined(planes):
    left = jnp.concatenate(planes[:2], axis=0)
    return jnp.concatenate([left, jnp.concatenate(planes[2:], axis=0)], axis=1)


def parted(values):
    return [
        values[i % 2 * GX : i % 2 * GX + GX, i // 2 * LANES : (i // 2 + 1) * LANES] for i in range(4)
    ]


def load_planes(ref, step):
    return joined([ref[pl.ds(step * 4 + i, GX, stride=PITCH), :] for i in range(4)])


def store_planes(ref, step, values):
    for i, plane in enumerate(parted(values)):
        ref[pl.ds(step * 4 + i, GX, stride=PITCH), :] = plane


def load_x_planes(ref, step):
    return joined([ref[pl.ds((step * 4 + i) * PITCH, GX), :] for i in range(4)])


def store_x_planes(ref, step, values):
    for i, plane in enumerate(parted(values)):
        ref[pl.ds((step * 4 + i) * PITCH, GX), :] = plane


def count_vector(pairs, live):
    slots = pairs.shape[1]
    row = lax.broadcasted_iota(jnp.int32, (16, slots), 0)
    lane = lax.broadcasted_iota(jnp.int32, (LANES, slots), 0) - SPARE
    first = (pairs[0:1] == row) & (lax.broadcasted_iota(jnp.int32, (16, slots), 1) < live)
    second = jnp.where(pairs[1:2] == lane, 1.0, 0.0)
    contract = (((1,), (1,)), ((), ()))
    return lax.dot_general(jnp.where(first, 1.0, 0.0), second, contract, preferred_element_type=F32)


def unroll_rows(copy):
    for k in range(FLAT):
        copy(k, slice(k * LANES, (k + 1) * LANES))


def pack_kernel(band_ref, out_ref, flat_ref, wide_ref):
    def to_rows(k, lanes):
        flat_ref[k : k + 1, :] = band_ref[0:1, lanes].astype(F32)

    unroll_rows(to_rows)
    unused = FLAT_ROWS - FLAT
    flat_ref[FLAT:FLAT_ROWS, :] = jnp.zeros((unused, LANES), F32)
    lane = lax.broadcasted_iota(jnp.int32, (1, LANES), 1)
    for q in range(16):
        row, offset = divmod(q * GX, LANES)
        packed = jnp.zeros((CHUNK, LANES), F32)
        for third in range(SIDE):
            start = third * CHUNK * 5 + row
            values = flat_ref[pl.ds(start, CHUNK, stride=5), :]
            if offset + GX > LANES:
                after = flat_ref[pl.ds(start + 1, CHUNK, stride=5), :]
                values = jnp.where(lane >= offset, values, after)
            shift = (third * GX - offset) % LANES
            values = pltpu.roll(values, shift, 1) if shift else values
            packed = jnp.where(lane // GX == third, values, packed)
        wide_ref[pl.ds(q, CHUNK, stride=16), :] = packed
    out_ref[0] = wide_ref[...].astype(BF16)


def list_kernel(pairs_ref, live_ref, out_ref):
    out_ref[...] = count_vector(pairs_ref[0], live_ref[...])


def count_kernel(col_total, packed_ref, own_ref, mate_ref, out_ref):
    out_ref[...] = packed_ref[...]
    counts = own_ref[...] + pltpu.roll(mate_ref[...], col_total, 0)
    out_ref[0, 0:16, :] = (packed_ref[0, 0:16, :].astype(F32) + counts).astype(BF16)


def spread_waves(own_bands, repeat_ref, wave_refs):
    for band, wave_ref in zip(own_bands, wave_refs):
        wide = dot(band, repeat_ref[...])
        for third in range(SIDE):
            wave_ref[pl.ds(third * PACK, PACK), :] = wide[:, third * LANES : (third + 1) * LANES]


def clear(sum_refs):
    for sum_ref in sum_refs:
        sum_ref[...] = jnp.zeros_like(sum_ref)


def lane_side():
    return lax.broadcasted_iota(jnp.int32, (1, LANES), 1) // GX


def solve_trios(first, count, lists, load_band, tables, wave_refs, sum_refs, scratch):
    spread_ref, _, z_ref, z_back_ref, row_ref, row_back_ref, kernel_ref = tables
    trio_ref, partner_ref, work_ref, work2_ref = scratch
    slot_list, band_list, weight_list = lists
    side = lane_side()

    def by_side(values):
        row = jnp.zeros((1, LANES), F32)
        for p in range(SIDE):
            row = jnp.where(side == p, values[p].astype(F32), row)
        return row

    def trio(at, carry):
        places = [first + at * SIDE + p for p in range(SIDE)]
        for p, place in enumerate(places):
            load_band(slot_list[place], trio_ref, p)
        bands = [band_list[place] for place in places]
        weights = [weight_list[place] for place in places]
        is_mate = by_side(bands) > 0.5
        scales = [
            by_side([jnp.where(bands[p] == which, weights[p], 0) for p in range(SIDE)])
            for which in range(2)
        ]
        wide = dot(trio_ref[...], spread_ref[...])
        for third in range(SIDE):
            partner_ref[pl.ds(third * PACK, PACK), :] = wide[:, third * LANES : (third + 1) * LANES]

        steps = range(GX // 4)

        def forward():
            values = []
            for step in steps:
                wave = jnp.where(is_mate, wave_refs[1][quad(step), :], wave_refs[0][quad(step), :])
                values.append(partner_ref[quad(step), :] * wave)
            values = [contract_lanes(v, z_ref[...]) for v in values]
            values = [contract_rows(row_ref[...], fold(v)) for v in values]
            for step, v in zip(steps, values):
                store_x_planes(work_ref, step, v)

        def across():
            values = [load_planes(work_ref, step) for step in steps]
            values = [contract_rows(row_ref[...], v) for v in values]
            values = [v * fold(kernel_ref[quad(step), :]) for step, v in zip(steps, values)]
            values = [contract_rows(row_back_ref[...], v) for v in values]
            for step, v in zip(steps, values):
                store_planes(work2_ref, step, v)

        def back():
            values = [load_x_planes(work2_ref, step) for step in steps]
            values = [unfold(contract_rows(row_back_ref[...], v)) for v in values]
            values = [contract_lanes(v, z_back_ref[...]) for v in values]
            for step, v in zip(steps, values):
                v = v * partner_ref[quad(step), :]
                for sum_ref, scale in zip(sum_refs, scales):
                    sum_ref[quad(step), :] = sum_ref[quad(step), :] + v * scale

        for phase in (forward, across, back):
            phase()
        return carry

    lax.fori_loop(0, count, trio, 0)


def flat_fields(sum_refs, out_refs):
    lane = lax.broadcasted_iota(jnp.int32, (1, LANES), 1)
    rows = LIVE // 16
    for sum_ref, out_ref in zip(sum_refs, out_refs):
        flat = [jnp.zeros((rows, LANES), F32)] * 5
        for q in range(16):
            row, offset = divmod(q * GX, LANES)
            values = sum_ref[pl.ds(q, rows, stride=16), :]
            moved = jnp.zeros((rows, LANES), F32)
            for p in range(SIDE):
                shift = (offset - p * GX) % LANES
                moved = moved + (pltpu.roll(values, shift, 1) if shift else values)
            flat[row] = jnp.where(lane >= offset, moved, flat[row])
            if offset + GX > LANES:
                flat[row + 1] = jnp.where(lane < offset + GX - LANES, moved, flat[row + 1])
        for row in range(5):
            out_ref[pl.ds(row, rows, stride=5), :] = flat[row]


def near_kernel(row_total, col_total, part, *refs):
    stages = STAGES[: part + 1]
    blocks = [block for stage in stages for block in stage]
    band_refs, refs = refs[: len(blocks)], refs[len(blocks) :]
    bands = [(ref, at) for ref, block in zip(band_refs, blocks) for at in range(len(block))]
    flips = [flip for block in blocks for flip in block]
    mate_ref, tables, refs = refs[0], refs[1:8], refs[8:]
    if part:
        wave_refs, given_refs, out_refs, refs = refs[:2], refs[2:4], refs[4:6], refs[6:]
    else:
        wave_refs, out_refs, refs = refs[:2], refs[2:4], refs[4:]
    (count_vmem, count_smem, slot_list, band_list, weight_list), refs = refs[:5], refs[5:]
    scratch, sem = refs[:4], refs[4]
    sum_refs = refs[5:] if part == 2 else out_refs

    lane = lax.broadcasted_iota(jnp.int32, (8, LANES), 1)
    counts = jnp.zeros((8, LANES), F32)
    for s, (ref, at) in enumerate(bands):
        spare = ref[at, 0:16, :].astype(F32)[0:8]
        shift = (s * row_total - SPARE) % LANES
        moved = pltpu.roll(spare, shift, 1) if shift else spare
        counts = jnp.where(lane // row_total == s, moved, counts)
    count_vmem[...] = counts.astype(jnp.int32)
    copy = pltpu.make_async_copy(count_vmem, count_smem, sem)
    copy.start()
    if part:
        for sum_ref, given_ref in zip(sum_refs, given_refs):
            sum_ref[...] = given_ref[...]
    else:
        clear(sum_refs)
        spread_waves((band_refs[0][0], mate_ref[0]), tables[1], wave_refs)
    copy.wait()
    row = lax.axis_index("row")
    col = lax.axis_index("col")
    total = jnp.int32(0)
    done = jnp.int32(0)
    place = 0
    for step, stage in enumerate(stages):
        here = range(place, place + sum(len(block) for block in stage))
        place = here.stop
        for which, at in itertools.product(range(2), here):
            row_flip, col_flip = flips[at]
            row_place = flips.index((0, col_flip)) * row_total
            col_place = flips.index((row_flip, 0)) * row_total
            weight = count_smem[col ^ which, row_place + (row ^ row_flip)]
            if at or which:
                mirror = which * col_total + (col ^ col_flip)
                weight = weight + count_smem[mirror, col_place + row]
            slot_list[total] = at
            band_list[total] = which
            weight_list[total] = weight
            total = total + jnp.where(weight > 0, 1, 0)
        if step < 2:
            trios = jnp.minimum((total - done) // SIDE, CAPS[step])
            if step < part:
                done = done + trios * SIDE
    if part == 2:
        trios = (total - done + SIDE - 1) // SIDE
        for p in range(SIDE - 1):
            slot_list[total + p] = 0
            band_list[total + p] = 0
            weight_list[total + p] = 0

    def load_band(wanted, target, p):
        for place, (ref, at) in enumerate(bands):

            @pl.when(wanted == place)
            def _():
                target[:, p * LANES : (p + 1) * LANES] = ref[at]

    lists = (slot_list, band_list, weight_list)
    solve_trios(done, trios, lists, load_band, tables, wave_refs, sum_refs, scratch)
    if part == 2:
        flat_fields(sum_refs, out_refs)


def far_kernel(total_ref, slot_list, band_list, weight_list, bands_ref, own_ref, mate_ref, *refs):
    tables, out_refs, refs = refs[:7], refs[7:9], refs[9:]
    buffer, wave_refs, sum_refs, scratch = refs[0], refs[1:3], refs[3:5], refs[5:]
    spread_waves((own_ref[0], mate_ref[0]), tables[1], wave_refs)
    clear(sum_refs)

    def load_band(place, target, p):
        pltpu.sync_copy(bands_ref.at[place], buffer)
        target[:, p * LANES : (p + 1) * LANES] = buffer[...]

    lists = (slot_list, band_list, weight_list)
    trios = (total_ref[0] + SIDE - 1) // SIDE
    solve_trios(0, trios, lists, load_band, tables, wave_refs, sum_refs, scratch)
    flat_fields(sum_refs, out_refs)


def finish_kernel(own_ref, part_ref, out_ref):
    def to_lanes(k, lanes):
        out_ref[0:1, lanes] = own_ref[k : k + 1, :] + part_ref[k : k + 1, :]

    unroll_rows(to_lanes)


VMEM_SPEC = pl.BlockSpec(memory_space=pltpu.VMEM)
SMEM_SPEC = pl.BlockSpec(memory_space=pltpu.SMEM)
ANY_SPEC = pl.BlockSpec(memory_space=pl.ANY)
PARAMS = pltpu.CompilerParams(vmem_limit_bytes=VMEM_LIMIT)


def solve_tables():
    basis, _, _ = real_basis()
    return [
        spread_table(),
        repeat_table(),
        right_table(basis.T),
        right_table(basis),
        left_table(basis),
        left_table(basis.T),
        kernel_table(),
    ]


def solve_scratch():
    return [pltpu.VMEM((PACK, SIDE * LANES), BF16)] + [pltpu.VMEM((ROWS, LANES), F32)] * 3


def pair_of(rows):
    return [jax.ShapeDtypeStruct((rows, LANES), F32)] * 2


def swap(values, axis, size, flip):
    return lax.ppermute(values, axis, [(i, i ^ flip) for i in range(size)])


def count_pairs(pair_list, pair_count, row_total, col_total):
    slots = pair_list.shape[1]
    live = lax.iota(jnp.int32, slots) < pair_count[0]
    first = pair_list[0, :, 0][:, None, None] == lax.iota(jnp.int32, col_total)[None, :, None]
    second = pair_list[0, :, 1][:, None, None] == lax.iota(jnp.int32, row_total)[None, None, :]
    return jnp.sum((first & second & live[:, None, None]).astype(F32), axis=0)


def pack_band(orbitals):
    return pl.pallas_call(
        pack_kernel,
        out_shape=jax.ShapeDtypeStruct((1, PACK, LANES), BF16),
        in_specs=[VMEM_SPEC],
        out_specs=VMEM_SPEC,
        scratch_shapes=[pltpu.VMEM((FLAT_ROWS, LANES), F32), pltpu.VMEM((PACK, LANES), F32)],
        compiler_params=PARAMS,
        name="pack_band",
    )(orbitals)


def list_counts(pair_list, pair_count):
    return pl.pallas_call(
        list_kernel,
        out_shape=jax.ShapeDtypeStruct((16, LANES), F32),
        in_specs=[VMEM_SPEC] * 2,
        out_specs=VMEM_SPEC,
        compiler_params=PARAMS,
        name="list_counts",
    )(jnp.swapaxes(pair_list, 1, 2), pair_count.reshape(1, 1))


def add_counts(packed, col_total, counts, mate_counts):
    return pl.pallas_call(
        functools.partial(count_kernel, col_total),
        out_shape=jax.ShapeDtypeStruct(packed.shape, BF16),
        in_specs=[VMEM_SPEC] * 3,
        out_specs=VMEM_SPEC,
        compiler_params=PARAMS,
        name="add_counts",
    )(packed, counts, mate_counts)


def finish(own, part):
    return pl.pallas_call(
        finish_kernel,
        out_shape=jax.ShapeDtypeStruct((1, LIVE * GX), F32),
        in_specs=[VMEM_SPEC] * 2,
        out_specs=VMEM_SPEC,
        compiler_params=PARAMS,
        name="add_parts",
    )(own, part)


NEAR = (8, 4)
STAGES = (
    (((0, 0),), ((4, 0),), ((2, 0),), ((1, 0),), ((0, 2),)),
    (((4, 2), (2, 2)), ((5, 0), (1, 2)), ((6, 0), (3, 0))),
    (((6, 2), (3, 2)), ((5, 2),), ((7, 0),), ((7, 2),)),
)
CAPS = (2, 2)


def near_part(row_total, col_total, part, operands):
    places = 2 * row_total * (col_total // 2) + SIDE
    out_shape = pair_of(ROWS)
    if part == 0:
        out_shape = out_shape * 2
    if part == 2:
        out_shape = pair_of(FLAT)
    operands = list(operands)
    cost = pl.CostEstimate(flops=4 * 10**9, bytes_accessed=2 * 10**7, transcendentals=0)
    return pl.pallas_call(
        functools.partial(near_kernel, row_total, col_total, part),
        out_shape=out_shape,
        in_specs=[VMEM_SPEC] * len(operands),
        out_specs=[VMEM_SPEC] * len(out_shape),
        scratch_shapes=[
            pltpu.VMEM((8, LANES), jnp.int32),
            pltpu.SMEM((8, LANES), jnp.int32),
            pltpu.SMEM((places,), jnp.int32),
            pltpu.SMEM((places,), jnp.int32),
            pltpu.SMEM((places,), jnp.int32),
        ]
        + solve_scratch()
        + [pltpu.SemaphoreType.DMA]
        + [pltpu.VMEM((ROWS, LANES), F32)] * (2 if part == 2 else 0),
        compiler_params=PARAMS,
        cost_estimate=cost,
        name="solve_part",
    )(*operands)


def near_shards(row_total, col_total, orbitals, pair_list, pair_count):
    row_swap = lambda values, flip: swap(values, "row", row_total, flip)
    col_swap = lambda values, flip: swap(values, "col", col_total, flip)
    both = lambda a, b: jnp.concatenate([a, b], axis=0)

    def corner_swap(values):
        places = list(itertools.product(range(row_total), range(col_total)))
        at = lambda row, col: row * col_total + col
        pairs = [(at(row, col), at(row ^ 3, col)) for row, col in places]
        return lax.ppermute(values, ("row", "col"), pairs)

    counts = list_counts(pair_list, pair_count)
    own = add_counts(pack_band(orbitals), col_total, counts, col_swap(counts, 1))
    in_order = lambda *values: lax.optimization_barrier(values)
    mate, x, y, z, w = in_order(
        col_swap(own, 1), col_swap(own, 2), row_swap(own, 1), row_swap(own, 2), row_swap(own, 4)
    )
    w_z, w_x, w_y = in_order(both(w, z), both(w, x), both(w, y))
    over_x, over_y, over_z = col_swap(w_z, 2), row_swap(w_x, 1), row_swap(w_y, 2)
    tables = [jnp.asarray(table) for table in solve_tables()]
    blocks = [own, w, z, y, x]
    *waves, sum0, sum1 = near_part(row_total, col_total, 0, [*blocks, mate, *tables])
    sum0, sum1, over_x, over_y, over_z = in_order(sum0, sum1, over_x, over_y, over_z)
    last = (
        col_swap(over_z, 2),
        row_swap(over_x[:1], 1),
        row_swap(over_y[:1], 2),
        corner_swap(over_x[:1]),
    )
    for part, arrived in enumerate(((over_x, over_y, over_z), last), 1):
        blocks += arrived
        operands = [*blocks, mate, *tables, *waves, sum0, sum1]
        sum0, sum1 = near_part(row_total, col_total, part, operands)
    return finish(sum0, col_swap(sum1, 1))


def far_shards(row_total, col_total, orbitals, pair_list, pair_count):
    counts = count_pairs(pair_list, pair_count, row_total, col_total)
    own = pack_band(orbitals)
    axes = ("row", "col")
    table = lax.all_gather(counts.reshape(-1), axes)
    table = table.reshape(row_total, col_total, col_total, row_total)
    wide = col_total // 2
    column = lax.all_gather(own[0], "row")
    columns = [column] + [swap(column, "col", col_total, 2 * x) for x in range(1, wide)]
    bands = jnp.concatenate(columns, axis=0)
    row = lax.axis_index("row")
    col = lax.axis_index("col")
    mine = jnp.stack([col, col ^ 1])
    other_col = ((col // 2) ^ lax.iota(jnp.int32, wide)) * 2 + col % 2
    other_row = lax.iota(jnp.int32, row_total)
    direct = table[row][other_col][:, mine]
    direct = jnp.transpose(direct, (1, 2, 0))
    mirror = table[:, :, :, row][:, mine][:, :, other_col]
    mirror = jnp.transpose(mirror, (1, 0, 2))
    same = (mine[:, None, None] == other_col[None, None, :]) & (other_row == row)[None, :, None]
    weights = (direct + jnp.where(same, 0.0, mirror)).astype(jnp.int32).reshape(-1)
    index = lax.iota(jnp.int32, weights.shape[0])
    order = jnp.argsort(jnp.where(weights > 0, 0, 1), stable=True)
    pad = lambda values: jnp.pad(values.astype(jnp.int32), (0, SIDE))
    slots = row_total * wide
    slot = order % slots
    band = (slot % wide) * row_total + slot // wide
    total = jnp.sum((weights > 0).astype(jnp.int32)).reshape(1)
    fields = pl.pallas_call(
        far_kernel,
        out_shape=pair_of(FLAT),
        in_specs=[SMEM_SPEC] * 4 + [ANY_SPEC] + [VMEM_SPEC] * 9,
        out_specs=[VMEM_SPEC] * 2,
        scratch_shapes=[pltpu.VMEM((PACK, LANES), BF16)]
        + [pltpu.VMEM((ROWS, LANES), F32)] * 4
        + solve_scratch(),
        compiler_params=PARAMS,
        name="solve_pairs",
    )(
        total,
        pad(band),
        pad(order // slots),
        pad(weights[order]),
        bands,
        own,
        swap(own, "col", col_total, 1),
        *map(jnp.asarray, solve_tables()),
    )
    return finish(fields[0], swap(fields[1], "col", col_total, 1))


def solution(mesh):
    row_total, col_total = mesh.shape["row"], mesh.shape["col"]
    near = (row_total, col_total) == NEAR
    shards = near_shards if near else far_shards
    return jax.shard_map(
        functools.partial(shards, row_total, col_total),
        mesh=mesh,
        in_specs=(P(("row", "col"), None), P(("row", "col"), None, None), P(("row", "col"))),
        out_specs=P(("row", "col"), None),
        check_vma=False,
    )
```

```python
import functools
import itertools

import jax
import jax.numpy as jnp
import ml_dtypes
import numpy as np
from jax import lax
from jax.experimental import pallas as pl
from jax.experimental.pallas import tpu as pltpu
from jax.sharding import PartitionSpec as P

GX = 40
LANES = 128
SIDE = 3
THIRD = -(-GX // SIDE)
PACK = THIRD * GX
ROWS = SIDE * PACK
LIVE = GX * GX
SPARE = SIDE * GX
FLAT = LIVE * GX // LANES
CHUNK = PACK // 16
FLAT_ROWS = SIDE * CHUNK * 5 + 8
PITCHED = LIVE // 16 * 17
DUO = 2 * GX
QUAD = 4 * GX
PITCH = GX + 1
VMEM_LIMIT = 16 * 1024 * 1024
screen_width = 0.9
F32 = jnp.float32
BF16 = jnp.bfloat16


def real_basis():
    half = GX // 2
    point = np.arange(GX)
    rows = [np.cos(2 * np.pi * (k * point % GX) / GX) for k in range(half + 1)]
    rows += [np.sin(2 * np.pi * (k * point % GX) / GX) for k in range(1, half)]
    frequency = np.concatenate([np.arange(half + 1), np.arange(1, half)])
    norm = np.where((frequency == 0) | (frequency == half), 1.0, 2.0) / GX
    return np.stack(rows), frequency, norm


def halves(table):
    high = table.astype(ml_dtypes.bfloat16)
    low = (table - high.astype(np.float64)).astype(ml_dtypes.bfloat16)
    return high, low


def left_table(table):
    high, low = halves(np.kron(np.eye(2), table))
    return np.concatenate([high, low, high], axis=1)


def right_table(table):
    wide = np.zeros((LANES, LANES))
    for p in range(SIDE):
        wide[p * GX : (p + 1) * GX, p * GX : (p + 1) * GX] = table
    high, low = halves(wide)
    both = np.concatenate([high, low], axis=1)
    return np.concatenate([both, both], axis=0)


def kernel_table():
    _, frequency, norm = real_basis()
    wave = frequency * (2.0 * np.pi / GX)
    squared = wave * wave
    total = squared[:, None, None] + squared[None, :, None] + squared[None, None, :]
    safe = np.where(total > 0, total, 1.0)
    screened = 4.0 * np.pi * (1.0 - np.exp(-safe / (4.0 * screen_width**2))) / safe
    kernel = np.where(total > 0, screened, np.pi / screen_width**2)
    kernel = kernel * norm[:, None, None] * norm[None, :, None] * norm[None, None, :]
    rows = np.swapaxes(kernel, 0, 1).reshape(LIVE, GX)
    out = np.zeros((LIVE, LANES), np.float32)
    for p in range(SIDE):
        out[:, p * GX : (p + 1) * GX] = rows
    return out


def place(out, row, col):
    for z in range(GX):
        out[row + z, col + z] = 1.0


def spread_table():
    out = np.zeros((SIDE * LANES, SIDE * LANES), np.float32)
    for third in range(SIDE):
        for p in range(SIDE):
            place(out, p * LANES + third * GX, third * LANES + p * GX)
    return out.astype(ml_dtypes.bfloat16)


def repeat_table():
    out = np.zeros((LANES, SIDE * LANES), np.float32)
    for third in range(SIDE):
        for p in range(SIDE):
            place(out, third * GX, third * LANES + p * GX)
    return out.astype(ml_dtypes.bfloat16)


def dot(a, b):
    return jnp.dot(a, b, preferred_element_type=F32)


def split(values):
    high = values.astype(BF16)
    return high, (values - high.astype(F32)).astype(BF16)


def contract_rows(table, values):
    high, low = split(values)
    return dot(table, jnp.concatenate([high, high, low], axis=0))


def contract_lanes(values, table):
    both = dot(jnp.concatenate(split(values), axis=1), table)
    return both[:, :LANES] + both[:, LANES:]


def fold(values):
    return jnp.concatenate([values[:DUO], values[DUO:]], axis=1)


def unfold(values):
    return jnp.concatenate([values[:, :LANES], values[:, LANES:]], axis=0)


def quad(step):
    return pl.ds(step * QUAD, QUAD)


def joined(planes):
    left = jnp.concatenate(planes[:2], axis=0)
    return jnp.concatenate([left, jnp.concatenate(planes[2:], axis=0)], axis=1)


def parted(values):
    return [
        values[i % 2 * GX : i % 2 * GX + GX, i // 2 * LANES : (i // 2 + 1) * LANES] for i in range(4)
    ]


def load_planes(ref, step):
    return joined([ref[pl.ds(step * 4 + i, GX, stride=PITCH), :] for i in range(4)])


def store_planes(ref, step, values):
    for i, plane in enumerate(parted(values)):
        ref[pl.ds(step * 4 + i, GX, stride=PITCH), :] = plane


def load_x_planes(ref, step):
    return joined([ref[pl.ds((step * 4 + i) * PITCH, GX), :] for i in range(4)])


def store_x_planes(ref, step, values):
    for i, plane in enumerate(parted(values)):
        ref[pl.ds((step * 4 + i) * PITCH, GX), :] = plane


def count_vector(pairs, live):
    slots = pairs.shape[1]
    row = lax.broadcasted_iota(jnp.int32, (16, slots), 0)
    lane = lax.broadcasted_iota(jnp.int32, (LANES, slots), 0) - SPARE
    first = (pairs[0:1] == row) & (lax.broadcasted_iota(jnp.int32, (16, slots), 1) < live)
    second = jnp.where(pairs[1:2] == lane, 1.0, 0.0)
    contract = (((1,), (1,)), ((), ()))
    return lax.dot_general(jnp.where(first, 1.0, 0.0), second, contract, preferred_element_type=F32)


def unroll_rows(copy):
    for k in range(FLAT):
        copy(k, slice(k * LANES, (k + 1) * LANES))


def pack_kernel(band_ref, out_ref, flat_ref, wide_ref):
    def to_rows(k, lanes):
        flat_ref[k : k + 1, :] = band_ref[0:1, lanes].astype(F32)

    unroll_rows(to_rows)
    unused = FLAT_ROWS - FLAT
    flat_ref[FLAT:FLAT_ROWS, :] = jnp.zeros((unused, LANES), F32)
    lane = lax.broadcasted_iota(jnp.int32, (1, LANES), 1)
    for q in range(16):
        row, offset = divmod(q * GX, LANES)
        packed = jnp.zeros((CHUNK, LANES), F32)
        for third in range(SIDE):
            start = third * CHUNK * 5 + row
            values = flat_ref[pl.ds(start, CHUNK, stride=5), :]
            if offset + GX > LANES:
                after = flat_ref[pl.ds(start + 1, CHUNK, stride=5), :]
                values = jnp.where(lane >= offset, values, after)
            shift = (third * GX - offset) % LANES
            values = pltpu.roll(values, shift, 1) if shift else values
            packed = jnp.where(lane // GX == third, values, packed)
        wide_ref[pl.ds(q, CHUNK, stride=16), :] = packed
    out_ref[0] = wide_ref[...].astype(BF16)


def list_kernel(pairs_ref, live_ref, out_ref):
    out_ref[...] = count_vector(pairs_ref[0], live_ref[...])


def count_kernel(col_total, packed_ref, own_ref, mate_ref, out_ref):
    out_ref[...] = packed_ref[...]
    counts = own_ref[...] + pltpu.roll(mate_ref[...], col_total, 0)
    out_ref[0, 0:16, :] = (packed_ref[0, 0:16, :].astype(F32) + counts).astype(BF16)


def spread_waves(own_bands, repeat_ref, wave_refs):
    for band, wave_ref in zip(own_bands, wave_refs):
        wide = dot(band, repeat_ref[...])
        for third in range(SIDE):
            wave_ref[pl.ds(third * PACK, PACK), :] = wide[:, third * LANES : (third + 1) * LANES]


def clear(sum_refs):
    for sum_ref in sum_refs:
        sum_ref[...] = jnp.zeros_like(sum_ref)


def lane_side():
    return lax.broadcasted_iota(jnp.int32, (1, LANES), 1) // GX


def solve_trios(first, count, lists, load_band, tables, wave_refs, sum_refs, scratch):
    spread_ref, _, z_ref, z_back_ref, row_ref, row_back_ref, kernel_ref = tables
    trio_ref, partner_ref, work_ref, work2_ref = scratch
    slot_list, band_list, weight_list = lists
    side = lane_side()

    def by_side(values):
        row = jnp.zeros((1, LANES), F32)
        for p in range(SIDE):
            row = jnp.where(side == p, values[p].astype(F32), row)
        return row

    def trio(at, carry):
        places = [first + at * SIDE + p for p in range(SIDE)]
        for p, place in enumerate(places):
            load_band(slot_list[place], trio_ref, p)
        bands = [band_list[place] for place in places]
        weights = [weight_list[place] for place in places]
        is_mate = by_side(bands) > 0.5
        scales = [
            by_side([jnp.where(bands[p] == which, weights[p], 0) for p in range(SIDE)])
            for which in range(2)
        ]
        wide = dot(trio_ref[...], spread_ref[...])
        for third in range(SIDE):
            partner_ref[pl.ds(third * PACK, PACK), :] = wide[:, third * LANES : (third + 1) * LANES]

        steps = range(GX // 4)

        def forward():
            values = []
            for step in steps:
                wave = jnp.where(is_mate, wave_refs[1][quad(step), :], wave_refs[0][quad(step), :])
                values.append(partner_ref[quad(step), :] * wave)
            values = [contract_lanes(v, z_ref[...]) for v in values]
            values = [contract_rows(row_ref[...], fold(v)) for v in values]
            for step, v in zip(steps, values):
                store_x_planes(work_ref, step, v)

        def across():
            values = [load_planes(work_ref, step) for step in steps]
            values = [contract_rows(row_ref[...], v) for v in values]
            values = [v * fold(kernel_ref[quad(step), :]) for step, v in zip(steps, values)]
            values = [contract_rows(row_back_ref[...], v) for v in values]
            for step, v in zip(steps, values):
                store_planes(work2_ref, step, v)

        def back():
            values = [load_x_planes(work2_ref, step) for step in steps]
            values = [unfold(contract_rows(row_back_ref[...], v)) for v in values]
            values = [contract_lanes(v, z_back_ref[...]) for v in values]
            for step, v in zip(steps, values):
                v = v * partner_ref[quad(step), :]
                for sum_ref, scale in zip(sum_refs, scales):
                    sum_ref[quad(step), :] = sum_ref[quad(step), :] + v * scale

        for phase in (forward, across, back):
            phase()
        return carry

    lax.fori_loop(0, count, trio, 0)


def flat_field(sum_ref, out_ref, pitched_ref):
    lane = lax.broadcasted_iota(jnp.int32, (1, LANES), 1)
    rows = LIVE // 16
    for group in range(rows):
        pitched_ref[group * 17 : group * 17 + 16, :] = sum_ref[group * 16 : group * 16 + 16, :]
    flat = [jnp.zeros((rows, LANES), F32)] * 5
    for q in range(16):
        row, offset = divmod(q * GX, LANES)
        values = pitched_ref[pl.ds(q, rows, stride=17), :]
        moved = jnp.zeros((rows, LANES), F32)
        for p in range(SIDE):
            shift = (offset - p * GX) % LANES
            moved = moved + (pltpu.roll(values, shift, 1) if shift else values)
        flat[row] = jnp.where(lane >= offset, moved, flat[row])
        if offset + GX > LANES:
            flat[row + 1] = jnp.where(lane < offset + GX - LANES, moved, flat[row + 1])
    for row in range(5):
        out_ref[pl.ds(row, rows, stride=5), :] = flat[row]


def near_kernel(row_total, col_total, part, *refs):
    stages = STAGES[: part + 1]
    blocks = [block for stage in stages for block in stage]
    band_refs, refs = refs[: len(blocks)], refs[len(blocks) :]
    bands = [(ref, at) for ref, block in zip(band_refs, blocks) for at in range(len(block))]
    flips = [flip for block in blocks for flip in block]
    mate_ref, tables, refs = refs[0], refs[1:8], refs[8:]
    if part:
        wave_refs, given_refs, out_refs, refs = refs[:2], refs[2:4], refs[4:6], refs[6:]
    else:
        wave_refs, out_refs, refs = refs[:2], refs[2:4], refs[4:]
    (count_vmem, count_smem, slot_list, band_list, weight_list), refs = refs[:5], refs[5:]
    scratch, sem = refs[:4], refs[4]
    sum_refs = (out_refs[0], refs[5]) if part == 2 else out_refs

    lane = lax.broadcasted_iota(jnp.int32, (8, LANES), 1)
    counts = jnp.zeros((8, LANES), F32)
    for s, (ref, at) in enumerate(bands):
        spare = ref[at, 0:16, :].astype(F32)[0:8]
        shift = (s * row_total - SPARE) % LANES
        moved = pltpu.roll(spare, shift, 1) if shift else spare
        counts = jnp.where(lane // row_total == s, moved, counts)
    count_vmem[...] = counts.astype(jnp.int32)
    copy = pltpu.make_async_copy(count_vmem, count_smem, sem)
    copy.start()
    if part:
        for sum_ref, given_ref in zip(sum_refs, given_refs):
            sum_ref[...] = given_ref[...]
    else:
        clear(sum_refs)
        spread_waves((band_refs[0][0], mate_ref[0]), tables[1], wave_refs)
    copy.wait()
    row = lax.axis_index("row")
    col = lax.axis_index("col")
    total = jnp.int32(0)
    done = jnp.int32(0)
    place = 0
    for step, stage in enumerate(stages):
        here = range(place, place + sum(len(block) for block in stage))
        place = here.stop
        for which, at in itertools.product(range(2), here):
            row_flip, col_flip = flips[at]
            row_place = flips.index((0, col_flip)) * row_total
            col_place = flips.index((row_flip, 0)) * row_total
            weight = count_smem[col ^ which, row_place + (row ^ row_flip)]
            if at or which:
                mirror = which * col_total + (col ^ col_flip)
                weight = weight + count_smem[mirror, col_place + row]
            slot_list[total] = at
            band_list[total] = which
            weight_list[total] = weight
            total = total + jnp.where(weight > 0, 1, 0)
        if step < 2:
            trios = jnp.minimum((total - done) // SIDE, CAPS[step])
            if step < part:
                done = done + trios * SIDE
    if part == 2:
        trios = (total - done + SIDE - 1) // SIDE
        for p in range(SIDE - 1):
            slot_list[total + p] = 0
            band_list[total + p] = 0
            weight_list[total + p] = 0

    def load_band(wanted, target, p):
        for place, (ref, at) in enumerate(bands):

            @pl.when(wanted == place)
            def _():
                target[:, p * LANES : (p + 1) * LANES] = ref[at]

    lists = (slot_list, band_list, weight_list)
    solve_trios(done, trios, lists, load_band, tables, wave_refs, sum_refs, scratch)
    if part == 2:
        flat_field(sum_refs[1], out_refs[1], refs[6])


def far_kernel(total_ref, slot_list, band_list, weight_list, bands_ref, own_ref, mate_ref, *refs):
    tables, out_refs, refs = refs[:7], refs[7:9], refs[9:]
    buffer, wave_refs, sum_refs = refs[0], refs[1:3], (out_refs[0], refs[3])
    pitched_ref, scratch = refs[4], refs[5:]
    spread_waves((own_ref[0], mate_ref[0]), tables[1], wave_refs)
    clear(sum_refs)

    def load_band(place, target, p):
        pltpu.sync_copy(bands_ref.at[place], buffer)
        target[:, p * LANES : (p + 1) * LANES] = buffer[...]

    lists = (slot_list, band_list, weight_list)
    trios = (total_ref[0] + SIDE - 1) // SIDE
    solve_trios(0, trios, lists, load_band, tables, wave_refs, sum_refs, scratch)
    flat_field(sum_refs[1], out_refs[1], pitched_ref)


def flat_kernel(sum_ref, out_ref, pitched_ref):
    flat_field(sum_ref, out_ref, pitched_ref)


def finish_kernel(own_ref, part_ref, out_ref):
    def to_lanes(k, lanes):
        out_ref[0:1, lanes] = own_ref[k : k + 1, :] + part_ref[k : k + 1, :]

    unroll_rows(to_lanes)


VMEM_SPEC = pl.BlockSpec(memory_space=pltpu.VMEM)
SMEM_SPEC = pl.BlockSpec(memory_space=pltpu.SMEM)
ANY_SPEC = pl.BlockSpec(memory_space=pl.ANY)
PARAMS = pltpu.CompilerParams(vmem_limit_bytes=VMEM_LIMIT)


def solve_tables():
    basis, _, _ = real_basis()
    return [
        spread_table(),
        repeat_table(),
        right_table(basis.T),
        right_table(basis),
        left_table(basis),
        left_table(basis.T),
        kernel_table(),
    ]


def solve_scratch():
    return [pltpu.VMEM((PACK, SIDE * LANES), BF16)] + [pltpu.VMEM((ROWS, LANES), F32)] * 3


def wide_of(rows):
    return jax.ShapeDtypeStruct((rows, LANES), F32)


def swap(values, axis, size, flip):
    return lax.ppermute(values, axis, [(i, i ^ flip) for i in range(size)])


def count_pairs(pair_list, pair_count, row_total, col_total):
    slots = pair_list.shape[1]
    live = lax.iota(jnp.int32, slots) < pair_count[0]
    first = pair_list[0, :, 0][:, None, None] == lax.iota(jnp.int32, col_total)[None, :, None]
    second = pair_list[0, :, 1][:, None, None] == lax.iota(jnp.int32, row_total)[None, None, :]
    return jnp.sum((first & second & live[:, None, None]).astype(F32), axis=0)


def pack_band(orbitals):
    return pl.pallas_call(
        pack_kernel,
        out_shape=jax.ShapeDtypeStruct((1, PACK, LANES), BF16),
        in_specs=[VMEM_SPEC],
        out_specs=VMEM_SPEC,
        scratch_shapes=[pltpu.VMEM((FLAT_ROWS, LANES), F32), pltpu.VMEM((PACK, LANES), F32)],
        compiler_params=PARAMS,
        name="pack_band",
    )(orbitals)


def list_counts(pair_list, pair_count):
    return pl.pallas_call(
        list_kernel,
        out_shape=jax.ShapeDtypeStruct((16, LANES), F32),
        in_specs=[VMEM_SPEC] * 2,
        out_specs=VMEM_SPEC,
        compiler_params=PARAMS,
        name="list_counts",
    )(jnp.swapaxes(pair_list, 1, 2), pair_count.reshape(1, 1))


def add_counts(packed, col_total, counts, mate_counts):
    return pl.pallas_call(
        functools.partial(count_kernel, col_total),
        out_shape=jax.ShapeDtypeStruct(packed.shape, BF16),
        in_specs=[VMEM_SPEC] * 3,
        out_specs=VMEM_SPEC,
        compiler_params=PARAMS,
        name="add_counts",
    )(packed, counts, mate_counts)


def flatten(sums):
    return pl.pallas_call(
        flat_kernel,
        out_shape=wide_of(FLAT),
        in_specs=[VMEM_SPEC],
        out_specs=VMEM_SPEC,
        scratch_shapes=[pltpu.VMEM((PITCHED, LANES), F32)],
        compiler_params=PARAMS,
        name="flatten",
    )(sums)


def finish(own, part):
    return pl.pallas_call(
        finish_kernel,
        out_shape=jax.ShapeDtypeStruct((1, LIVE * GX), F32),
        in_specs=[VMEM_SPEC] * 2,
        out_specs=VMEM_SPEC,
        compiler_params=PARAMS,
        name="add_parts",
    )(own, part)


NEAR = (8, 4)
STAGES = (
    (((0, 0),), ((4, 0),), ((2, 0),), ((1, 0),), ((0, 2),)),
    (((4, 2), (2, 2)), ((5, 0), (1, 2)), ((6, 0), (3, 0))),
    (((6, 2), (3, 2)), ((5, 2),), ((7, 0),), ((7, 2),)),
)
CAPS = (2, 2)


def near_part(row_total, col_total, part, operands):
    places = 2 * row_total * (col_total // 2) + SIDE
    out_shape = [wide_of(ROWS)] * 2
    if part == 0:
        out_shape = out_shape * 2
    if part == 2:
        out_shape = [wide_of(ROWS), wide_of(FLAT)]
    operands = list(operands)
    cost = pl.CostEstimate(flops=4 * 10**9, bytes_accessed=2 * 10**7, transcendentals=0)
    return pl.pallas_call(
        functools.partial(near_kernel, row_total, col_total, part),
        out_shape=out_shape,
        in_specs=[VMEM_SPEC] * len(operands),
        out_specs=[VMEM_SPEC] * len(out_shape),
        scratch_shapes=[
            pltpu.VMEM((8, LANES), jnp.int32),
            pltpu.SMEM((8, LANES), jnp.int32),
            pltpu.SMEM((places,), jnp.int32),
            pltpu.SMEM((places,), jnp.int32),
            pltpu.SMEM((places,), jnp.int32),
        ]
        + solve_scratch()
        + [pltpu.SemaphoreType.DMA]
        + ([pltpu.VMEM((rows, LANES), F32) for rows in (ROWS, PITCHED)] if part == 2 else []),
        compiler_params=PARAMS,
        cost_estimate=cost,
        name="solve_part",
    )(*operands)


def near_shards(row_total, col_total, orbitals, pair_list, pair_count):
    row_swap = lambda values, flip: swap(values, "row", row_total, flip)
    col_swap = lambda values, flip: swap(values, "col", col_total, flip)
    both = lambda a, b: jnp.concatenate([a, b], axis=0)

    def corner_swap(values):
        places = list(itertools.product(range(row_total), range(col_total)))
        at = lambda row, col: row * col_total + col
        pairs = [(at(row, col), at(row ^ 3, col)) for row, col in places]
        return lax.ppermute(values, ("row", "col"), pairs)

    counts = list_counts(pair_list, pair_count)
    own = add_counts(pack_band(orbitals), col_total, counts, col_swap(counts, 1))
    in_order = lambda *values: lax.optimization_barrier(values)
    mate, x, y, z, w = in_order(
        col_swap(own, 1), col_swap(own, 2), row_swap(own, 1), row_swap(own, 2), row_swap(own, 4)
    )
    w_z, w_x, w_y = in_order(both(w, z), both(w, x), both(w, y))
    over_x, over_y, over_z = col_swap(w_z, 2), row_swap(w_x, 1), row_swap(w_y, 2)
    tables = [jnp.asarray(table) for table in solve_tables()]
    blocks = [own, w, z, y, x]
    *waves, sum0, sum1 = near_part(row_total, col_total, 0, [*blocks, mate, *tables])
    sum0, sum1, over_x, over_y, over_z = in_order(sum0, sum1, over_x, over_y, over_z)
    last = (
        col_swap(over_z, 2),
        row_swap(over_x[:1], 1),
        row_swap(over_y[:1], 2),
        corner_swap(over_x[:1]),
    )
    for part, arrived in enumerate(((over_x, over_y, over_z), last), 1):
        blocks += arrived
        operands = [*blocks, mate, *tables, *waves, sum0, sum1]
        sum0, sum1 = near_part(row_total, col_total, part, operands)
    return finish(flatten(sum0), col_swap(sum1, 1))


def far_shards(row_total, col_total, orbitals, pair_list, pair_count):
    counts = count_pairs(pair_list, pair_count, row_total, col_total)
    own = pack_band(orbitals)
    axes = ("row", "col")
    table = lax.all_gather(counts.reshape(-1), axes)
    table = table.reshape(row_total, col_total, col_total, row_total)
    wide = col_total // 2
    column = lax.all_gather(own[0], "row")
    columns = [column] + [swap(column, "col", col_total, 2 * x) for x in range(1, wide)]
    bands = jnp.concatenate(columns, axis=0)
    row = lax.axis_index("row")
    col = lax.axis_index("col")
    mine = jnp.stack([col, col ^ 1])
    other_col = ((col // 2) ^ lax.iota(jnp.int32, wide)) * 2 + col % 2
    other_row = lax.iota(jnp.int32, row_total)
    direct = table[row][other_col][:, mine]
    direct = jnp.transpose(direct, (1, 2, 0))
    mirror = table[:, :, :, row][:, mine][:, :, other_col]
    mirror = jnp.transpose(mirror, (1, 0, 2))
    same = (mine[:, None, None] == other_col[None, None, :]) & (other_row == row)[None, :, None]
    weights = (direct + jnp.where(same, 0.0, mirror)).astype(jnp.int32).reshape(-1)
    index = lax.iota(jnp.int32, weights.shape[0])
    order = jnp.argsort(jnp.where(weights > 0, 0, 1), stable=True)
    pad = lambda values: jnp.pad(values.astype(jnp.int32), (0, SIDE))
    slots = row_total * wide
    slot = order % slots
    band = (slot % wide) * row_total + slot // wide
    total = jnp.sum((weights > 0).astype(jnp.int32)).reshape(1)
    fields = pl.pallas_call(
        far_kernel,
        out_shape=[wide_of(ROWS), wide_of(FLAT)],
        in_specs=[SMEM_SPEC] * 4 + [ANY_SPEC] + [VMEM_SPEC] * 9,
        out_specs=[VMEM_SPEC] * 2,
        scratch_shapes=[pltpu.VMEM((PACK, LANES), BF16)]
        + [pltpu.VMEM((rows, LANES), F32) for rows in (ROWS, ROWS, ROWS, PITCHED)]
        + solve_scratch(),
        compiler_params=PARAMS,
        name="solve_pairs",
    )(
        total,
        pad(band),
        pad(order // slots),
        pad(weights[order]),
        bands,
        own,
        swap(own, "col", col_total, 1),
        *map(jnp.asarray, solve_tables()),
    )
    return finish(flatten(fields[0]), swap(fields[1], "col", col_total, 1))


def solution(mesh):
    row_total, col_total = mesh.shape["row"], mesh.shape["col"]
    near = (row_total, col_total) == NEAR
    shards = near_shards if near else far_shards
    return jax.shard_map(
        functools.partial(shards, row_total, col_total),
        mesh=mesh,
        in_specs=(P(("row", "col"), None), P(("row", "col"), None, None), P(("row", "col"))),
        out_specs=P(("row", "col"), None),
        check_vma=False,
    )
```

```python
import functools
import itertools

import jax
import jax.numpy as jnp
import ml_dtypes
import numpy as np
from jax import lax
from jax.experimental import pallas as pl
from jax.experimental.pallas import tpu as pltpu
from jax.sharding import PartitionSpec as P

GX = 40
LANES = 128
SIDE = 3
THIRD = GX // SIDE
PART = THIRD * GX
PACK = -(-PART // 16) * 16
LIVE = GX * GX
SPARE = SIDE * GX
LAST = LANES - SPARE
LAST_PARTS = GX // LAST
TABLE = 208
FLAT = LIVE * GX // LANES
CHUNK = PACK // 16
FLAT_ROWS = 512
PITCHED = LIVE // 16 * 17
DUO = 2 * GX
QUAD = 4 * GX
PITCH = GX + 1
VMEM_LIMIT = 16 * 1024 * 1024
screen_width = 0.9
F32 = jnp.float32
BF16 = jnp.bfloat16


def real_basis():
    half = GX // 2
    point = np.arange(GX)
    rows = [np.cos(2 * np.pi * (k * point % GX) / GX) for k in range(half + 1)]
    rows += [np.sin(2 * np.pi * (k * point % GX) / GX) for k in range(1, half)]
    frequency = np.concatenate([np.arange(half + 1), np.arange(1, half)])
    norm = np.where((frequency == 0) | (frequency == half), 1.0, 2.0) / GX
    return np.stack(rows), frequency, norm


def halves(table):
    high = table.astype(ml_dtypes.bfloat16)
    low = (table - high.astype(np.float64)).astype(ml_dtypes.bfloat16)
    return high, low


def left_table(table):
    high, low = halves(np.kron(np.eye(2), table))
    return np.concatenate([high, low, high], axis=1)


def right_table(table):
    wide = np.zeros((LANES, LANES))
    for p in range(SIDE):
        wide[p * GX : (p + 1) * GX, p * GX : (p + 1) * GX] = table
    high, low = halves(wide)
    both = np.concatenate([high, low], axis=1)
    return np.concatenate([both, both], axis=0)


def kernel_table():
    _, frequency, norm = real_basis()
    wave = frequency * (2.0 * np.pi / GX)
    squared = wave * wave
    total = squared[:, None, None] + squared[None, :, None] + squared[None, None, :]
    safe = np.where(total > 0, total, 1.0)
    screened = 4.0 * np.pi * (1.0 - np.exp(-safe / (4.0 * screen_width**2))) / safe
    kernel = np.where(total > 0, screened, np.pi / screen_width**2)
    kernel = kernel * norm[:, None, None] * norm[None, :, None] * norm[None, None, :]
    rows = np.swapaxes(kernel, 0, 1).reshape(LIVE, GX)
    out = np.zeros((LIVE, LANES), np.float32)
    for p in range(SIDE):
        out[:, p * GX : (p + 1) * GX] = rows
    return out


def dot(a, b):
    return jnp.dot(a, b, preferred_element_type=F32)


def split(values):
    high = values.astype(BF16)
    return high, (values - high.astype(F32)).astype(BF16)


def contract_rows(table, values):
    high, low = split(values)
    return dot(table, jnp.concatenate([high, high, low], axis=0))


def contract_lanes(values, table):
    both = dot(jnp.concatenate(split(values), axis=1), table)
    return both[:, :LANES] + both[:, LANES:]


def fold(values):
    return jnp.concatenate([values[:DUO], values[DUO:]], axis=1)


def unfold(values):
    return jnp.concatenate([values[:, :LANES], values[:, LANES:]], axis=0)


def quad(step):
    return pl.ds(step * QUAD, QUAD)


def joined(planes):
    left = jnp.concatenate(planes[:2], axis=0)
    return jnp.concatenate([left, jnp.concatenate(planes[2:], axis=0)], axis=1)


def parted(values):
    return [
        values[i % 2 * GX : i % 2 * GX + GX, i // 2 * LANES : (i // 2 + 1) * LANES] for i in range(4)
    ]


def load_planes(ref, step):
    return joined([ref[pl.ds(step * 4 + i, GX, stride=PITCH), :] for i in range(4)])


def store_planes(ref, step, values):
    for i, plane in enumerate(parted(values)):
        ref[pl.ds(step * 4 + i, GX, stride=PITCH), :] = plane


def load_x_planes(ref, step):
    return joined([ref[pl.ds((step * 4 + i) * PITCH, GX), :] for i in range(4)])


def store_x_planes(ref, step, values):
    for i, plane in enumerate(parted(values)):
        ref[pl.ds((step * 4 + i) * PITCH, GX), :] = plane


def count_vector(pairs, live):
    slots = pairs.shape[1]
    row = lax.broadcasted_iota(jnp.int32, (16, slots), 0)
    lane = lax.broadcasted_iota(jnp.int32, (LANES, slots), 0) - SPARE
    first = (pairs[0:1] == row) & (lax.broadcasted_iota(jnp.int32, (16, slots), 1) < live)
    second = jnp.where(pairs[1:2] == lane, 1.0, 0.0)
    contract = (((1,), (1,)), ((), ()))
    return lax.dot_general(jnp.where(first, 1.0, 0.0), second, contract, preferred_element_type=F32)


def unroll_rows(copy):
    for k in range(FLAT):
        copy(k, slice(k * LANES, (k + 1) * LANES))


def pack_kernel(band_ref, out_ref, flat_ref, wide_ref, last_ref):
    def to_rows(k, lanes):
        flat_ref[k : k + 1, :] = band_ref[0:1, lanes].astype(F32)

    unroll_rows(to_rows)
    unused = FLAT_ROWS - FLAT
    flat_ref[FLAT:FLAT_ROWS, :] = jnp.zeros((unused, LANES), F32)
    lane = lax.broadcasted_iota(jnp.int32, (1, LANES), 1)

    def rows_of(first, count, target):
        group, q = divmod(first, 16)
        row, offset = divmod(q * GX, LANES)
        start = group * 5 + row
        values = flat_ref[pl.ds(start, count, stride=5), :]
        if offset + GX > LANES:
            after = flat_ref[pl.ds(start + 1, count, stride=5), :]
            values = jnp.where(lane >= offset, values, after)
        shift = (target - offset) % LANES
        return pltpu.roll(values, shift, 1) if shift else values

    for q in range(16):
        packed = jnp.zeros((CHUNK, LANES), F32)
        for third in range(SIDE):
            values = rows_of(third * PART + q, CHUNK, third * GX)
            packed = jnp.where(lane // GX == third, values, packed)
        wide_ref[pl.ds(q, CHUNK, stride=16), :] = packed
        last_ref[pl.ds(q, 3, stride=16), :] = rows_of(SIDE * PART + q, 3, 0)
    for part in range(LAST_PARTS):
        rows = slice(part * GX, (part + 1) * GX)
        values = pltpu.roll(last_ref[0:GX, :], SPARE - part * LAST, 1)
        wide_ref[rows, :] = jnp.where(lane >= SPARE, values, wide_ref[rows, :])
    out_ref[0] = wide_ref[...].astype(BF16)


def list_kernel(pairs_ref, live_ref, out_ref):
    out_ref[...] = count_vector(pairs_ref[0], live_ref[...])


def count_kernel(col_total, packed_ref, own_ref, mate_ref, out_ref):
    out_ref[...] = packed_ref[...]
    counts = own_ref[...] + pltpu.roll(mate_ref[...], col_total, 0)
    rows = slice(TABLE, TABLE + 16)
    out_ref[0, rows, :] = (packed_ref[0, rows, :].astype(F32) + counts).astype(BF16)


def spread(load, out_ref):
    lane = lax.broadcasted_iota(jnp.int32, (1, LANES), 1)
    for start in range(0, PACK, DUO):
        count = min(DUO, PACK - start)
        bands = [load(p, slice(start, start + count)).astype(F32) for p in range(SIDE)]
        count = min(count, PART - start)
        for third in range(SIDE):
            wide = jnp.zeros((count, LANES), F32)
            for p, values in enumerate(bands):
                shift = (p - third) * GX % LANES
                values = values[:count]
                values = pltpu.roll(values, shift, 1) if shift else values
                wide = jnp.where(lane // GX == p, values, wide)
            out_ref[third * PART + start : third * PART + start + count, :] = wide
    wide = jnp.zeros((GX, LANES), F32)
    for p in range(SIDE):
        band = load(p, slice(0, TABLE)).astype(F32)
        for part in range(LAST_PARTS):
            lanes = p * GX + part * LAST
            values = pltpu.roll(band[part * GX : (part + 1) * GX], (lanes - SPARE) % LANES, 1)
            wide = jnp.where((lane >= lanes) & (lane < lanes + LAST), values, wide)
    out_ref[SIDE * PART : LIVE, :] = wide


def spread_waves(band_refs, wave_refs):
    for (ref, at), wave_ref in zip(band_refs, wave_refs):
        spread(lambda p, rows: ref[at, rows, :], wave_ref)


def clear(sum_refs):
    for sum_ref in sum_refs:
        sum_ref[...] = jnp.zeros_like(sum_ref)


def lane_side():
    return lax.broadcasted_iota(jnp.int32, (1, LANES), 1) // GX


def solve_trios(first, count, lists, load_band, tables, wave_refs, sum_refs, scratch):
    z_ref, z_back_ref, row_ref, row_back_ref, kernel_ref = tables
    trio_ref, partner_ref, work_ref, work2_ref = scratch
    slot_list, band_list, weight_list = lists
    side = lane_side()

    def by_side(values):
        row = jnp.zeros((1, LANES), F32)
        for p in range(SIDE):
            row = jnp.where(side == p, values[p].astype(F32), row)
        return row

    def trio(at, carry):
        places = [first + at * SIDE + p for p in range(SIDE)]
        for p, place in enumerate(places):
            load_band(slot_list[place], trio_ref, p)
        bands = [band_list[place] for place in places]
        weights = [weight_list[place] for place in places]
        is_mate = by_side(bands) > 0.5
        scales = [
            by_side([jnp.where(bands[p] == which, weights[p], 0) for p in range(SIDE)])
            for which in range(2)
        ]
        spread(lambda p, rows: trio_ref[p, rows, :], partner_ref)

        steps = range(GX // 4)

        def forward():
            values = []
            for step in steps:
                wave = jnp.where(is_mate, wave_refs[1][quad(step), :], wave_refs[0][quad(step), :])
                values.append(partner_ref[quad(step), :] * wave)
            values = [contract_lanes(v, z_ref[...]) for v in values]
            values = [contract_rows(row_ref[...], fold(v)) for v in values]
            for step, v in zip(steps, values):
                store_x_planes(work_ref, step, v)

        def across():
            values = [load_planes(work_ref, step) for step in steps]
            values = [contract_rows(row_ref[...], v) for v in values]
            values = [v * fold(kernel_ref[quad(step), :]) for step, v in zip(steps, values)]
            values = [contract_rows(row_back_ref[...], v) for v in values]
            for step, v in zip(steps, values):
                store_planes(work2_ref, step, v)

        def back():
            values = [load_x_planes(work2_ref, step) for step in steps]
            values = [unfold(contract_rows(row_back_ref[...], v)) for v in values]
            values = [contract_lanes(v, z_back_ref[...]) for v in values]
            for step, v in zip(steps, values):
                v = v * partner_ref[quad(step), :]
                for sum_ref, scale in zip(sum_refs, scales):
                    sum_ref[quad(step), :] = sum_ref[quad(step), :] + v * scale

        for phase in (forward, across, back):
            phase()
        return carry

    lax.fori_loop(0, count, trio, 0)


def flat_field(sum_ref, out_ref, pitched_ref):
    lane = lax.broadcasted_iota(jnp.int32, (1, LANES), 1)
    rows = LIVE // 16
    for group in range(rows):
        pitched_ref[group * 17 : group * 17 + 16, :] = sum_ref[group * 16 : group * 16 + 16, :]
    flat = [jnp.zeros((rows, LANES), F32)] * 5
    for q in range(16):
        row, offset = divmod(q * GX, LANES)
        values = pitched_ref[pl.ds(q, rows, stride=17), :]
        moved = jnp.zeros((rows, LANES), F32)
        for p in range(SIDE):
            shift = (offset - p * GX) % LANES
            moved = moved + (pltpu.roll(values, shift, 1) if shift else values)
        flat[row] = jnp.where(lane >= offset, moved, flat[row])
        if offset + GX > LANES:
            flat[row + 1] = jnp.where(lane < offset + GX - LANES, moved, flat[row + 1])
    for row in range(5):
        out_ref[pl.ds(row, rows, stride=5), :] = flat[row]


def near_kernel(row_total, col_total, part, *refs):
    stages = STAGES[: part + 1]
    blocks = [block for stage in stages for block in stage]
    band_refs, refs = refs[: len(blocks)], refs[len(blocks) :]
    bands = [(ref, at) for ref, block in zip(band_refs, blocks) for at in range(len(block))]
    flips = [flip for block in blocks for flip in block]
    mate_ref, tables, refs = refs[0], refs[1:6], refs[6:]
    if part:
        wave_refs, given_refs, out_refs, refs = refs[:2], refs[2:4], refs[4:6], refs[6:]
    else:
        wave_refs, out_refs, refs = refs[:2], refs[2:4], refs[4:]
    (count_vmem, count_smem, slot_list, band_list, weight_list), refs = refs[:5], refs[5:]
    scratch, sem = refs[:4], refs[4]
    sum_refs = (out_refs[0], refs[5]) if part == 2 else out_refs

    lane = lax.broadcasted_iota(jnp.int32, (8, LANES), 1)
    counts = jnp.zeros((8, LANES), F32)
    for s, (ref, at) in enumerate(bands):
        spare = ref[at, TABLE : TABLE + 16, :].astype(F32)[0:8]
        shift = (s * row_total - SPARE) % LANES
        moved = pltpu.roll(spare, shift, 1) if shift else spare
        counts = jnp.where(lane // row_total == s, moved, counts)
    count_vmem[...] = counts.astype(jnp.int32)
    copy = pltpu.make_async_copy(count_vmem, count_smem, sem)
    copy.start()
    if part:
        for sum_ref, given_ref in zip(sum_refs, given_refs):
            sum_ref[...] = given_ref[...]
    else:
        clear(sum_refs)
        spread_waves(((band_refs[0], 0), (mate_ref, 0)), wave_refs)
    copy.wait()
    row = lax.axis_index("row")
    col = lax.axis_index("col")
    total = jnp.int32(0)
    done = jnp.int32(0)
    place = 0
    for step, stage in enumerate(stages):
        here = range(place, place + sum(len(block) for block in stage))
        place = here.stop
        for which, at in itertools.product(range(2), here):
            row_flip, col_flip = flips[at]
            row_place = flips.index((0, col_flip)) * row_total
            col_place = flips.index((row_flip, 0)) * row_total
            weight = count_smem[col ^ which, row_place + (row ^ row_flip)]
            if at or which:
                mirror = which * col_total + (col ^ col_flip)
                weight = weight + count_smem[mirror, col_place + row]
            slot_list[total] = at
            band_list[total] = which
            weight_list[total] = weight
            total = total + jnp.where(weight > 0, 1, 0)
        if step < 2:
            trios = jnp.minimum((total - done) // SIDE, CAPS[step])
            if step < part:
                done = done + trios * SIDE
    if part == 2:
        trios = (total - done + SIDE - 1) // SIDE
        for p in range(SIDE - 1):
            slot_list[total + p] = 0
            band_list[total + p] = 0
            weight_list[total + p] = 0

    def load_band(wanted, target, p):
        for place, (ref, at) in enumerate(bands):

            @pl.when(wanted == place)
            def _():
                target[p] = ref[at]

    lists = (slot_list, band_list, weight_list)
    solve_trios(done, trios, lists, load_band, tables, wave_refs, sum_refs, scratch)
    if part == 2:
        flat_field(sum_refs[1], out_refs[1], refs[6])


def far_kernel(total_ref, slot_list, band_list, weight_list, bands_ref, own_ref, mate_ref, *refs):
    tables, out_refs, refs = refs[:5], refs[5:7], refs[7:]
    buffer, wave_refs, sum_refs = refs[0], refs[1:3], (out_refs[0], refs[3])
    pitched_ref, scratch = refs[4], refs[5:]
    spread_waves(((own_ref, 0), (mate_ref, 0)), wave_refs)
    clear(sum_refs)

    def load_band(place, target, p):
        pltpu.sync_copy(bands_ref.at[place], buffer)
        target[p] = buffer[...]

    lists = (slot_list, band_list, weight_list)
    trios = (total_ref[0] + SIDE - 1) // SIDE
    solve_trios(0, trios, lists, load_band, tables, wave_refs, sum_refs, scratch)
    flat_field(sum_refs[1], out_refs[1], pitched_ref)


def flat_kernel(sum_ref, out_ref, pitched_ref):
    flat_field(sum_ref, out_ref, pitched_ref)


def finish_kernel(own_ref, part_ref, out_ref):
    def to_lanes(k, lanes):
        out_ref[0:1, lanes] = own_ref[k : k + 1, :] + part_ref[k : k + 1, :]

    unroll_rows(to_lanes)


VMEM_SPEC = pl.BlockSpec(memory_space=pltpu.VMEM)
SMEM_SPEC = pl.BlockSpec(memory_space=pltpu.SMEM)
ANY_SPEC = pl.BlockSpec(memory_space=pl.ANY)
PARAMS = pltpu.CompilerParams(vmem_limit_bytes=VMEM_LIMIT)


def solve_tables():
    basis, _, _ = real_basis()
    return [
        right_table(basis.T),
        right_table(basis),
        left_table(basis),
        left_table(basis.T),
        kernel_table(),
    ]


def solve_scratch():
    wide = [pltpu.VMEM((rows, LANES), F32) for rows in (LIVE, GX * PITCH, GX * PITCH)]
    return [pltpu.VMEM((SIDE, PACK, LANES), BF16)] + wide


def wide_of(rows):
    return jax.ShapeDtypeStruct((rows, LANES), F32)


def swap(values, axis, size, flip):
    return lax.ppermute(values, axis, [(i, i ^ flip) for i in range(size)])


def count_pairs(pair_list, pair_count, row_total, col_total):
    slots = pair_list.shape[1]
    live = lax.iota(jnp.int32, slots) < pair_count[0]
    first = pair_list[0, :, 0][:, None, None] == lax.iota(jnp.int32, col_total)[None, :, None]
    second = pair_list[0, :, 1][:, None, None] == lax.iota(jnp.int32, row_total)[None, None, :]
    return jnp.sum((first & second & live[:, None, None]).astype(F32), axis=0)


def pack_band(orbitals):
    return pl.pallas_call(
        pack_kernel,
        out_shape=jax.ShapeDtypeStruct((1, PACK, LANES), BF16),
        in_specs=[VMEM_SPEC],
        out_specs=VMEM_SPEC,
        scratch_shapes=[pltpu.VMEM((rows, LANES), F32) for rows in (FLAT_ROWS, PACK, 48)],
        compiler_params=PARAMS,
        name="pack_band",
    )(orbitals)


def list_counts(pair_list, pair_count):
    return pl.pallas_call(
        list_kernel,
        out_shape=jax.ShapeDtypeStruct((16, LANES), F32),
        in_specs=[VMEM_SPEC] * 2,
        out_specs=VMEM_SPEC,
        compiler_params=PARAMS,
        name="list_counts",
    )(jnp.swapaxes(pair_list, 1, 2), pair_count.reshape(1, 1))


def add_counts(packed, col_total, counts, mate_counts):
    return pl.pallas_call(
        functools.partial(count_kernel, col_total),
        out_shape=jax.ShapeDtypeStruct(packed.shape, BF16),
        in_specs=[VMEM_SPEC] * 3,
        out_specs=VMEM_SPEC,
        compiler_params=PARAMS,
        name="add_counts",
    )(packed, counts, mate_counts)


def flatten(sums):
    return pl.pallas_call(
        flat_kernel,
        out_shape=wide_of(FLAT),
        in_specs=[VMEM_SPEC],
        out_specs=VMEM_SPEC,
        scratch_shapes=[pltpu.VMEM((PITCHED, LANES), F32)],
        compiler_params=PARAMS,
        name="flatten",
    )(sums)


def finish(own, part):
    return pl.pallas_call(
        finish_kernel,
        out_shape=jax.ShapeDtypeStruct((1, LIVE * GX), F32),
        in_specs=[VMEM_SPEC] * 2,
        out_specs=VMEM_SPEC,
        compiler_params=PARAMS,
        name="add_parts",
    )(own, part)


NEAR = (8, 4)
STAGES = (
    (((0, 0),), ((4, 0),), ((2, 0),), ((1, 0),), ((0, 2),)),
    (((4, 2), (2, 2)), ((5, 0), (1, 2)), ((6, 0), (3, 0))),
    (((6, 2), (3, 2)), ((5, 2),), ((7, 0),), ((7, 2),)),
)
CAPS = (2, 2)


def near_part(row_total, col_total, part, operands):
    places = 2 * row_total * (col_total // 2) + SIDE
    out_shape = [wide_of(LIVE)] * 2
    if part == 0:
        out_shape = out_shape * 2
    if part == 2:
        out_shape = [wide_of(LIVE), wide_of(FLAT)]
    operands = list(operands)
    cost = pl.CostEstimate(flops=4 * 10**9, bytes_accessed=2 * 10**7, transcendentals=0)
    return pl.pallas_call(
        functools.partial(near_kernel, row_total, col_total, part),
        out_shape=out_shape,
        in_specs=[VMEM_SPEC] * len(operands),
        out_specs=[VMEM_SPEC] * len(out_shape),
        scratch_shapes=[
            pltpu.VMEM((8, LANES), jnp.int32),
            pltpu.SMEM((8, LANES), jnp.int32),
            pltpu.SMEM((places,), jnp.int32),
            pltpu.SMEM((places,), jnp.int32),
            pltpu.SMEM((places,), jnp.int32),
        ]
        + solve_scratch()
        + [pltpu.SemaphoreType.DMA]
        + ([pltpu.VMEM((rows, LANES), F32) for rows in (LIVE, PITCHED)] if part == 2 else []),
        compiler_params=PARAMS,
        cost_estimate=cost,
        name="solve_part",
    )(*operands)


def near_shards(row_total, col_total, orbitals, pair_list, pair_count):
    row_swap = lambda values, flip: swap(values, "row", row_total, flip)
    col_swap = lambda values, flip: swap(values, "col", col_total, flip)
    both = lambda a, b: jnp.concatenate([a, b], axis=0)

    def corner_swap(values):
        places = list(itertools.product(range(row_total), range(col_total)))
        at = lambda row, col: row * col_total + col
        pairs = [(at(row, col), at(row ^ 3, col)) for row, col in places]
        return lax.ppermute(values, ("row", "col"), pairs)

    counts = list_counts(pair_list, pair_count)
    own = add_counts(pack_band(orbitals), col_total, counts, col_swap(counts, 1))
    in_order = lambda *values: lax.optimization_barrier(values)
    mate, x, y, z, w = in_order(
        col_swap(own, 1), col_swap(own, 2), row_swap(own, 1), row_swap(own, 2), row_swap(own, 4)
    )
    w_z, w_x, w_y = in_order(both(w, z), both(w, x), both(w, y))
    over_x, over_y, over_z = col_swap(w_z, 2), row_swap(w_x, 1), row_swap(w_y, 2)
    tables = [jnp.asarray(table) for table in solve_tables()]
    blocks = [own, w, z, y, x]
    *waves, sum0, sum1 = near_part(row_total, col_total, 0, [*blocks, mate, *tables])
    sum0, sum1, over_x, over_y, over_z = in_order(sum0, sum1, over_x, over_y, over_z)
    last = (
        col_swap(over_z, 2),
        row_swap(over_x[:1], 1),
        row_swap(over_y[:1], 2),
        corner_swap(over_x[:1]),
    )
    for part, arrived in enumerate(((over_x, over_y, over_z), last), 1):
        blocks += arrived
        operands = [*blocks, mate, *tables, *waves, sum0, sum1]
        sum0, sum1 = near_part(row_total, col_total, part, operands)
    return finish(flatten(sum0), col_swap(sum1, 1))


def far_shards(row_total, col_total, orbitals, pair_list, pair_count):
    counts = count_pairs(pair_list, pair_count, row_total, col_total)
    own = pack_band(orbitals)
    axes = ("row", "col")
    table = lax.all_gather(counts.reshape(-1), axes)
    table = table.reshape(row_total, col_total, col_total, row_total)
    wide = col_total // 2
    column = lax.all_gather(own[0], "row")
    columns = [column] + [swap(column, "col", col_total, 2 * x) for x in range(1, wide)]
    bands = jnp.concatenate(columns, axis=0)
    row = lax.axis_index("row")
    col = lax.axis_index("col")
    mine = jnp.stack([col, col ^ 1])
    other_col = ((col // 2) ^ lax.iota(jnp.int32, wide)) * 2 + col % 2
    other_row = lax.iota(jnp.int32, row_total)
    direct = table[row][other_col][:, mine]
    direct = jnp.transpose(direct, (1, 2, 0))
    mirror = table[:, :, :, row][:, mine][:, :, other_col]
    mirror = jnp.transpose(mirror, (1, 0, 2))
    same = (mine[:, None, None] == other_col[None, None, :]) & (other_row == row)[None, :, None]
    weights = (direct + jnp.where(same, 0.0, mirror)).astype(jnp.int32).reshape(-1)
    index = lax.iota(jnp.int32, weights.shape[0])
    order = jnp.argsort(jnp.where(weights > 0, 0, 1), stable=True)
    pad = lambda values: jnp.pad(values.astype(jnp.int32), (0, SIDE))
    slots = row_total * wide
    slot = order % slots
    band = (slot % wide) * row_total + slot // wide
    total = jnp.sum((weights > 0).astype(jnp.int32)).reshape(1)
    fields = pl.pallas_call(
        far_kernel,
        out_shape=[wide_of(LIVE), wide_of(FLAT)],
        in_specs=[SMEM_SPEC] * 4 + [ANY_SPEC] + [VMEM_SPEC] * 7,
        out_specs=[VMEM_SPEC] * 2,
        scratch_shapes=[pltpu.VMEM((PACK, LANES), BF16)]
        + [pltpu.VMEM((rows, LANES), F32) for rows in (LIVE, LIVE, LIVE, PITCHED)]
        + solve_scratch(),
        compiler_params=PARAMS,
        name="solve_pairs",
    )(
        total,
        pad(band),
        pad(order // slots),
        pad(weights[order]),
        bands,
        own,
        swap(own, "col", col_total, 1),
        *map(jnp.asarray, solve_tables()),
    )
    return finish(flatten(fields[0]), swap(fields[1], "col", col_total, 1))


def solution(mesh):
    row_total, col_total = mesh.shape["row"], mesh.shape["col"]
    near = (row_total, col_total) == NEAR
    shards = near_shards if near else far_shards
    return jax.shard_map(
        functools.partial(shards, row_total, col_total),
        mesh=mesh,
        in_specs=(P(("row", "col"), None), P(("row", "col"), None, None), P(("row", "col"))),
        out_specs=P(("row", "col"), None),
        check_vma=False,
    )
```

```python
import functools
import itertools

import jax
import jax.numpy as jnp
import ml_dtypes
import numpy as np
from jax import lax
from jax.experimental import pallas as pl
from jax.experimental.pallas import tpu as pltpu
from jax.sharding import PartitionSpec as P

GX = 40
LANES = 128
SIDE = 3
THIRD = GX // SIDE
PART = THIRD * GX
PACK = -(-PART // 16) * 16
LIVE = GX * GX
SPARE = SIDE * GX
LAST = LANES - SPARE
LAST_PARTS = GX // LAST
TABLE = 208
FLAT = LIVE * GX // LANES
CHUNK = PACK // 16
FLAT_ROWS = 512
PITCHED = LIVE // 16 * 17
DUO = 2 * GX
QUAD = 4 * GX
PITCH = GX + 1
VMEM_LIMIT = 16 * 1024 * 1024
screen_width = 0.9
F32 = jnp.float32
BF16 = jnp.bfloat16


def real_basis():
    half = GX // 2
    point = np.arange(GX)
    rows = [np.cos(2 * np.pi * (k * point % GX) / GX) for k in range(half + 1)]
    rows += [np.sin(2 * np.pi * (k * point % GX) / GX) for k in range(1, half)]
    frequency = np.concatenate([np.arange(half + 1), np.arange(1, half)])
    norm = np.where((frequency == 0) | (frequency == half), 1.0, 2.0) / GX
    return np.stack(rows), frequency, norm


def halves(table):
    high = table.astype(ml_dtypes.bfloat16)
    low = (table - high.astype(np.float64)).astype(ml_dtypes.bfloat16)
    return high, low


def left_table(table):
    high, low = halves(np.kron(np.eye(2), table))
    return np.concatenate([high, low, high], axis=1)


def right_table(table):
    wide = np.zeros((LANES, LANES))
    for p in range(SIDE):
        wide[p * GX : (p + 1) * GX, p * GX : (p + 1) * GX] = table
    high, low = halves(wide)
    both = np.concatenate([high, low], axis=1)
    return np.concatenate([both, both], axis=0)


def kernel_table():
    _, frequency, norm = real_basis()
    wave = frequency * (2.0 * np.pi / GX)
    squared = wave * wave
    total = squared[:, None, None] + squared[None, :, None] + squared[None, None, :]
    safe = np.where(total > 0, total, 1.0)
    screened = 4.0 * np.pi * (1.0 - np.exp(-safe / (4.0 * screen_width**2))) / safe
    kernel = np.where(total > 0, screened, np.pi / screen_width**2)
    kernel = kernel * norm[:, None, None] * norm[None, :, None] * norm[None, None, :]
    rows = np.swapaxes(kernel, 0, 1).reshape(LIVE, GX)
    out = np.zeros((LIVE, LANES), np.float32)
    for p in range(SIDE):
        out[:, p * GX : (p + 1) * GX] = rows
    return out


def dot(a, b):
    return jnp.dot(a, b, preferred_element_type=F32)


def split(values):
    high = values.astype(BF16)
    return high, (values - high.astype(F32)).astype(BF16)


def contract_rows(table, values):
    high, low = split(values)
    return dot(table, jnp.concatenate([high, high, low], axis=0))


def contract_lanes(values, table):
    both = dot(jnp.concatenate(split(values), axis=1), table)
    return both[:, :LANES] + both[:, LANES:]


def fold(values):
    return jnp.concatenate([values[:DUO], values[DUO:]], axis=1)


def unfold(values):
    return jnp.concatenate([values[:, :LANES], values[:, LANES:]], axis=0)


def quad(step):
    return pl.ds(step * QUAD, QUAD)


def joined(planes):
    left = jnp.concatenate(planes[:2], axis=0)
    return jnp.concatenate([left, jnp.concatenate(planes[2:], axis=0)], axis=1)


def parted(values):
    return [
        values[i % 2 * GX : i % 2 * GX + GX, i // 2 * LANES : (i // 2 + 1) * LANES] for i in range(4)
    ]


def load_planes(ref, step):
    return joined([ref[pl.ds(step * 4 + i, GX, stride=PITCH), :] for i in range(4)])


def store_planes(ref, step, values):
    for i, plane in enumerate(parted(values)):
        ref[pl.ds(step * 4 + i, GX, stride=PITCH), :] = plane


def load_x_planes(ref, step):
    return joined([ref[pl.ds((step * 4 + i) * PITCH, GX), :] for i in range(4)])


def store_x_planes(ref, step, values):
    for i, plane in enumerate(parted(values)):
        ref[pl.ds((step * 4 + i) * PITCH, GX), :] = plane


def count_vector(pairs, live):
    slots = pairs.shape[1]
    row = lax.broadcasted_iota(jnp.int32, (16, slots), 0)
    lane = lax.broadcasted_iota(jnp.int32, (LANES, slots), 0) - SPARE
    first = (pairs[0:1] == row) & (lax.broadcasted_iota(jnp.int32, (16, slots), 1) < live)
    second = jnp.where(pairs[1:2] == lane, 1.0, 0.0)
    contract = (((1,), (1,)), ((), ()))
    return lax.dot_general(jnp.where(first, 1.0, 0.0), second, contract, preferred_element_type=F32)


def unroll_rows(copy):
    for k in range(FLAT):
        copy(k, slice(k * LANES, (k + 1) * LANES))


def pack_kernel(band_ref, out_ref, flat_ref, wide_ref, last_ref):
    def to_rows(k, lanes):
        flat_ref[k : k + 1, :] = band_ref[0:1, lanes].astype(F32)

    unroll_rows(to_rows)
    unused = FLAT_ROWS - FLAT
    flat_ref[FLAT:FLAT_ROWS, :] = jnp.zeros((unused, LANES), F32)
    lane = lax.broadcasted_iota(jnp.int32, (1, LANES), 1)

    def rows_of(first, count, target):
        group, q = divmod(first, 16)
        row, offset = divmod(q * GX, LANES)
        start = group * 5 + row
        values = flat_ref[pl.ds(start, count, stride=5), :]
        if offset + GX > LANES:
            after = flat_ref[pl.ds(start + 1, count, stride=5), :]
            values = jnp.where(lane >= offset, values, after)
        shift = (target - offset) % LANES
        return pltpu.roll(values, shift, 1) if shift else values

    for q in range(16):
        packed = jnp.zeros((CHUNK, LANES), F32)
        for third in range(SIDE):
            values = rows_of(third * PART + q, CHUNK, third * GX)
            packed = jnp.where(lane // GX == third, values, packed)
        wide_ref[pl.ds(q, CHUNK, stride=16), :] = packed
        last_ref[pl.ds(q, 3, stride=16), :] = rows_of(SIDE * PART + q, 3, 0)
    for part in range(LAST_PARTS):
        rows = slice(part * GX, (part + 1) * GX)
        values = pltpu.roll(last_ref[0:GX, :], SPARE - part * LAST, 1)
        wide_ref[rows, :] = jnp.where(lane >= SPARE, values, wide_ref[rows, :])
    out_ref[0] = wide_ref[...].astype(BF16)


def list_kernel(pairs_ref, live_ref, out_ref):
    out_ref[...] = count_vector(pairs_ref[0], live_ref[...])


def count_kernel(col_total, packed_ref, own_ref, mate_ref, out_ref):
    out_ref[...] = packed_ref[...]
    counts = own_ref[...] + pltpu.roll(mate_ref[...], col_total, 0)
    rows = slice(TABLE, TABLE + 16)
    out_ref[0, rows, :] = (packed_ref[0, rows, :].astype(F32) + counts).astype(BF16)


def spread(load, out_ref):
    lane = lax.broadcasted_iota(jnp.int32, (1, LANES), 1)
    for start in range(0, PACK, DUO):
        count = min(DUO, PACK - start)
        bands = [load(p, slice(start, start + count)).astype(F32) for p in range(SIDE)]
        count = min(count, PART - start)
        for third in range(SIDE):
            wide = jnp.zeros((count, LANES), F32)
            for p, values in enumerate(bands):
                shift = (p - third) * GX % LANES
                values = values[:count]
                values = pltpu.roll(values, shift, 1) if shift else values
                wide = jnp.where(lane // GX == p, values, wide)
            out_ref[third * PART + start : third * PART + start + count, :] = wide
    wide = jnp.zeros((GX, LANES), F32)
    for p in range(SIDE):
        band = load(p, slice(0, TABLE)).astype(F32)
        for part in range(LAST_PARTS):
            lanes = p * GX + part * LAST
            values = pltpu.roll(band[part * GX : (part + 1) * GX], (lanes - SPARE) % LANES, 1)
            wide = jnp.where((lane >= lanes) & (lane < lanes + LAST), values, wide)
    out_ref[SIDE * PART : LIVE, :] = wide


def spread_waves(band_refs, wave_refs):
    for (ref, at), wave_ref in zip(band_refs, wave_refs):
        spread(lambda p, rows: ref[at, rows, :], wave_ref)


def clear(sum_refs):
    for sum_ref in sum_refs:
        sum_ref[...] = jnp.zeros_like(sum_ref)


def lane_side():
    return lax.broadcasted_iota(jnp.int32, (1, LANES), 1) // GX


def solve_trios(first, count, lists, load_band, tables, wave_refs, sum_refs, scratch):
    z_ref, z_back_ref, row_ref, row_back_ref, kernel_ref = tables
    trio_ref, partner_ref, work_ref, work2_ref = scratch
    slot_list, band_list, weight_list = lists
    side = lane_side()

    def by_side(values):
        row = jnp.zeros((1, LANES), F32)
        for p in range(SIDE):
            row = jnp.where(side == p, values[p].astype(F32), row)
        return row

    def trio(at, carry):
        places = [first + at * SIDE + p for p in range(SIDE)]
        for p, place in enumerate(places):
            load_band(slot_list[place], trio_ref, p)
        bands = [band_list[place] for place in places]
        weights = [weight_list[place] for place in places]
        is_mate = by_side(bands) > 0.5
        scales = [
            by_side([jnp.where(bands[p] == which, weights[p], 0) for p in range(SIDE)])
            for which in range(2)
        ]
        spread(lambda p, rows: trio_ref[p, rows, :], partner_ref)

        steps = range(GX // 4)

        def forward():
            values = []
            for step in steps:
                wave = jnp.where(is_mate, wave_refs[1][quad(step), :], wave_refs[0][quad(step), :])
                values.append(partner_ref[quad(step), :] * wave)
            values = [contract_lanes(v, z_ref[...]) for v in values]
            values = [contract_rows(row_ref[...], fold(v)) for v in values]
            for step, v in zip(steps, values):
                store_x_planes(work_ref, step, v)

        def across():
            values = [load_planes(work_ref, step) for step in steps]
            values = [contract_rows(row_ref[...], v) for v in values]
            values = [v * fold(kernel_ref[quad(step), :]) for step, v in zip(steps, values)]
            values = [contract_rows(row_back_ref[...], v) for v in values]
            for step, v in zip(steps, values):
                store_planes(work2_ref, step, v)

        def back():
            values = [load_x_planes(work2_ref, step) for step in steps]
            values = [unfold(contract_rows(row_back_ref[...], v)) for v in values]
            values = [contract_lanes(v, z_back_ref[...]) for v in values]
            for step, v in zip(steps, values):
                v = v * partner_ref[quad(step), :]
                for sum_ref, scale in zip(sum_refs, scales):
                    sum_ref[quad(step), :] = sum_ref[quad(step), :] + v * scale

        for phase in (forward, across, back):
            phase()
        return carry

    lax.fori_loop(0, count, trio, 0)


def flat_field(sum_ref, out_ref, pitched_ref):
    lane = lax.broadcasted_iota(jnp.int32, (1, LANES), 1)
    rows = LIVE // 16
    for group in range(rows):
        pitched_ref[group * 17 : group * 17 + 16, :] = sum_ref[group * 16 : group * 16 + 16, :]
    flat = [jnp.zeros((rows, LANES), F32)] * 5
    for q in range(16):
        row, offset = divmod(q * GX, LANES)
        values = pitched_ref[pl.ds(q, rows, stride=17), :]
        moved = jnp.zeros((rows, LANES), F32)
        for p in range(SIDE):
            shift = (offset - p * GX) % LANES
            moved = moved + (pltpu.roll(values, shift, 1) if shift else values)
        flat[row] = jnp.where(lane >= offset, moved, flat[row])
        if offset + GX > LANES:
            flat[row + 1] = jnp.where(lane < offset + GX - LANES, moved, flat[row + 1])
    for row in range(5):
        out_ref[pl.ds(row, rows, stride=5), :] = flat[row]


def near_kernel(row_total, col_total, part, *refs):
    stages = STAGES[: part + 1]
    blocks = [block for stage in stages for block in stage]
    band_refs, refs = refs[: len(blocks)], refs[len(blocks) :]
    bands = [(ref, at) for ref, block in zip(band_refs, blocks) for at in range(len(block))]
    flips = [flip for block in blocks for flip in block]
    mate_ref, tables, refs = refs[0], refs[1:6], refs[6:]
    if part:
        wave_refs, given_refs, out_refs, refs = refs[:2], refs[2:4], refs[4:6], refs[6:]
    else:
        wave_refs, out_refs, refs = refs[:2], refs[2:4], refs[4:]
    (count_vmem, count_smem, slot_list, band_list, weight_list), refs = refs[:5], refs[5:]
    scratch, sem = refs[:4], refs[4]
    sum_refs = (out_refs[0], refs[5]) if part == 2 else out_refs

    lane = lax.broadcasted_iota(jnp.int32, (8, LANES), 1)
    counts = jnp.zeros((8, LANES), F32)
    for s, (ref, at) in enumerate(bands):
        spare = ref[at, TABLE : TABLE + 16, :].astype(F32)[0:8]
        shift = (s * row_total - SPARE) % LANES
        moved = pltpu.roll(spare, shift, 1) if shift else spare
        counts = jnp.where(lane // row_total == s, moved, counts)
    count_vmem[...] = counts.astype(jnp.int32)
    copy = pltpu.make_async_copy(count_vmem, count_smem, sem)
    copy.start()
    if part:
        for sum_ref, given_ref in zip(sum_refs, given_refs):
            sum_ref[...] = given_ref[...]
    else:
        clear(sum_refs)
        spread_waves(((band_refs[0], 0), (mate_ref, 0)), wave_refs)
    copy.wait()
    row = lax.axis_index("row")
    col = lax.axis_index("col")
    total = jnp.int32(0)
    done = jnp.int32(0)
    place = 0
    for step, stage in enumerate(stages):
        here = range(place, place + sum(len(block) for block in stage))
        place = here.stop
        for which, at in itertools.product(range(2), here):
            row_flip, col_flip = flips[at]
            row_place = flips.index((0, col_flip)) * row_total
            col_place = flips.index((row_flip, 0)) * row_total
            weight = count_smem[col ^ which, row_place + (row ^ row_flip)]
            if at or which:
                mirror = which * col_total + (col ^ col_flip)
                weight = weight + count_smem[mirror, col_place + row]
            slot_list[total] = at
            band_list[total] = which
            weight_list[total] = weight
            total = total + jnp.where(weight > 0, 1, 0)
        trios = (total - done + SIDE - 1) // SIDE
        if step < 2:
            trios = jnp.minimum(trios, CAPS[step])
        if step < part:
            done = jnp.minimum(done + trios * SIDE, total)
    for p in range(SIDE - 1):
        slot_list[total + p] = 0
        band_list[total + p] = 0
        weight_list[total + p] = 0

    def load_band(wanted, target, p):
        for place, (ref, at) in enumerate(bands):

            @pl.when(wanted == place)
            def _():
                target[p] = ref[at]

    lists = (slot_list, band_list, weight_list)
    solve_trios(done, trios, lists, load_band, tables, wave_refs, sum_refs, scratch)
    if part == 2:
        flat_field(sum_refs[1], out_refs[1], refs[6])


def far_kernel(total_ref, slot_list, band_list, weight_list, bands_ref, own_ref, mate_ref, *refs):
    tables, out_refs, refs = refs[:5], refs[5:7], refs[7:]
    buffer, wave_refs, sum_refs = refs[0], refs[1:3], (out_refs[0], refs[3])
    pitched_ref, scratch = refs[4], refs[5:]
    spread_waves(((own_ref, 0), (mate_ref, 0)), wave_refs)
    clear(sum_refs)

    def load_band(place, target, p):
        pltpu.sync_copy(bands_ref.at[place], buffer)
        target[p] = buffer[...]

    lists = (slot_list, band_list, weight_list)
    trios = (total_ref[0] + SIDE - 1) // SIDE
    solve_trios(0, trios, lists, load_band, tables, wave_refs, sum_refs, scratch)
    flat_field(sum_refs[1], out_refs[1], pitched_ref)


def flat_kernel(sum_ref, out_ref, pitched_ref):
    flat_field(sum_ref, out_ref, pitched_ref)


def finish_kernel(own_ref, part_ref, out_ref):
    def to_lanes(k, lanes):
        out_ref[0:1, lanes] = own_ref[k : k + 1, :] + part_ref[k : k + 1, :]

    unroll_rows(to_lanes)


VMEM_SPEC = pl.BlockSpec(memory_space=pltpu.VMEM)
SMEM_SPEC = pl.BlockSpec(memory_space=pltpu.SMEM)
ANY_SPEC = pl.BlockSpec(memory_space=pl.ANY)
PARAMS = pltpu.CompilerParams(vmem_limit_bytes=VMEM_LIMIT)


def solve_tables():
    basis, _, _ = real_basis()
    return [
        right_table(basis.T),
        right_table(basis),
        left_table(basis),
        left_table(basis.T),
        kernel_table(),
    ]


def solve_scratch():
    wide = [pltpu.VMEM((rows, LANES), F32) for rows in (LIVE, GX * PITCH, GX * PITCH)]
    return [pltpu.VMEM((SIDE, PACK, LANES), BF16)] + wide


def wide_of(rows):
    return jax.ShapeDtypeStruct((rows, LANES), F32)


def swap(values, axis, size, flip):
    return lax.ppermute(values, axis, [(i, i ^ flip) for i in range(size)])


def count_pairs(pair_list, pair_count, row_total, col_total):
    slots = pair_list.shape[1]
    live = lax.iota(jnp.int32, slots) < pair_count[0]
    first = pair_list[0, :, 0][:, None, None] == lax.iota(jnp.int32, col_total)[None, :, None]
    second = pair_list[0, :, 1][:, None, None] == lax.iota(jnp.int32, row_total)[None, None, :]
    return jnp.sum((first & second & live[:, None, None]).astype(F32), axis=0)


def pack_band(orbitals):
    return pl.pallas_call(
        pack_kernel,
        out_shape=jax.ShapeDtypeStruct((1, PACK, LANES), BF16),
        in_specs=[VMEM_SPEC],
        out_specs=VMEM_SPEC,
        scratch_shapes=[pltpu.VMEM((rows, LANES), F32) for rows in (FLAT_ROWS, PACK, 48)],
        compiler_params=PARAMS,
        name="pack_band",
    )(orbitals)


def list_counts(pair_list, pair_count):
    return pl.pallas_call(
        list_kernel,
        out_shape=jax.ShapeDtypeStruct((16, LANES), F32),
        in_specs=[VMEM_SPEC] * 2,
        out_specs=VMEM_SPEC,
        compiler_params=PARAMS,
        name="list_counts",
    )(jnp.swapaxes(pair_list, 1, 2), pair_count.reshape(1, 1))


def add_counts(packed, col_total, counts, mate_counts):
    return pl.pallas_call(
        functools.partial(count_kernel, col_total),
        out_shape=jax.ShapeDtypeStruct(packed.shape, BF16),
        in_specs=[VMEM_SPEC] * 3,
        out_specs=VMEM_SPEC,
        compiler_params=PARAMS,
        name="add_counts",
    )(packed, counts, mate_counts)


def flatten(sums):
    return pl.pallas_call(
        flat_kernel,
        out_shape=wide_of(FLAT),
        in_specs=[VMEM_SPEC],
        out_specs=VMEM_SPEC,
        scratch_shapes=[pltpu.VMEM((PITCHED, LANES), F32)],
        compiler_params=PARAMS,
        name="flatten",
    )(sums)


def finish(own, part):
    return pl.pallas_call(
        finish_kernel,
        out_shape=jax.ShapeDtypeStruct((1, LIVE * GX), F32),
        in_specs=[VMEM_SPEC] * 2,
        out_specs=VMEM_SPEC,
        compiler_params=PARAMS,
        name="add_parts",
    )(own, part)


NEAR = (8, 4)
STAGES = (
    (((0, 0),), ((4, 0),), ((2, 0),), ((1, 0),), ((0, 2),)),
    (((4, 2), (2, 2)), ((5, 0), (1, 2)), ((6, 0), (3, 0))),
    (((6, 2), (3, 2)), ((5, 2),), ((7, 0),), ((7, 2),)),
)
CAPS = (1, 2)


def near_part(row_total, col_total, part, operands):
    places = 2 * row_total * (col_total // 2) + SIDE
    out_shape = [wide_of(LIVE)] * 2
    if part == 0:
        out_shape = out_shape * 2
    if part == 2:
        out_shape = [wide_of(LIVE), wide_of(FLAT)]
    operands = list(operands)
    cost = pl.CostEstimate(flops=4 * 10**9, bytes_accessed=2 * 10**7, transcendentals=0)
    return pl.pallas_call(
        functools.partial(near_kernel, row_total, col_total, part),
        out_shape=out_shape,
        in_specs=[VMEM_SPEC] * len(operands),
        out_specs=[VMEM_SPEC] * len(out_shape),
        scratch_shapes=[
            pltpu.VMEM((8, LANES), jnp.int32),
            pltpu.SMEM((8, LANES), jnp.int32),
            pltpu.SMEM((places,), jnp.int32),
            pltpu.SMEM((places,), jnp.int32),
            pltpu.SMEM((places,), jnp.int32),
        ]
        + solve_scratch()
        + [pltpu.SemaphoreType.DMA]
        + ([pltpu.VMEM((rows, LANES), F32) for rows in (LIVE, PITCHED)] if part == 2 else []),
        compiler_params=PARAMS,
        cost_estimate=cost,
        name="solve_part",
    )(*operands)


def near_shards(row_total, col_total, orbitals, pair_list, pair_count):
    row_swap = lambda values, flip: swap(values, "row", row_total, flip)
    col_swap = lambda values, flip: swap(values, "col", col_total, flip)
    both = lambda a, b: jnp.concatenate([a, b], axis=0)

    def corner_swap(values):
        places = list(itertools.product(range(row_total), range(col_total)))
        at = lambda row, col: row * col_total + col
        pairs = [(at(row, col), at(row ^ 3, col)) for row, col in places]
        return lax.ppermute(values, ("row", "col"), pairs)

    counts = list_counts(pair_list, pair_count)
    own = add_counts(pack_band(orbitals), col_total, counts, col_swap(counts, 1))
    in_order = lambda *values: lax.optimization_barrier(values)
    mate, x, y, z, w = in_order(
        col_swap(own, 1), col_swap(own, 2), row_swap(own, 1), row_swap(own, 2), row_swap(own, 4)
    )
    w_z, w_x, w_y = in_order(both(w, z), both(w, x), both(w, y))
    over_x, over_y, over_z = col_swap(w_z, 2), row_swap(w_x, 1), row_swap(w_y, 2)
    tables = [jnp.asarray(table) for table in solve_tables()]
    blocks = [own, w, z, y, x]
    *waves, sum0, sum1 = near_part(row_total, col_total, 0, [*blocks, mate, *tables])
    sum0, sum1, over_x, over_y, over_z = in_order(sum0, sum1, over_x, over_y, over_z)
    last = (
        col_swap(over_z, 2),
        row_swap(over_x[:1], 1),
        row_swap(over_y[:1], 2),
        corner_swap(over_x[:1]),
    )
    for part, arrived in enumerate(((over_x, over_y, over_z), last), 1):
        blocks += arrived
        operands = [*blocks, mate, *tables, *waves, sum0, sum1]
        sum0, sum1 = near_part(row_total, col_total, part, operands)
    return finish(flatten(sum0), col_swap(sum1, 1))


def far_shards(row_total, col_total, orbitals, pair_list, pair_count):
    counts = count_pairs(pair_list, pair_count, row_total, col_total)
    own = pack_band(orbitals)
    axes = ("row", "col")
    table = lax.all_gather(counts.reshape(-1), axes)
    table = table.reshape(row_total, col_total, col_total, row_total)
    wide = col_total // 2
    column = lax.all_gather(own[0], "row")
    columns = [column] + [swap(column, "col", col_total, 2 * x) for x in range(1, wide)]
    bands = jnp.concatenate(columns, axis=0)
    row = lax.axis_index("row")
    col = lax.axis_index("col")
    mine = jnp.stack([col, col ^ 1])
    other_col = ((col // 2) ^ lax.iota(jnp.int32, wide)) * 2 + col % 2
    other_row = lax.iota(jnp.int32, row_total)
    direct = table[row][other_col][:, mine]
    direct = jnp.transpose(direct, (1, 2, 0))
    mirror = table[:, :, :, row][:, mine][:, :, other_col]
    mirror = jnp.transpose(mirror, (1, 0, 2))
    same = (mine[:, None, None] == other_col[None, None, :]) & (other_row == row)[None, :, None]
    weights = (direct + jnp.where(same, 0.0, mirror)).astype(jnp.int32).reshape(-1)
    index = lax.iota(jnp.int32, weights.shape[0])
    order = jnp.argsort(jnp.where(weights > 0, 0, 1), stable=True)
    pad = lambda values: jnp.pad(values.astype(jnp.int32), (0, SIDE))
    slots = row_total * wide
    slot = order % slots
    band = (slot % wide) * row_total + slot // wide
    total = jnp.sum((weights > 0).astype(jnp.int32)).reshape(1)
    fields = pl.pallas_call(
        far_kernel,
        out_shape=[wide_of(LIVE), wide_of(FLAT)],
        in_specs=[SMEM_SPEC] * 4 + [ANY_SPEC] + [VMEM_SPEC] * 7,
        out_specs=[VMEM_SPEC] * 2,
        scratch_shapes=[pltpu.VMEM((PACK, LANES), BF16)]
        + [pltpu.VMEM((rows, LANES), F32) for rows in (LIVE, LIVE, LIVE, PITCHED)]
        + solve_scratch(),
        compiler_params=PARAMS,
        name="solve_pairs",
    )(
        total,
        pad(band),
        pad(order // slots),
        pad(weights[order]),
        bands,
        own,
        swap(own, "col", col_total, 1),
        *map(jnp.asarray, solve_tables()),
    )
    return finish(flatten(fields[0]), swap(fields[1], "col", col_total, 1))


def solution(mesh):
    row_total, col_total = mesh.shape["row"], mesh.shape["col"]
    near = (row_total, col_total) == NEAR
    shards = near_shards if near else far_shards
    return jax.shard_map(
        functools.partial(shards, row_total, col_total),
        mesh=mesh,
        in_specs=(P(("row", "col"), None), P(("row", "col"), None, None), P(("row", "col"))),
        out_specs=P(("row", "col"), None),
        check_vma=False,
    )
```

```python
import functools
import itertools

import jax
import jax.numpy as jnp
import ml_dtypes
import numpy as np
from jax import lax
from jax.experimental import pallas as pl
from jax.experimental.pallas import tpu as pltpu
from jax.sharding import PartitionSpec as P

GX = 40
LANES = 128
SIDE = 3
THIRD = GX // SIDE
PART = THIRD * GX
PACK = -(-PART // 16) * 16
LIVE = GX * GX
SPARE = SIDE * GX
LAST = LANES - SPARE
LAST_PARTS = GX // LAST
TABLE = 208
FLAT = LIVE * GX // LANES
CHUNK = PACK // 16
FLAT_ROWS = 512
PITCHED = LIVE // 16 * 17
DUO = 2 * GX
QUAD = 4 * GX
PITCH = GX + 1
VMEM_LIMIT = 16 * 1024 * 1024
screen_width = 0.9
F32 = jnp.float32
BF16 = jnp.bfloat16


def real_basis():
    half = GX // 2
    point = np.arange(GX)
    rows = [np.cos(2 * np.pi * (k * point % GX) / GX) for k in range(half + 1)]
    rows += [np.sin(2 * np.pi * (k * point % GX) / GX) for k in range(1, half)]
    frequency = np.concatenate([np.arange(half + 1), np.arange(1, half)])
    norm = np.where((frequency == 0) | (frequency == half), 1.0, 2.0) / GX
    return np.stack(rows), frequency, norm


def halves(table):
    high = table.astype(ml_dtypes.bfloat16)
    low = (table - high.astype(np.float64)).astype(ml_dtypes.bfloat16)
    return high, low


def left_table(table):
    high, low = halves(np.kron(np.eye(2), table))
    return np.concatenate([high, low, high], axis=1)


def right_table(table):
    wide = np.zeros((LANES, LANES))
    for p in range(SIDE):
        wide[p * GX : (p + 1) * GX, p * GX : (p + 1) * GX] = table
    high, low = halves(wide)
    both = np.concatenate([high, low], axis=1)
    return np.concatenate([both, both], axis=0)


def kernel_table():
    _, frequency, norm = real_basis()
    wave = frequency * (2.0 * np.pi / GX)
    squared = wave * wave
    total = squared[:, None, None] + squared[None, :, None] + squared[None, None, :]
    safe = np.where(total > 0, total, 1.0)
    screened = 4.0 * np.pi * (1.0 - np.exp(-safe / (4.0 * screen_width**2))) / safe
    kernel = np.where(total > 0, screened, np.pi / screen_width**2)
    kernel = kernel * norm[:, None, None] * norm[None, :, None] * norm[None, None, :]
    rows = np.swapaxes(kernel, 0, 1).reshape(LIVE, GX)
    out = np.zeros((LIVE, LANES), np.float32)
    for p in range(SIDE):
        out[:, p * GX : (p + 1) * GX] = rows
    return out


def dot(a, b):
    return jnp.dot(a, b, preferred_element_type=F32)


def split(values):
    high = values.astype(BF16)
    return high, (values - high.astype(F32)).astype(BF16)


def contract_rows(table, values):
    high, low = split(values)
    return dot(table, jnp.concatenate([high, high, low], axis=0))


def contract_lanes(values, table):
    both = dot(jnp.concatenate(split(values), axis=1), table)
    return both[:, :LANES] + both[:, LANES:]


def fold(values):
    return jnp.concatenate([values[:DUO], values[DUO:]], axis=1)


def unfold(values):
    return jnp.concatenate([values[:, :LANES], values[:, LANES:]], axis=0)


def quad(step):
    return pl.ds(step * QUAD, QUAD)


def joined(planes):
    left = jnp.concatenate(planes[:2], axis=0)
    return jnp.concatenate([left, jnp.concatenate(planes[2:], axis=0)], axis=1)


def parted(values):
    return [
        values[i % 2 * GX : i % 2 * GX + GX, i // 2 * LANES : (i // 2 + 1) * LANES] for i in range(4)
    ]


def load_planes(ref, step):
    return joined([ref[pl.ds(step * 4 + i, GX, stride=PITCH), :] for i in range(4)])


def store_planes(ref, step, values):
    for i, plane in enumerate(parted(values)):
        ref[pl.ds(step * 4 + i, GX, stride=PITCH), :] = plane


def load_x_planes(ref, step):
    return joined([ref[pl.ds((step * 4 + i) * PITCH, GX), :] for i in range(4)])


def store_x_planes(ref, step, values):
    for i, plane in enumerate(parted(values)):
        ref[pl.ds((step * 4 + i) * PITCH, GX), :] = plane


def count_vector(pairs, live):
    slots = pairs.shape[1]
    row = lax.broadcasted_iota(jnp.int32, (16, slots), 0)
    lane = lax.broadcasted_iota(jnp.int32, (LANES, slots), 0) - SPARE
    first = (pairs[0:1] == row) & (lax.broadcasted_iota(jnp.int32, (16, slots), 1) < live)
    second = jnp.where(pairs[1:2] == lane, 1.0, 0.0)
    contract = (((1,), (1,)), ((), ()))
    return lax.dot_general(jnp.where(first, 1.0, 0.0), second, contract, preferred_element_type=F32)


def unroll_rows(copy):
    for k in range(FLAT):
        copy(k, slice(k * LANES, (k + 1) * LANES))


def pack_kernel(band_ref, out_ref, flat_ref, wide_ref, last_ref):
    def to_rows(k, lanes):
        flat_ref[k : k + 1, :] = band_ref[0:1, lanes].astype(F32)

    unroll_rows(to_rows)
    unused = FLAT_ROWS - FLAT
    flat_ref[FLAT:FLAT_ROWS, :] = jnp.zeros((unused, LANES), F32)
    lane = lax.broadcasted_iota(jnp.int32, (1, LANES), 1)

    def rows_of(first, count, target):
        group, q = divmod(first, 16)
        row, offset = divmod(q * GX, LANES)
        start = group * 5 + row
        values = flat_ref[pl.ds(start, count, stride=5), :]
        if offset + GX > LANES:
            after = flat_ref[pl.ds(start + 1, count, stride=5), :]
            values = jnp.where(lane >= offset, values, after)
        shift = (target - offset) % LANES
        return pltpu.roll(values, shift, 1) if shift else values

    for q in range(16):
        packed = jnp.zeros((CHUNK, LANES), F32)
        for third in range(SIDE):
            values = rows_of(third * PART + q, CHUNK, third * GX)
            packed = jnp.where(lane // GX == third, values, packed)
        wide_ref[pl.ds(q, CHUNK, stride=16), :] = packed
        last_ref[pl.ds(q, 3, stride=16), :] = rows_of(SIDE * PART + q, 3, 0)
    for part in range(LAST_PARTS):
        rows = slice(part * GX, (part + 1) * GX)
        values = pltpu.roll(last_ref[0:GX, :], SPARE - part * LAST, 1)
        wide_ref[rows, :] = jnp.where(lane >= SPARE, values, wide_ref[rows, :])
    out_ref[0] = wide_ref[...].astype(BF16)


def list_kernel(pairs_ref, live_ref, out_ref):
    out_ref[...] = count_vector(pairs_ref[0], live_ref[...])


def count_kernel(col_total, packed_ref, own_ref, mate_ref, out_ref):
    out_ref[...] = packed_ref[...]
    counts = own_ref[...] + pltpu.roll(mate_ref[...], col_total, 0)
    rows = slice(TABLE, TABLE + 16)
    out_ref[0, rows, :] = (packed_ref[0, rows, :].astype(F32) + counts).astype(BF16)


def spread(load, out_ref):
    lane = lax.broadcasted_iota(jnp.int32, (1, LANES), 1)
    for start in range(0, PACK, DUO):
        count = min(DUO, PACK - start)
        bands = [load(p, slice(start, start + count)).astype(F32) for p in range(SIDE)]
        count = min(count, PART - start)
        for third in range(SIDE):
            wide = jnp.zeros((count, LANES), F32)
            for p, values in enumerate(bands):
                shift = (p - third) * GX % LANES
                values = values[:count]
                values = pltpu.roll(values, shift, 1) if shift else values
                wide = jnp.where(lane // GX == p, values, wide)
            out_ref[third * PART + start : third * PART + start + count, :] = wide
    wide = jnp.zeros((GX, LANES), F32)
    for p in range(SIDE):
        band = load(p, slice(0, TABLE)).astype(F32)
        for part in range(LAST_PARTS):
            lanes = p * GX + part * LAST
            values = pltpu.roll(band[part * GX : (part + 1) * GX], (lanes - SPARE) % LANES, 1)
            wide = jnp.where((lane >= lanes) & (lane < lanes + LAST), values, wide)
    out_ref[SIDE * PART : LIVE, :] = wide


def spread_waves(band_refs, wave_refs):
    for (ref, at), wave_ref in zip(band_refs, wave_refs):
        spread(lambda p, rows: ref[at, rows, :], wave_ref)


def clear(sum_refs):
    for sum_ref in sum_refs:
        sum_ref[...] = jnp.zeros_like(sum_ref)


def lane_side():
    return lax.broadcasted_iota(jnp.int32, (1, LANES), 1) // GX


def solve_trios(first, count, lists, load_band, tables, wave_refs, sum_refs, scratch):
    z_ref, z_back_ref, row_ref, row_back_ref, kernel_ref = tables
    trio_ref, partner_ref, work_ref, work2_ref = scratch
    slot_list, band_list, weight_list = lists
    side = lane_side()

    def by_side(values):
        row = jnp.zeros((1, LANES), F32)
        for p in range(SIDE):
            row = jnp.where(side == p, values[p].astype(F32), row)
        return row

    def trio(at, carry):
        places = [first + at * SIDE + p for p in range(SIDE)]
        for p, place in enumerate(places):
            load_band(slot_list[place], trio_ref, p)
        bands = [band_list[place] for place in places]
        weights = [weight_list[place] for place in places]
        is_mate = by_side(bands) > 0.5
        scales = [
            by_side([jnp.where(bands[p] == which, weights[p], 0) for p in range(SIDE)])
            for which in range(2)
        ]
        spread(lambda p, rows: trio_ref[p, rows, :], partner_ref)

        steps = range(GX // 4)

        def forward():
            values = []
            for step in steps:
                wave = jnp.where(is_mate, wave_refs[1][quad(step), :], wave_refs[0][quad(step), :])
                values.append(partner_ref[quad(step), :] * wave)
            values = [contract_lanes(v, z_ref[...]) for v in values]
            values = [contract_rows(row_ref[...], fold(v)) for v in values]
            for step, v in zip(steps, values):
                store_x_planes(work_ref, step, v)

        def across():
            values = [load_planes(work_ref, step) for step in steps]
            values = [contract_rows(row_ref[...], v) for v in values]
            values = [v * fold(kernel_ref[quad(step), :]) for step, v in zip(steps, values)]
            values = [contract_rows(row_back_ref[...], v) for v in values]
            for step, v in zip(steps, values):
                store_planes(work2_ref, step, v)

        def back():
            values = [load_x_planes(work2_ref, step) for step in steps]
            values = [unfold(contract_rows(row_back_ref[...], v)) for v in values]
            values = [contract_lanes(v, z_back_ref[...]) for v in values]
            for step, v in zip(steps, values):
                v = v * partner_ref[quad(step), :]
                for sum_ref, scale in zip(sum_refs, scales):
                    sum_ref[quad(step), :] = sum_ref[quad(step), :] + v * scale

        for phase in (forward, across, back):
            phase()
        return carry

    lax.fori_loop(0, count, trio, 0)


def flat_field(sum_ref, out_ref, pitched_ref):
    lane = lax.broadcasted_iota(jnp.int32, (1, LANES), 1)
    rows = LIVE // 16
    for group in range(rows):
        pitched_ref[group * 17 : group * 17 + 16, :] = sum_ref[group * 16 : group * 16 + 16, :]
    flat = [jnp.zeros((rows, LANES), F32)] * 5
    for q in range(16):
        row, offset = divmod(q * GX, LANES)
        values = pitched_ref[pl.ds(q, rows, stride=17), :]
        moved = jnp.zeros((rows, LANES), F32)
        for p in range(SIDE):
            shift = (offset - p * GX) % LANES
            moved = moved + (pltpu.roll(values, shift, 1) if shift else values)
        flat[row] = jnp.where(lane >= offset, moved, flat[row])
        if offset + GX > LANES:
            flat[row + 1] = jnp.where(lane < offset + GX - LANES, moved, flat[row + 1])
    for row in range(5):
        out_ref[pl.ds(row, rows, stride=5), :] = flat[row]


def near_kernel(row_total, col_total, part, *refs):
    stages = STAGES[: part + 1]
    blocks = [block for stage in stages for block in stage]
    band_refs, refs = refs[: len(blocks)], refs[len(blocks) :]
    bands = [(ref, at) for ref, block in zip(band_refs, blocks) for at in range(len(block))]
    flips = [flip for block in blocks for flip in block]
    homes = [flip for flip in flips if flip[1] % 2 == 0]
    mate_ref, tables, refs = refs[0], refs[1:6], refs[6:]
    if part:
        wave_refs, given_refs, out_refs, refs = refs[:2], refs[2:4], refs[4:6], refs[6:]
    else:
        wave_refs, out_refs, refs = refs[:2], refs[2:4], refs[4:]
    (count_vmem, count_smem, slot_list, band_list, weight_list), refs = refs[:5], refs[5:]
    scratch, sem = refs[:4], refs[4]
    sum_refs = (out_refs[0], refs[5]) if part == 2 else out_refs

    lane = lax.broadcasted_iota(jnp.int32, (8, LANES), 1)
    counts = jnp.zeros((8, LANES), F32)
    for s, flip in enumerate(homes):
        ref, at = bands[flips.index(flip)]
        spare = ref[at, TABLE : TABLE + 16, :].astype(F32)[0:8]
        shift = (s * row_total - SPARE) % LANES
        moved = pltpu.roll(spare, shift, 1) if shift else spare
        counts = jnp.where(lane // row_total == s, moved, counts)
    count_vmem[...] = counts.astype(jnp.int32)
    copy = pltpu.make_async_copy(count_vmem, count_smem, sem)
    copy.start()
    if part:
        for sum_ref, given_ref in zip(sum_refs, given_refs):
            sum_ref[...] = given_ref[...]
    else:
        clear(sum_refs)
        spread_waves(((band_refs[0], 0), (mate_ref, 0)), wave_refs)
    copy.wait()
    row = lax.axis_index("row")
    col = lax.axis_index("col")
    total = jnp.int32(0)
    done = jnp.int32(0)
    place = 0
    for step, stage in enumerate(stages):
        here = range(place, place + sum(len(block) for block in stage))
        place = here.stop
        for which, at in itertools.product(range(2), here):
            row_flip, col_flip = flips[at]
            other_core = col_flip % 2
            row_place = homes.index((0, col_flip - other_core)) * row_total
            col_place = homes.index((row_flip, 0)) * row_total
            first = other_core * col_total + (col ^ which)
            weight = count_smem[first, row_place + (row ^ row_flip)]
            if at or which:
                mirror = which * col_total + (col ^ col_flip)
                weight = weight + count_smem[mirror, col_place + row]
            if (row_flip, col_flip) in SHIFTED:
                weight = jnp.where(col % 2 == 1, weight, 0)
            slot_list[total] = at
            band_list[total] = which
            weight_list[total] = weight
            total = total + jnp.where(weight > 0, 1, 0)
        trios = (total - done + SIDE - 1) // SIDE
        if step < 2:
            trios = jnp.minimum(trios, CAPS[step])
        if step < part:
            done = jnp.minimum(done + trios * SIDE, total)
    for p in range(SIDE - 1):
        slot_list[total + p] = 0
        band_list[total + p] = 0
        weight_list[total + p] = 0

    def load_band(wanted, target, p):
        for place, (ref, at) in enumerate(bands):

            @pl.when(wanted == place)
            def _():
                target[p] = ref[at]

    lists = (slot_list, band_list, weight_list)
    solve_trios(done, trios, lists, load_band, tables, wave_refs, sum_refs, scratch)
    if part == 2:
        flat_field(sum_refs[1], out_refs[1], refs[6])


def far_kernel(total_ref, slot_list, band_list, weight_list, bands_ref, own_ref, mate_ref, *refs):
    tables, out_refs, refs = refs[:5], refs[5:7], refs[7:]
    buffer, wave_refs, sum_refs = refs[0], refs[1:3], (out_refs[0], refs[3])
    pitched_ref, scratch = refs[4], refs[5:]
    spread_waves(((own_ref, 0), (mate_ref, 0)), wave_refs)
    clear(sum_refs)

    def load_band(place, target, p):
        pltpu.sync_copy(bands_ref.at[place], buffer)
        target[p] = buffer[...]

    lists = (slot_list, band_list, weight_list)
    trios = (total_ref[0] + SIDE - 1) // SIDE
    solve_trios(0, trios, lists, load_band, tables, wave_refs, sum_refs, scratch)
    flat_field(sum_refs[1], out_refs[1], pitched_ref)


def flat_kernel(sum_ref, out_ref, pitched_ref):
    flat_field(sum_ref, out_ref, pitched_ref)


def finish_kernel(own_ref, part_ref, out_ref):
    def to_lanes(k, lanes):
        out_ref[0:1, lanes] = own_ref[k : k + 1, :] + part_ref[k : k + 1, :]

    unroll_rows(to_lanes)


VMEM_SPEC = pl.BlockSpec(memory_space=pltpu.VMEM)
SMEM_SPEC = pl.BlockSpec(memory_space=pltpu.SMEM)
ANY_SPEC = pl.BlockSpec(memory_space=pl.ANY)
PARAMS = pltpu.CompilerParams(vmem_limit_bytes=VMEM_LIMIT)


def solve_tables():
    basis, _, _ = real_basis()
    return [
        right_table(basis.T),
        right_table(basis),
        left_table(basis),
        left_table(basis.T),
        kernel_table(),
    ]


def solve_scratch():
    wide = [pltpu.VMEM((rows, LANES), F32) for rows in (LIVE, GX * PITCH, GX * PITCH)]
    return [pltpu.VMEM((SIDE, PACK, LANES), BF16)] + wide


def wide_of(rows):
    return jax.ShapeDtypeStruct((rows, LANES), F32)


def swap(values, axis, size, flip):
    return lax.ppermute(values, axis, [(i, i ^ flip) for i in range(size)])


def count_pairs(pair_list, pair_count, row_total, col_total):
    slots = pair_list.shape[1]
    live = lax.iota(jnp.int32, slots) < pair_count[0]
    first = pair_list[0, :, 0][:, None, None] == lax.iota(jnp.int32, col_total)[None, :, None]
    second = pair_list[0, :, 1][:, None, None] == lax.iota(jnp.int32, row_total)[None, None, :]
    return jnp.sum((first & second & live[:, None, None]).astype(F32), axis=0)


def pack_band(orbitals):
    return pl.pallas_call(
        pack_kernel,
        out_shape=jax.ShapeDtypeStruct((1, PACK, LANES), BF16),
        in_specs=[VMEM_SPEC],
        out_specs=VMEM_SPEC,
        scratch_shapes=[pltpu.VMEM((rows, LANES), F32) for rows in (FLAT_ROWS, PACK, 48)],
        compiler_params=PARAMS,
        name="pack_band",
    )(orbitals)


def list_counts(pair_list, pair_count):
    return pl.pallas_call(
        list_kernel,
        out_shape=jax.ShapeDtypeStruct((16, LANES), F32),
        in_specs=[VMEM_SPEC] * 2,
        out_specs=VMEM_SPEC,
        compiler_params=PARAMS,
        name="list_counts",
    )(jnp.swapaxes(pair_list, 1, 2), pair_count.reshape(1, 1))


def add_counts(packed, col_total, counts, mate_counts):
    return pl.pallas_call(
        functools.partial(count_kernel, col_total),
        out_shape=jax.ShapeDtypeStruct(packed.shape, BF16),
        in_specs=[VMEM_SPEC] * 3,
        out_specs=VMEM_SPEC,
        compiler_params=PARAMS,
        name="add_counts",
    )(packed, counts, mate_counts)


def flatten(sums):
    return pl.pallas_call(
        flat_kernel,
        out_shape=wide_of(FLAT),
        in_specs=[VMEM_SPEC],
        out_specs=VMEM_SPEC,
        scratch_shapes=[pltpu.VMEM((PITCHED, LANES), F32)],
        compiler_params=PARAMS,
        name="flatten",
    )(sums)


def finish(own, part):
    return pl.pallas_call(
        finish_kernel,
        out_shape=jax.ShapeDtypeStruct((1, LIVE * GX), F32),
        in_specs=[VMEM_SPEC] * 2,
        out_specs=VMEM_SPEC,
        compiler_params=PARAMS,
        name="add_parts",
    )(own, part)


NEAR = (8, 4)
STAGES = (
    (((0, 0),), ((4, 0),), ((2, 0),), ((1, 0),), ((0, 2),)),
    (((4, 2), (2, 2)), ((5, 0), (1, 2)), ((6, 0), (3, 0)), ((4, 1), (2, 1))),
    (((6, 2), (3, 2)), ((5, 2),), ((7, 0),), ((7, 2),)),
)
CAPS = (1, 2)
SHIFTED = ((4, 0), (2, 0), (4, 1), (2, 1))


def near_part(row_total, col_total, part, operands):
    places = 2 * sum(len(block) for stage in STAGES for block in stage) + SIDE
    out_shape = [wide_of(LIVE)] * 2
    if part == 0:
        out_shape = out_shape * 2
    if part == 2:
        out_shape = [wide_of(LIVE), wide_of(FLAT)]
    operands = list(operands)
    cost = pl.CostEstimate(flops=4 * 10**9, bytes_accessed=2 * 10**7, transcendentals=0)
    return pl.pallas_call(
        functools.partial(near_kernel, row_total, col_total, part),
        out_shape=out_shape,
        in_specs=[VMEM_SPEC] * len(operands),
        out_specs=[VMEM_SPEC] * len(out_shape),
        scratch_shapes=[
            pltpu.VMEM((8, LANES), jnp.int32),
            pltpu.SMEM((8, LANES), jnp.int32),
            pltpu.SMEM((places,), jnp.int32),
            pltpu.SMEM((places,), jnp.int32),
            pltpu.SMEM((places,), jnp.int32),
        ]
        + solve_scratch()
        + [pltpu.SemaphoreType.DMA]
        + ([pltpu.VMEM((rows, LANES), F32) for rows in (LIVE, PITCHED)] if part == 2 else []),
        compiler_params=PARAMS,
        cost_estimate=cost,
        name="solve_part",
    )(*operands)


def near_shards(row_total, col_total, orbitals, pair_list, pair_count):
    row_swap = lambda values, flip: swap(values, "row", row_total, flip)
    col_swap = lambda values, flip: swap(values, "col", col_total, flip)
    both = lambda a, b: jnp.concatenate([a, b], axis=0)

    def corner_swap(values):
        places = list(itertools.product(range(row_total), range(col_total)))
        at = lambda row, col: row * col_total + col
        pairs = [(at(row, col), at(row ^ 3, col)) for row, col in places]
        return lax.ppermute(values, ("row", "col"), pairs)

    counts = list_counts(pair_list, pair_count)
    own = add_counts(pack_band(orbitals), col_total, counts, col_swap(counts, 1))
    in_order = lambda *values: lax.optimization_barrier(values)
    mate, x, y, z, w = in_order(
        col_swap(own, 1), col_swap(own, 2), row_swap(own, 1), row_swap(own, 2), row_swap(own, 4)
    )
    w_z, w_x, w_y = in_order(both(w, z), both(w, x), both(w, y))
    over_x, over_y, over_z = col_swap(w_z, 2), row_swap(w_x, 1), row_swap(w_y, 2)
    tables = [jnp.asarray(table) for table in solve_tables()]
    blocks = [own, w, z, y, x]
    *waves, sum0, sum1 = near_part(row_total, col_total, 0, [*blocks, mate, *tables])
    other, sum0, sum1, over_x, over_y, over_z = in_order(
        col_swap(w_z, 1), sum0, sum1, over_x, over_y, over_z
    )
    last = (
        col_swap(over_z, 2),
        row_swap(over_x[:1], 1),
        row_swap(over_y[:1], 2),
        corner_swap(over_x[:1]),
    )
    for part, arrived in enumerate(((over_x, over_y, over_z, other), last), 1):
        blocks += arrived
        operands = [*blocks, mate, *tables, *waves, sum0, sum1]
        sum0, sum1 = near_part(row_total, col_total, part, operands)
    return finish(flatten(sum0), col_swap(sum1, 1))


def far_shards(row_total, col_total, orbitals, pair_list, pair_count):
    counts = count_pairs(pair_list, pair_count, row_total, col_total)
    own = pack_band(orbitals)
    axes = ("row", "col")
    table = lax.all_gather(counts.reshape(-1), axes)
    table = table.reshape(row_total, col_total, col_total, row_total)
    wide = col_total // 2
    column = lax.all_gather(own[0], "row")
    columns = [column] + [swap(column, "col", col_total, 2 * x) for x in range(1, wide)]
    bands = jnp.concatenate(columns, axis=0)
    row = lax.axis_index("row")
    col = lax.axis_index("col")
    mine = jnp.stack([col, col ^ 1])
    other_col = ((col // 2) ^ lax.iota(jnp.int32, wide)) * 2 + col % 2
    other_row = lax.iota(jnp.int32, row_total)
    direct = table[row][other_col][:, mine]
    direct = jnp.transpose(direct, (1, 2, 0))
    mirror = table[:, :, :, row][:, mine][:, :, other_col]
    mirror = jnp.transpose(mirror, (1, 0, 2))
    same = (mine[:, None, None] == other_col[None, None, :]) & (other_row == row)[None, :, None]
    weights = (direct + jnp.where(same, 0.0, mirror)).astype(jnp.int32).reshape(-1)
    index = lax.iota(jnp.int32, weights.shape[0])
    order = jnp.argsort(jnp.where(weights > 0, 0, 1), stable=True)
    pad = lambda values: jnp.pad(values.astype(jnp.int32), (0, SIDE))
    slots = row_total * wide
    slot = order % slots
    band = (slot % wide) * row_total + slot // wide
    total = jnp.sum((weights > 0).astype(jnp.int32)).reshape(1)
    fields = pl.pallas_call(
        far_kernel,
        out_shape=[wide_of(LIVE), wide_of(FLAT)],
        in_specs=[SMEM_SPEC] * 4 + [ANY_SPEC] + [VMEM_SPEC] * 7,
        out_specs=[VMEM_SPEC] * 2,
        scratch_shapes=[pltpu.VMEM((PACK, LANES), BF16)]
        + [pltpu.VMEM((rows, LANES), F32) for rows in (LIVE, LIVE, LIVE, PITCHED)]
        + solve_scratch(),
        compiler_params=PARAMS,
        name="solve_pairs",
    )(
        total,
        pad(band),
        pad(order // slots),
        pad(weights[order]),
        bands,
        own,
        swap(own, "col", col_total, 1),
        *map(jnp.asarray, solve_tables()),
    )
    return finish(flatten(fields[0]), swap(fields[1], "col", col_total, 1))


def solution(mesh):
    row_total, col_total = mesh.shape["row"], mesh.shape["col"]
    near = (row_total, col_total) == NEAR
    shards = near_shards if near else far_shards
    return jax.shard_map(
        functools.partial(shards, row_total, col_total),
        mesh=mesh,
        in_specs=(P(("row", "col"), None), P(("row", "col"), None, None), P(("row", "col"))),
        out_specs=P(("row", "col"), None),
        check_vma=False,
    )
```

```python
import functools
import itertools

import jax
import jax.numpy as jnp
import ml_dtypes
import numpy as np
from jax import lax
from jax.experimental import pallas as pl
from jax.experimental.pallas import tpu as pltpu
from jax.sharding import PartitionSpec as P

GX = 40
LANES = 128
SIDE = 3
THIRD = GX // SIDE
PART = THIRD * GX
PACK = -(-PART // 16) * 16
LIVE = GX * GX
SPARE = SIDE * GX
LAST = LANES - SPARE
LAST_PARTS = GX // LAST
TABLE = 208
FLAT = LIVE * GX // LANES
CHUNK = PACK // 16
FLAT_ROWS = 512
PITCHED = LIVE // 16 * 17
DUO = 2 * GX
QUAD = 4 * GX
PITCH = GX + 1
VMEM_LIMIT = 16 * 1024 * 1024
screen_width = 0.9
F32 = jnp.float32
BF16 = jnp.bfloat16


def real_basis():
    half = GX // 2
    point = np.arange(GX)
    rows = [np.cos(2 * np.pi * (k * point % GX) / GX) for k in range(half + 1)]
    rows += [np.sin(2 * np.pi * (k * point % GX) / GX) for k in range(1, half)]
    frequency = np.concatenate([np.arange(half + 1), np.arange(1, half)])
    norm = np.where((frequency == 0) | (frequency == half), 1.0, 2.0) / GX
    return np.stack(rows), frequency, norm


def halves(table):
    high = table.astype(ml_dtypes.bfloat16)
    low = (table - high.astype(np.float64)).astype(ml_dtypes.bfloat16)
    return high, low


def left_table(table):
    high, low = halves(np.kron(np.eye(2), table))
    return np.concatenate([high, low, high], axis=1)


def right_table(table):
    wide = np.zeros((LANES, LANES))
    for p in range(SIDE):
        wide[p * GX : (p + 1) * GX, p * GX : (p + 1) * GX] = table
    high, low = halves(wide)
    both = np.concatenate([high, low], axis=1)
    return np.concatenate([both, both], axis=0)


def kernel_table():
    _, frequency, norm = real_basis()
    wave = frequency * (2.0 * np.pi / GX)
    squared = wave * wave
    total = squared[:, None, None] + squared[None, :, None] + squared[None, None, :]
    safe = np.where(total > 0, total, 1.0)
    screened = 4.0 * np.pi * (1.0 - np.exp(-safe / (4.0 * screen_width**2))) / safe
    kernel = np.where(total > 0, screened, np.pi / screen_width**2)
    kernel = kernel * norm[:, None, None] * norm[None, :, None] * norm[None, None, :]
    rows = np.swapaxes(kernel, 0, 1).reshape(LIVE, GX)
    out = np.zeros((LIVE, LANES), np.float32)
    for p in range(SIDE):
        out[:, p * GX : (p + 1) * GX] = rows
    return out


def dot(a, b):
    return jnp.dot(a, b, preferred_element_type=F32)


def split(values):
    high = values.astype(BF16)
    return high, (values - high.astype(F32)).astype(BF16)


def contract_rows(table, values):
    high, low = split(values)
    return dot(table, jnp.concatenate([high, high, low], axis=0))


def contract_lanes(values, table):
    both = dot(jnp.concatenate(split(values), axis=1), table)
    return both[:, :LANES] + both[:, LANES:]


def fold(values):
    return jnp.concatenate([values[:DUO], values[DUO:]], axis=1)


def unfold(values):
    return jnp.concatenate([values[:, :LANES], values[:, LANES:]], axis=0)


def quad(step):
    return pl.ds(step * QUAD, QUAD)


def joined(planes):
    left = jnp.concatenate(planes[:2], axis=0)
    return jnp.concatenate([left, jnp.concatenate(planes[2:], axis=0)], axis=1)


def parted(values):
    return [
        values[i % 2 * GX : i % 2 * GX + GX, i // 2 * LANES : (i // 2 + 1) * LANES] for i in range(4)
    ]


def load_planes(ref, step):
    return joined([ref[pl.ds(step * 4 + i, GX, stride=PITCH), :] for i in range(4)])


def store_planes(ref, step, values):
    for i, plane in enumerate(parted(values)):
        ref[pl.ds(step * 4 + i, GX, stride=PITCH), :] = plane


def load_x_planes(ref, step):
    return joined([ref[pl.ds((step * 4 + i) * PITCH, GX), :] for i in range(4)])


def store_x_planes(ref, step, values):
    for i, plane in enumerate(parted(values)):
        ref[pl.ds((step * 4 + i) * PITCH, GX), :] = plane


def count_vector(pairs, live):
    slots = pairs.shape[1]
    row = lax.broadcasted_iota(jnp.int32, (16, slots), 0)
    lane = lax.broadcasted_iota(jnp.int32, (LANES, slots), 0) - SPARE
    first = (pairs[0:1] == row) & (lax.broadcasted_iota(jnp.int32, (16, slots), 1) < live)
    second = jnp.where(pairs[1:2] == lane, 1.0, 0.0)
    contract = (((1,), (1,)), ((), ()))
    return lax.dot_general(jnp.where(first, 1.0, 0.0), second, contract, preferred_element_type=F32)


def unroll_rows(copy):
    for k in range(FLAT):
        copy(k, slice(k * LANES, (k + 1) * LANES))


def pack_kernel(band_ref, out_ref, flat_ref, wide_ref, last_ref):
    def to_rows(k, lanes):
        flat_ref[k : k + 1, :] = band_ref[0:1, lanes].astype(F32)

    unroll_rows(to_rows)
    unused = FLAT_ROWS - FLAT
    flat_ref[FLAT:FLAT_ROWS, :] = jnp.zeros((unused, LANES), F32)
    lane = lax.broadcasted_iota(jnp.int32, (1, LANES), 1)

    def rows_of(first, count, target):
        group, q = divmod(first, 16)
        row, offset = divmod(q * GX, LANES)
        start = group * 5 + row
        values = flat_ref[pl.ds(start, count, stride=5), :]
        if offset + GX > LANES:
            after = flat_ref[pl.ds(start + 1, count, stride=5), :]
            values = jnp.where(lane >= offset, values, after)
        shift = (target - offset) % LANES
        return pltpu.roll(values, shift, 1) if shift else values

    for q in range(16):
        packed = jnp.zeros((CHUNK, LANES), F32)
        for third in range(SIDE):
            values = rows_of(third * PART + q, CHUNK, third * GX)
            packed = jnp.where(lane // GX == third, values, packed)
        wide_ref[pl.ds(q, CHUNK, stride=16), :] = packed
        last_ref[pl.ds(q, 3, stride=16), :] = rows_of(SIDE * PART + q, 3, 0)
    for part in range(LAST_PARTS):
        rows = slice(part * GX, (part + 1) * GX)
        values = pltpu.roll(last_ref[0:GX, :], SPARE - part * LAST, 1)
        wide_ref[rows, :] = jnp.where(lane >= SPARE, values, wide_ref[rows, :])
    out_ref[0] = wide_ref[...].astype(BF16)


def list_kernel(pairs_ref, live_ref, out_ref):
    out_ref[...] = count_vector(pairs_ref[0], live_ref[...])


def count_kernel(col_total, packed_ref, own_ref, mate_ref, out_ref):
    out_ref[...] = packed_ref[...]
    counts = own_ref[...] + pltpu.roll(mate_ref[...], col_total, 0)
    rows = slice(TABLE, TABLE + 16)
    out_ref[0, rows, :] = (packed_ref[0, rows, :].astype(F32) + counts).astype(BF16)


def spread(load, out_ref):
    lane = lax.broadcasted_iota(jnp.int32, (1, LANES), 1)
    for start in range(0, PACK, DUO):
        count = min(DUO, PACK - start)
        bands = [load(p, slice(start, start + count)).astype(F32) for p in range(SIDE)]
        count = min(count, PART - start)
        for third in range(SIDE):
            wide = jnp.zeros((count, LANES), F32)
            for p, values in enumerate(bands):
                shift = (p - third) * GX % LANES
                values = values[:count]
                values = pltpu.roll(values, shift, 1) if shift else values
                wide = jnp.where(lane // GX == p, values, wide)
            out_ref[third * PART + start : third * PART + start + count, :] = wide
    wide = jnp.zeros((GX, LANES), F32)
    for p in range(SIDE):
        band = load(p, slice(0, TABLE)).astype(F32)
        for part in range(LAST_PARTS):
            lanes = p * GX + part * LAST
            values = pltpu.roll(band[part * GX : (part + 1) * GX], (lanes - SPARE) % LANES, 1)
            wide = jnp.where((lane >= lanes) & (lane < lanes + LAST), values, wide)
    out_ref[SIDE * PART : LIVE, :] = wide


def spread_waves(band_refs, wave_refs):
    for (ref, at), wave_ref in zip(band_refs, wave_refs):
        spread(lambda p, rows: ref[at, rows, :], wave_ref)


def clear(sum_refs):
    for sum_ref in sum_refs:
        sum_ref[...] = jnp.zeros_like(sum_ref)


def lane_side():
    return lax.broadcasted_iota(jnp.int32, (1, LANES), 1) // GX


def solve_trios(first, count, lists, load_band, tables, wave_refs, sum_refs, scratch):
    z_ref, z_back_ref, row_ref, row_back_ref, kernel_ref = tables
    trio_ref, partner_ref, work_ref, work2_ref = scratch
    slot_list, band_list, weight_list = lists
    side = lane_side()

    def by_side(values):
        row = jnp.zeros((1, LANES), F32)
        for p in range(SIDE):
            row = jnp.where(side == p, values[p].astype(F32), row)
        return row

    def trio(at, carry):
        places = [first + at * SIDE + p for p in range(SIDE)]
        for p, place in enumerate(places):
            load_band(slot_list[place], trio_ref, p)
        bands = [band_list[place] for place in places]
        weights = [weight_list[place] for place in places]
        is_mate = by_side(bands) > 0.5
        scales = [
            by_side([jnp.where(bands[p] == which, weights[p], 0) for p in range(SIDE)])
            for which in range(2)
        ]
        spread(lambda p, rows: trio_ref[p, rows, :], partner_ref)

        steps = range(GX // 4)

        def forward():
            values = []
            for step in steps:
                wave = jnp.where(is_mate, wave_refs[1][quad(step), :], wave_refs[0][quad(step), :])
                values.append(partner_ref[quad(step), :] * wave)
            values = [contract_lanes(v, z_ref[...]) for v in values]
            values = [contract_rows(row_ref[...], fold(v)) for v in values]
            for step, v in zip(steps, values):
                store_x_planes(work_ref, step, v)

        def across():
            values = [load_planes(work_ref, step) for step in steps]
            values = [contract_rows(row_ref[...], v) for v in values]
            values = [v * fold(kernel_ref[quad(step), :]) for step, v in zip(steps, values)]
            values = [contract_rows(row_back_ref[...], v) for v in values]
            for step, v in zip(steps, values):
                store_planes(work2_ref, step, v)

        def back():
            values = [load_x_planes(work2_ref, step) for step in steps]
            values = [unfold(contract_rows(row_back_ref[...], v)) for v in values]
            values = [contract_lanes(v, z_back_ref[...]) for v in values]
            for step, v in zip(steps, values):
                v = v * partner_ref[quad(step), :]
                for sum_ref, scale in zip(sum_refs, scales):
                    sum_ref[quad(step), :] = sum_ref[quad(step), :] + v * scale

        for phase in (forward, across, back):
            phase()
        return carry

    lax.fori_loop(0, count, trio, 0)


def flat_field(sum_ref, out_ref, pitched_ref):
    lane = lax.broadcasted_iota(jnp.int32, (1, LANES), 1)
    rows = LIVE // 16
    for group in range(rows):
        pitched_ref[group * 17 : group * 17 + 16, :] = sum_ref[group * 16 : group * 16 + 16, :]
    flat = [jnp.zeros((rows, LANES), F32)] * 5
    for q in range(16):
        row, offset = divmod(q * GX, LANES)
        values = pitched_ref[pl.ds(q, rows, stride=17), :]
        moved = jnp.zeros((rows, LANES), F32)
        for p in range(SIDE):
            shift = (offset - p * GX) % LANES
            moved = moved + (pltpu.roll(values, shift, 1) if shift else values)
        flat[row] = jnp.where(lane >= offset, moved, flat[row])
        if offset + GX > LANES:
            flat[row + 1] = jnp.where(lane < offset + GX - LANES, moved, flat[row + 1])
    for row in range(5):
        out_ref[pl.ds(row, rows, stride=5), :] = flat[row]


def near_kernel(row_total, col_total, part, *refs):
    stages = STAGES[: part + 1]
    blocks = [block for stage in stages for block in stage]
    band_refs, refs = refs[: len(blocks)], refs[len(blocks) :]
    bands = [(ref, at) for ref, block in zip(band_refs, blocks) for at in range(len(block))]
    flips = [flip for block in blocks for flip in block]
    homes = [flip for flip in flips if flip[1] % 2 == 0]
    mate_ref, tables, refs = refs[0], refs[1:6], refs[6:]
    if part:
        wave_refs, given_refs, out_refs, refs = refs[:2], refs[2:4], refs[4:6], refs[6:]
    else:
        wave_refs, out_refs, refs = refs[:2], refs[2:4], refs[4:]
    (count_vmem, count_smem, slot_list, band_list, weight_list), refs = refs[:5], refs[5:]
    scratch, sem = refs[:4], refs[4]
    sum_refs = (out_refs[0], refs[5]) if part == 2 else out_refs

    lane = lax.broadcasted_iota(jnp.int32, (8, LANES), 1)
    counts = jnp.zeros((8, LANES), F32)
    for s, flip in enumerate(homes):
        ref, at = bands[flips.index(flip)]
        spare = ref[at, TABLE : TABLE + 16, :].astype(F32)[0:8]
        shift = (s * row_total - SPARE) % LANES
        moved = pltpu.roll(spare, shift, 1) if shift else spare
        counts = jnp.where(lane // row_total == s, moved, counts)
    count_vmem[...] = counts.astype(jnp.int32)
    copy = pltpu.make_async_copy(count_vmem, count_smem, sem)
    copy.start()
    if part:
        for sum_ref, given_ref in zip(sum_refs, given_refs):
            sum_ref[...] = given_ref[...]
    else:
        clear(sum_refs)
        spread_waves(((band_refs[0], 0), (mate_ref, 0)), wave_refs)
    copy.wait()
    row = lax.axis_index("row")
    col = lax.axis_index("col")
    total = jnp.int32(0)
    done = jnp.int32(0)
    place = 0
    for step, stage in enumerate(stages):
        here = range(place, place + sum(len(block) for block in stage))
        place = here.stop
        for which, at in itertools.product(range(2), here):
            row_flip, col_flip = flips[at]
            other_core = col_flip % 2
            row_place = homes.index((0, col_flip - other_core)) * row_total
            col_place = homes.index((row_flip, 0)) * row_total
            first = other_core * col_total + (col ^ which)
            weight = count_smem[first, row_place + (row ^ row_flip)]
            if at or which:
                mirror = which * col_total + (col ^ col_flip)
                weight = weight + count_smem[mirror, col_place + row]
            if (row_flip, col_flip) in SHIFTED:
                weight = jnp.where(col % 2 == 1, weight, 0)
            slot_list[total] = at
            band_list[total] = which
            weight_list[total] = weight
            total = total + jnp.where(weight > 0, 1, 0)
        trios = (total - done + SIDE - 1) // SIDE
        if step < 2:
            trios = jnp.minimum(trios, CAPS[step])
        if step < part:
            done = jnp.minimum(done + trios * SIDE, total)
    for p in range(SIDE - 1):
        slot_list[total + p] = 0
        band_list[total + p] = 0
        weight_list[total + p] = 0

    def load_band(wanted, target, p):
        for place, (ref, at) in enumerate(bands):

            @pl.when(wanted == place)
            def _():
                target[p] = ref[at]

    lists = (slot_list, band_list, weight_list)
    solve_trios(done, trios, lists, load_band, tables, wave_refs, sum_refs, scratch)
    if part == 2:
        flat_field(sum_refs[1], out_refs[1], refs[6])


def far_kernel(total_ref, slot_list, band_list, weight_list, bands_ref, own_ref, mate_ref, *refs):
    tables, out_refs, refs = refs[:5], refs[5:7], refs[7:]
    buffer, wave_refs, sum_refs = refs[0], refs[1:3], (out_refs[0], refs[3])
    pitched_ref, scratch = refs[4], refs[5:]
    spread_waves(((own_ref, 0), (mate_ref, 0)), wave_refs)
    clear(sum_refs)

    def load_band(place, target, p):
        pltpu.sync_copy(bands_ref.at[place], buffer)
        target[p] = buffer[...]

    lists = (slot_list, band_list, weight_list)
    trios = (total_ref[0] + SIDE - 1) // SIDE
    solve_trios(0, trios, lists, load_band, tables, wave_refs, sum_refs, scratch)
    flat_field(sum_refs[1], out_refs[1], pitched_ref)


def flat_kernel(sum_ref, out_ref, pitched_ref):
    flat_field(sum_ref, out_ref, pitched_ref)


def finish_kernel(own_ref, part_ref, out_ref):
    def to_lanes(k, lanes):
        out_ref[0:1, lanes] = own_ref[k : k + 1, :] + part_ref[k : k + 1, :]

    unroll_rows(to_lanes)


VMEM_SPEC = pl.BlockSpec(memory_space=pltpu.VMEM)
SMEM_SPEC = pl.BlockSpec(memory_space=pltpu.SMEM)
ANY_SPEC = pl.BlockSpec(memory_space=pl.ANY)
PARAMS = pltpu.CompilerParams(vmem_limit_bytes=VMEM_LIMIT)


def solve_tables():
    basis, _, _ = real_basis()
    return [
        right_table(basis.T),
        right_table(basis),
        left_table(basis),
        left_table(basis.T),
        kernel_table(),
    ]


def solve_scratch():
    wide = [pltpu.VMEM((rows, LANES), F32) for rows in (LIVE, GX * PITCH, GX * PITCH)]
    return [pltpu.VMEM((SIDE, PACK, LANES), BF16)] + wide


def wide_of(rows):
    return jax.ShapeDtypeStruct((rows, LANES), F32)


def swap(values, axis, size, flip):
    return lax.ppermute(values, axis, [(i, i ^ flip) for i in range(size)])


def count_pairs(pair_list, pair_count, row_total, col_total):
    slots = pair_list.shape[1]
    live = lax.iota(jnp.int32, slots) < pair_count[0]
    first = pair_list[0, :, 0][:, None, None] == lax.iota(jnp.int32, col_total)[None, :, None]
    second = pair_list[0, :, 1][:, None, None] == lax.iota(jnp.int32, row_total)[None, None, :]
    return jnp.sum((first & second & live[:, None, None]).astype(F32), axis=0)


def pack_band(orbitals):
    return pl.pallas_call(
        pack_kernel,
        out_shape=jax.ShapeDtypeStruct((1, PACK, LANES), BF16),
        in_specs=[VMEM_SPEC],
        out_specs=VMEM_SPEC,
        scratch_shapes=[pltpu.VMEM((rows, LANES), F32) for rows in (FLAT_ROWS, PACK, 48)],
        compiler_params=PARAMS,
        name="pack_band",
    )(orbitals)


def list_counts(pair_list, pair_count):
    return pl.pallas_call(
        list_kernel,
        out_shape=jax.ShapeDtypeStruct((16, LANES), F32),
        in_specs=[VMEM_SPEC] * 2,
        out_specs=VMEM_SPEC,
        compiler_params=PARAMS,
        name="list_counts",
    )(jnp.swapaxes(pair_list, 1, 2), pair_count.reshape(1, 1))


def add_counts(packed, col_total, counts, mate_counts):
    return pl.pallas_call(
        functools.partial(count_kernel, col_total),
        out_shape=jax.ShapeDtypeStruct(packed.shape, BF16),
        in_specs=[VMEM_SPEC] * 3,
        out_specs=VMEM_SPEC,
        compiler_params=PARAMS,
        name="add_counts",
    )(packed, counts, mate_counts)


def flatten(sums):
    return pl.pallas_call(
        flat_kernel,
        out_shape=wide_of(FLAT),
        in_specs=[VMEM_SPEC],
        out_specs=VMEM_SPEC,
        scratch_shapes=[pltpu.VMEM((PITCHED, LANES), F32)],
        compiler_params=PARAMS,
        name="flatten",
    )(sums)


def finish(own, part):
    return pl.pallas_call(
        finish_kernel,
        out_shape=jax.ShapeDtypeStruct((1, LIVE * GX), F32),
        in_specs=[VMEM_SPEC] * 2,
        out_specs=VMEM_SPEC,
        compiler_params=PARAMS,
        name="add_parts",
    )(own, part)


NEAR = (8, 4)
STAGES = (
    (((0, 0),), ((4, 0),), ((2, 0),), ((1, 0),), ((0, 2),)),
    (((4, 2), (2, 2)), ((5, 0), (1, 2)), ((6, 0), (3, 0)), ((4, 1), (2, 1))),
    (((6, 2), (3, 2)), ((5, 2),), ((7, 0),), ((7, 2),)),
)
CAPS = (1, 2)
SHIFTED = ((4, 0), (2, 0), (4, 1), (2, 1))


def near_part(row_total, col_total, part, operands):
    places = 2 * sum(len(block) for stage in STAGES for block in stage) + SIDE
    out_shape = [wide_of(LIVE)] * 2
    if part == 0:
        out_shape = out_shape * 2
    if part == 2:
        out_shape = [wide_of(LIVE), wide_of(FLAT)]
    operands = list(operands)
    cost = pl.CostEstimate(flops=4 * 10**9, bytes_accessed=2 * 10**7, transcendentals=0)
    return pl.pallas_call(
        functools.partial(near_kernel, row_total, col_total, part),
        out_shape=out_shape,
        in_specs=[VMEM_SPEC] * len(operands),
        out_specs=[VMEM_SPEC] * len(out_shape),
        scratch_shapes=[
            pltpu.VMEM((8, LANES), jnp.int32),
            pltpu.SMEM((8, LANES), jnp.int32),
            pltpu.SMEM((places,), jnp.int32),
            pltpu.SMEM((places,), jnp.int32),
            pltpu.SMEM((places,), jnp.int32),
        ]
        + solve_scratch()
        + [pltpu.SemaphoreType.DMA]
        + ([pltpu.VMEM((rows, LANES), F32) for rows in (LIVE, PITCHED)] if part == 2 else []),
        compiler_params=PARAMS,
        cost_estimate=cost,
        name="solve_part",
    )(*operands)


def near_shards(row_total, col_total, orbitals, pair_list, pair_count):
    row_swap = lambda values, flip: swap(values, "row", row_total, flip)
    col_swap = lambda values, flip: swap(values, "col", col_total, flip)
    both = lambda a, b: jnp.concatenate([a, b], axis=0)

    def corner_swap(values):
        places = list(itertools.product(range(row_total), range(col_total)))
        at = lambda row, col: row * col_total + col
        pairs = [(at(row, col), at(row ^ 3, col)) for row, col in places]
        return lax.ppermute(values, ("row", "col"), pairs)

    counts = list_counts(pair_list, pair_count)
    own = add_counts(pack_band(orbitals), col_total, counts, col_swap(counts, 1))
    in_order = lambda *values: lax.optimization_barrier(values)
    mate, x, y, z, w = in_order(
        col_swap(own, 1), col_swap(own, 2), row_swap(own, 1), row_swap(own, 2), row_swap(own, 4)
    )
    w_z, w_x, w_y = in_order(both(w, z), both(w, x), both(w, y))
    over_x, over_y, over_z = col_swap(w_z, 2), row_swap(w_x, 1), row_swap(w_y, 2)
    tables = [jnp.asarray(table) for table in solve_tables()]
    blocks = [own, w, z, y, x]
    *waves, sum0, sum1 = near_part(row_total, col_total, 0, [*blocks, mate, *tables])
    w_z, sum0 = in_order(w_z, sum0)
    other, sum0, sum1, over_x, over_y, over_z = in_order(
        col_swap(w_z, 1), sum0, sum1, over_x, over_y, over_z
    )
    last = (
        col_swap(over_z, 2),
        row_swap(over_x[:1], 1),
        row_swap(over_y[:1], 2),
        corner_swap(over_x[:1]),
    )
    for part, arrived in enumerate(((over_x, over_y, over_z, other), last), 1):
        blocks += arrived
        operands = [*blocks, mate, *tables, *waves, sum0, sum1]
        sum0, sum1 = near_part(row_total, col_total, part, operands)
    return finish(flatten(sum0), col_swap(sum1, 1))


def far_shards(row_total, col_total, orbitals, pair_list, pair_count):
    counts = count_pairs(pair_list, pair_count, row_total, col_total)
    own = pack_band(orbitals)
    axes = ("row", "col")
    table = lax.all_gather(counts.reshape(-1), axes)
    table = table.reshape(row_total, col_total, col_total, row_total)
    wide = col_total // 2
    column = lax.all_gather(own[0], "row")
    columns = [column] + [swap(column, "col", col_total, 2 * x) for x in range(1, wide)]
    bands = jnp.concatenate(columns, axis=0)
    row = lax.axis_index("row")
    col = lax.axis_index("col")
    mine = jnp.stack([col, col ^ 1])
    other_col = ((col // 2) ^ lax.iota(jnp.int32, wide)) * 2 + col % 2
    other_row = lax.iota(jnp.int32, row_total)
    direct = table[row][other_col][:, mine]
    direct = jnp.transpose(direct, (1, 2, 0))
    mirror = table[:, :, :, row][:, mine][:, :, other_col]
    mirror = jnp.transpose(mirror, (1, 0, 2))
    same = (mine[:, None, None] == other_col[None, None, :]) & (other_row == row)[None, :, None]
    weights = (direct + jnp.where(same, 0.0, mirror)).astype(jnp.int32).reshape(-1)
    index = lax.iota(jnp.int32, weights.shape[0])
    order = jnp.argsort(jnp.where(weights > 0, 0, 1), stable=True)
    pad = lambda values: jnp.pad(values.astype(jnp.int32), (0, SIDE))
    slots = row_total * wide
    slot = order % slots
    band = (slot % wide) * row_total + slot // wide
    total = jnp.sum((weights > 0).astype(jnp.int32)).reshape(1)
    fields = pl.pallas_call(
        far_kernel,
        out_shape=[wide_of(LIVE), wide_of(FLAT)],
        in_specs=[SMEM_SPEC] * 4 + [ANY_SPEC] + [VMEM_SPEC] * 7,
        out_specs=[VMEM_SPEC] * 2,
        scratch_shapes=[pltpu.VMEM((PACK, LANES), BF16)]
        + [pltpu.VMEM((rows, LANES), F32) for rows in (LIVE, LIVE, LIVE, PITCHED)]
        + solve_scratch(),
        compiler_params=PARAMS,
        name="solve_pairs",
    )(
        total,
        pad(band),
        pad(order // slots),
        pad(weights[order]),
        bands,
        own,
        swap(own, "col", col_total, 1),
        *map(jnp.asarray, solve_tables()),
    )
    return finish(flatten(fields[0]), swap(fields[1], "col", col_total, 1))


def solution(mesh):
    row_total, col_total = mesh.shape["row"], mesh.shape["col"]
    near = (row_total, col_total) == NEAR
    shards = near_shards if near else far_shards
    return jax.shard_map(
        functools.partial(shards, row_total, col_total),
        mesh=mesh,
        in_specs=(P(("row", "col"), None), P(("row", "col"), None, None), P(("row", "col"))),
        out_specs=P(("row", "col"), None),
        check_vma=False,
    )
```

```python
import functools
import itertools

import jax
import jax.numpy as jnp
import ml_dtypes
import numpy as np
from jax import lax
from jax.experimental import pallas as pl
from jax.experimental.pallas import tpu as pltpu
from jax.sharding import PartitionSpec as P

GX = 40
LANES = 128
SIDE = 3
THIRD = GX // SIDE
PART = THIRD * GX
PACK = -(-PART // 16) * 16
LIVE = GX * GX
SPARE = SIDE * GX
LAST = LANES - SPARE
LAST_PARTS = GX // LAST
TABLE = 208
FLAT = LIVE * GX // LANES
CHUNK = PACK // 16
FLAT_ROWS = 512
PITCHED = LIVE // 16 * 17
DUO = 2 * GX
QUAD = 4 * GX
PITCH = GX + 1
VMEM_LIMIT = 16 * 1024 * 1024
screen_width = 0.9
F32 = jnp.float32
BF16 = jnp.bfloat16


def real_basis():
    half = GX // 2
    point = np.arange(GX)
    rows = [np.cos(2 * np.pi * (k * point % GX) / GX) for k in range(half + 1)]
    rows += [np.sin(2 * np.pi * (k * point % GX) / GX) for k in range(1, half)]
    frequency = np.concatenate([np.arange(half + 1), np.arange(1, half)])
    norm = np.where((frequency == 0) | (frequency == half), 1.0, 2.0) / GX
    return np.stack(rows), frequency, norm


def halves(table):
    high = table.astype(ml_dtypes.bfloat16)
    low = (table - high.astype(np.float64)).astype(ml_dtypes.bfloat16)
    return high, low


def left_table(table):
    high, low = halves(np.kron(np.eye(2), table))
    return np.concatenate([high, low, high], axis=1)


def right_table(table):
    wide = np.zeros((LANES, LANES))
    for p in range(SIDE):
        wide[p * GX : (p + 1) * GX, p * GX : (p + 1) * GX] = table
    high, low = halves(wide)
    both = np.concatenate([high, low], axis=1)
    return np.concatenate([both, both], axis=0)


def kernel_table():
    _, frequency, norm = real_basis()
    wave = frequency * (2.0 * np.pi / GX)
    squared = wave * wave
    total = squared[:, None, None] + squared[None, :, None] + squared[None, None, :]
    safe = np.where(total > 0, total, 1.0)
    screened = 4.0 * np.pi * (1.0 - np.exp(-safe / (4.0 * screen_width**2))) / safe
    kernel = np.where(total > 0, screened, np.pi / screen_width**2)
    kernel = kernel * norm[:, None, None] * norm[None, :, None] * norm[None, None, :]
    rows = np.swapaxes(kernel, 0, 1).reshape(LIVE, GX)
    out = np.zeros((LIVE, LANES), np.float32)
    for p in range(SIDE):
        out[:, p * GX : (p + 1) * GX] = rows
    return out


def dot(a, b):
    return jnp.dot(a, b, preferred_element_type=F32)


def split(values):
    high = values.astype(BF16)
    return high, (values - high.astype(F32)).astype(BF16)


def contract_rows(table, values):
    high, low = split(values)
    return dot(table, jnp.concatenate([high, high, low], axis=0))


def contract_lanes(values, table):
    both = dot(jnp.concatenate(split(values), axis=1), table)
    return both[:, :LANES] + both[:, LANES:]


def contract_lanes_by_two(values, table):
    count = values[0].shape[0]
    out = []
    for at in range(0, len(values), 2):
        both = contract_lanes(jnp.concatenate(values[at : at + 2], axis=0), table)
        out += [both[:count], both[count:]]
    return out


def fold(values):
    return jnp.concatenate([values[:DUO], values[DUO:]], axis=1)


def unfold(values):
    return jnp.concatenate([values[:, :LANES], values[:, LANES:]], axis=0)


def quad(step):
    return pl.ds(step * QUAD, QUAD)


def joined(planes):
    left = jnp.concatenate(planes[:2], axis=0)
    return jnp.concatenate([left, jnp.concatenate(planes[2:], axis=0)], axis=1)


def parted(values):
    return [
        values[i % 2 * GX : i % 2 * GX + GX, i // 2 * LANES : (i // 2 + 1) * LANES] for i in range(4)
    ]


def load_planes(ref, step):
    return joined([ref[pl.ds(step * 4 + i, GX, stride=PITCH), :] for i in range(4)])


def store_planes(ref, step, values):
    for i, plane in enumerate(parted(values)):
        ref[pl.ds(step * 4 + i, GX, stride=PITCH), :] = plane


def load_x_planes(ref, step):
    return joined([ref[pl.ds((step * 4 + i) * PITCH, GX), :] for i in range(4)])


def store_x_planes(ref, step, values):
    for i, plane in enumerate(parted(values)):
        ref[pl.ds((step * 4 + i) * PITCH, GX), :] = plane


def count_vector(pairs, live):
    slots = pairs.shape[1]
    row = lax.broadcasted_iota(jnp.int32, (16, slots), 0)
    lane = lax.broadcasted_iota(jnp.int32, (LANES, slots), 0) - SPARE
    first = (pairs[0:1] == row) & (lax.broadcasted_iota(jnp.int32, (16, slots), 1) < live)
    second = jnp.where(pairs[1:2] == lane, 1.0, 0.0)
    contract = (((1,), (1,)), ((), ()))
    return lax.dot_general(jnp.where(first, 1.0, 0.0), second, contract, preferred_element_type=F32)


def unroll_rows(copy):
    for k in range(FLAT):
        copy(k, slice(k * LANES, (k + 1) * LANES))


def pack_kernel(band_ref, out_ref, flat_ref, wide_ref, last_ref):
    def to_rows(k, lanes):
        flat_ref[k : k + 1, :] = band_ref[0:1, lanes].astype(F32)

    unroll_rows(to_rows)
    unused = FLAT_ROWS - FLAT
    flat_ref[FLAT:FLAT_ROWS, :] = jnp.zeros((unused, LANES), F32)
    lane = lax.broadcasted_iota(jnp.int32, (1, LANES), 1)

    def rows_of(first, count, target):
        group, q = divmod(first, 16)
        row, offset = divmod(q * GX, LANES)
        start = group * 5 + row
        values = flat_ref[pl.ds(start, count, stride=5), :]
        if offset + GX > LANES:
            after = flat_ref[pl.ds(start + 1, count, stride=5), :]
            values = jnp.where(lane >= offset, values, after)
        shift = (target - offset) % LANES
        return pltpu.roll(values, shift, 1) if shift else values

    for q in range(16):
        packed = jnp.zeros((CHUNK, LANES), F32)
        for third in range(SIDE):
            values = rows_of(third * PART + q, CHUNK, third * GX)
            packed = jnp.where(lane // GX == third, values, packed)
        wide_ref[pl.ds(q, CHUNK, stride=16), :] = packed
        last_ref[pl.ds(q, 3, stride=16), :] = rows_of(SIDE * PART + q, 3, 0)
    for part in range(LAST_PARTS):
        rows = slice(part * GX, (part + 1) * GX)
        values = pltpu.roll(last_ref[0:GX, :], SPARE - part * LAST, 1)
        wide_ref[rows, :] = jnp.where(lane >= SPARE, values, wide_ref[rows, :])
    out_ref[0] = wide_ref[...].astype(BF16)


def list_kernel(pairs_ref, live_ref, out_ref):
    out_ref[...] = count_vector(pairs_ref[0], live_ref[...])


def count_kernel(col_total, packed_ref, own_ref, mate_ref, out_ref):
    out_ref[...] = packed_ref[...]
    counts = own_ref[...] + pltpu.roll(mate_ref[...], col_total, 0)
    rows = slice(TABLE, TABLE + 16)
    out_ref[0, rows, :] = (packed_ref[0, rows, :].astype(F32) + counts).astype(BF16)


def spread(load, out_ref):
    lane = lax.broadcasted_iota(jnp.int32, (1, LANES), 1)
    for start in range(0, PACK, DUO):
        count = min(DUO, PACK - start)
        bands = [load(p, slice(start, start + count)).astype(F32) for p in range(SIDE)]
        count = min(count, PART - start)
        for third in range(SIDE):
            wide = jnp.zeros((count, LANES), F32)
            for p, values in enumerate(bands):
                shift = (p - third) * GX % LANES
                values = values[:count]
                values = pltpu.roll(values, shift, 1) if shift else values
                wide = jnp.where(lane // GX == p, values, wide)
            out_ref[third * PART + start : third * PART + start + count, :] = wide
    wide = jnp.zeros((GX, LANES), F32)
    for p in range(SIDE):
        band = load(p, slice(0, TABLE)).astype(F32)
        for part in range(LAST_PARTS):
            lanes = p * GX + part * LAST
            values = pltpu.roll(band[part * GX : (part + 1) * GX], (lanes - SPARE) % LANES, 1)
            wide = jnp.where((lane >= lanes) & (lane < lanes + LAST), values, wide)
    out_ref[SIDE * PART : LIVE, :] = wide


def spread_waves(band_refs, wave_refs):
    for (ref, at), wave_ref in zip(band_refs, wave_refs):
        spread(lambda p, rows: ref[at, rows, :], wave_ref)


def clear(sum_refs):
    for sum_ref in sum_refs:
        sum_ref[...] = jnp.zeros_like(sum_ref)


def lane_side():
    return lax.broadcasted_iota(jnp.int32, (1, LANES), 1) // GX


def solve_trios(first, count, lists, load_band, tables, wave_refs, sum_refs, scratch):
    z_ref, z_back_ref, row_ref, row_back_ref, kernel_ref = tables
    trio_ref, partner_ref, work_ref, work2_ref = scratch
    slot_list, band_list, weight_list = lists
    side = lane_side()

    def by_side(values):
        row = jnp.zeros((1, LANES), F32)
        for p in range(SIDE):
            row = jnp.where(side == p, values[p].astype(F32), row)
        return row

    def trio(at, carry):
        places = [first + at * SIDE + p for p in range(SIDE)]
        for p, place in enumerate(places):
            load_band(slot_list[place], trio_ref, p)
        bands = [band_list[place] for place in places]
        weights = [weight_list[place] for place in places]
        is_mate = by_side(bands) > 0.5
        scales = [
            by_side([jnp.where(bands[p] == which, weights[p], 0) for p in range(SIDE)])
            for which in range(2)
        ]
        spread(lambda p, rows: trio_ref[p, rows, :], partner_ref)

        steps = range(GX // 4)

        def forward():
            values = []
            for step in steps:
                wave = jnp.where(is_mate, wave_refs[1][quad(step), :], wave_refs[0][quad(step), :])
                values.append(partner_ref[quad(step), :] * wave)
            values = contract_lanes_by_two(values, z_ref[...])
            values = [contract_rows(row_ref[...], fold(v)) for v in values]
            for step, v in zip(steps, values):
                store_x_planes(work_ref, step, v)

        def across():
            values = [load_planes(work_ref, step) for step in steps]
            values = [contract_rows(row_ref[...], v) for v in values]
            values = [v * fold(kernel_ref[quad(step), :]) for step, v in zip(steps, values)]
            values = [contract_rows(row_back_ref[...], v) for v in values]
            for step, v in zip(steps, values):
                store_planes(work2_ref, step, v)

        def back():
            values = [load_x_planes(work2_ref, step) for step in steps]
            values = [unfold(contract_rows(row_back_ref[...], v)) for v in values]
            values = contract_lanes_by_two(values, z_back_ref[...])
            for step, v in zip(steps, values):
                v = v * partner_ref[quad(step), :]
                for sum_ref, scale in zip(sum_refs, scales):
                    sum_ref[quad(step), :] = sum_ref[quad(step), :] + v * scale

        for phase in (forward, across, back):
            phase()
        return carry

    lax.fori_loop(0, count, trio, 0)


def flat_field(sum_ref, out_ref, pitched_ref):
    lane = lax.broadcasted_iota(jnp.int32, (1, LANES), 1)
    rows = LIVE // 16
    for group in range(rows):
        pitched_ref[group * 17 : group * 17 + 16, :] = sum_ref[group * 16 : group * 16 + 16, :]
    flat = [jnp.zeros((rows, LANES), F32)] * 5
    for q in range(16):
        row, offset = divmod(q * GX, LANES)
        values = pitched_ref[pl.ds(q, rows, stride=17), :]
        moved = jnp.zeros((rows, LANES), F32)
        for p in range(SIDE):
            shift = (offset - p * GX) % LANES
            moved = moved + (pltpu.roll(values, shift, 1) if shift else values)
        flat[row] = jnp.where(lane >= offset, moved, flat[row])
        if offset + GX > LANES:
            flat[row + 1] = jnp.where(lane < offset + GX - LANES, moved, flat[row + 1])
    for row in range(5):
        out_ref[pl.ds(row, rows, stride=5), :] = flat[row]


def near_kernel(row_total, col_total, part, *refs):
    stages = STAGES[: part + 1]
    blocks = [block for stage in stages for block in stage]
    band_refs, refs = refs[: len(blocks)], refs[len(blocks) :]
    bands = [(ref, at) for ref, block in zip(band_refs, blocks) for at in range(len(block))]
    flips = [flip for block in blocks for flip in block]
    homes = [flip for flip in flips if flip[1] % 2 == 0]
    mate_ref, tables, refs = refs[0], refs[1:6], refs[6:]
    if part:
        wave_refs, given_refs, out_refs, refs = refs[:2], refs[2:4], refs[4:6], refs[6:]
    else:
        wave_refs, out_refs, refs = refs[:2], refs[2:4], refs[4:]
    (count_vmem, count_smem, slot_list, band_list, weight_list), refs = refs[:5], refs[5:]
    scratch, sem = refs[:4], refs[4]
    sum_refs = (out_refs[0], refs[5]) if part == 2 else out_refs

    lane = lax.broadcasted_iota(jnp.int32, (8, LANES), 1)
    counts = jnp.zeros((8, LANES), F32)
    for s, flip in enumerate(homes):
        ref, at = bands[flips.index(flip)]
        spare = ref[at, TABLE : TABLE + 16, :].astype(F32)[0:8]
        shift = (s * row_total - SPARE) % LANES
        moved = pltpu.roll(spare, shift, 1) if shift else spare
        counts = jnp.where(lane // row_total == s, moved, counts)
    count_vmem[...] = counts.astype(jnp.int32)
    copy = pltpu.make_async_copy(count_vmem, count_smem, sem)
    copy.start()
    if part:
        for sum_ref, given_ref in zip(sum_refs, given_refs):
            sum_ref[...] = given_ref[...]
    else:
        clear(sum_refs)
        spread_waves(((band_refs[0], 0), (mate_ref, 0)), wave_refs)
    copy.wait()
    row = lax.axis_index("row")
    col = lax.axis_index("col")
    total = jnp.int32(0)
    done = jnp.int32(0)
    place = 0
    for step, stage in enumerate(stages):
        here = range(place, place + sum(len(block) for block in stage))
        place = here.stop
        for which, at in itertools.product(range(2), here):
            row_flip, col_flip = flips[at]
            other_core = col_flip % 2
            row_place = homes.index((0, col_flip - other_core)) * row_total
            col_place = homes.index((row_flip, 0)) * row_total
            first = other_core * col_total + (col ^ which)
            weight = count_smem[first, row_place + (row ^ row_flip)]
            if at or which:
                mirror = which * col_total + (col ^ col_flip)
                weight = weight + count_smem[mirror, col_place + row]
            if (row_flip, col_flip) in SHIFTED:
                weight = jnp.where(col % 2 == 1, weight, 0)
            slot_list[total] = at
            band_list[total] = which
            weight_list[total] = weight
            total = total + jnp.where(weight > 0, 1, 0)
        trios = (total - done + SIDE - 1) // SIDE
        if step < 2:
            trios = jnp.minimum(trios, CAPS[step])
        if step < part:
            done = jnp.minimum(done + trios * SIDE, total)
    for p in range(SIDE - 1):
        slot_list[total + p] = 0
        band_list[total + p] = 0
        weight_list[total + p] = 0

    def load_band(wanted, target, p):
        for place, (ref, at) in enumerate(bands):

            @pl.when(wanted == place)
            def _():
                target[p] = ref[at]

    lists = (slot_list, band_list, weight_list)
    solve_trios(done, trios, lists, load_band, tables, wave_refs, sum_refs, scratch)
    if part == 2:
        flat_field(sum_refs[1], out_refs[1], refs[6])


def far_kernel(total_ref, slot_list, band_list, weight_list, bands_ref, own_ref, mate_ref, *refs):
    tables, out_refs, refs = refs[:5], refs[5:7], refs[7:]
    buffer, wave_refs, sum_refs = refs[0], refs[1:3], (out_refs[0], refs[3])
    pitched_ref, scratch = refs[4], refs[5:]
    spread_waves(((own_ref, 0), (mate_ref, 0)), wave_refs)
    clear(sum_refs)

    def load_band(place, target, p):
        pltpu.sync_copy(bands_ref.at[place], buffer)
        target[p] = buffer[...]

    lists = (slot_list, band_list, weight_list)
    trios = (total_ref[0] + SIDE - 1) // SIDE
    solve_trios(0, trios, lists, load_band, tables, wave_refs, sum_refs, scratch)
    flat_field(sum_refs[1], out_refs[1], pitched_ref)


def flat_kernel(sum_ref, out_ref, pitched_ref):
    flat_field(sum_ref, out_ref, pitched_ref)


def finish_kernel(own_ref, part_ref, out_ref):
    def to_lanes(k, lanes):
        out_ref[0:1, lanes] = own_ref[k : k + 1, :] + part_ref[k : k + 1, :]

    unroll_rows(to_lanes)


VMEM_SPEC = pl.BlockSpec(memory_space=pltpu.VMEM)
SMEM_SPEC = pl.BlockSpec(memory_space=pltpu.SMEM)
ANY_SPEC = pl.BlockSpec(memory_space=pl.ANY)
PARAMS = pltpu.CompilerParams(vmem_limit_bytes=VMEM_LIMIT)


def solve_tables():
    basis, _, _ = real_basis()
    return [
        right_table(basis.T),
        right_table(basis),
        left_table(basis),
        left_table(basis.T),
        kernel_table(),
    ]


def solve_scratch():
    wide = [pltpu.VMEM((rows, LANES), F32) for rows in (LIVE, GX * PITCH, GX * PITCH)]
    return [pltpu.VMEM((SIDE, PACK, LANES), BF16)] + wide


def wide_of(rows):
    return jax.ShapeDtypeStruct((rows, LANES), F32)


def swap(values, axis, size, flip):
    return lax.ppermute(values, axis, [(i, i ^ flip) for i in range(size)])


def count_pairs(pair_list, pair_count, row_total, col_total):
    slots = pair_list.shape[1]
    live = lax.iota(jnp.int32, slots) < pair_count[0]
    first = pair_list[0, :, 0][:, None, None] == lax.iota(jnp.int32, col_total)[None, :, None]
    second = pair_list[0, :, 1][:, None, None] == lax.iota(jnp.int32, row_total)[None, None, :]
    return jnp.sum((first & second & live[:, None, None]).astype(F32), axis=0)


def pack_band(orbitals):
    return pl.pallas_call(
        pack_kernel,
        out_shape=jax.ShapeDtypeStruct((1, PACK, LANES), BF16),
        in_specs=[VMEM_SPEC],
        out_specs=VMEM_SPEC,
        scratch_shapes=[pltpu.VMEM((rows, LANES), F32) for rows in (FLAT_ROWS, PACK, 48)],
        compiler_params=PARAMS,
        name="pack_band",
    )(orbitals)


def list_counts(pair_list, pair_count):
    return pl.pallas_call(
        list_kernel,
        out_shape=jax.ShapeDtypeStruct((16, LANES), F32),
        in_specs=[VMEM_SPEC] * 2,
        out_specs=VMEM_SPEC,
        compiler_params=PARAMS,
        name="list_counts",
    )(jnp.swapaxes(pair_list, 1, 2), pair_count.reshape(1, 1))


def add_counts(packed, col_total, counts, mate_counts):
    return pl.pallas_call(
        functools.partial(count_kernel, col_total),
        out_shape=jax.ShapeDtypeStruct(packed.shape, BF16),
        in_specs=[VMEM_SPEC] * 3,
        out_specs=VMEM_SPEC,
        compiler_params=PARAMS,
        name="add_counts",
    )(packed, counts, mate_counts)


def flatten(sums):
    return pl.pallas_call(
        flat_kernel,
        out_shape=wide_of(FLAT),
        in_specs=[VMEM_SPEC],
        out_specs=VMEM_SPEC,
        scratch_shapes=[pltpu.VMEM((PITCHED, LANES), F32)],
        compiler_params=PARAMS,
        name="flatten",
    )(sums)


def finish(own, part):
    return pl.pallas_call(
        finish_kernel,
        out_shape=jax.ShapeDtypeStruct((1, LIVE * GX), F32),
        in_specs=[VMEM_SPEC] * 2,
        out_specs=VMEM_SPEC,
        compiler_params=PARAMS,
        name="add_parts",
    )(own, part)


NEAR = (8, 4)
STAGES = (
    (((0, 0),), ((4, 0),), ((2, 0),), ((1, 0),), ((0, 2),)),
    (((4, 2), (2, 2)), ((5, 0), (1, 2)), ((6, 0), (3, 0)), ((4, 1), (2, 1))),
    (((6, 2), (3, 2)), ((5, 2),), ((7, 0),), ((7, 2),)),
)
CAPS = (1, 2)
SHIFTED = ((4, 0), (2, 0), (4, 1), (2, 1))


def near_part(row_total, col_total, part, operands):
    places = 2 * sum(len(block) for stage in STAGES for block in stage) + SIDE
    out_shape = [wide_of(LIVE)] * 2
    if part == 0:
        out_shape = out_shape * 2
    if part == 2:
        out_shape = [wide_of(LIVE), wide_of(FLAT)]
    operands = list(operands)
    cost = pl.CostEstimate(flops=4 * 10**9, bytes_accessed=2 * 10**7, transcendentals=0)
    return pl.pallas_call(
        functools.partial(near_kernel, row_total, col_total, part),
        out_shape=out_shape,
        in_specs=[VMEM_SPEC] * len(operands),
        out_specs=[VMEM_SPEC] * len(out_shape),
        scratch_shapes=[
            pltpu.VMEM((8, LANES), jnp.int32),
            pltpu.SMEM((8, LANES), jnp.int32),
            pltpu.SMEM((places,), jnp.int32),
            pltpu.SMEM((places,), jnp.int32),
            pltpu.SMEM((places,), jnp.int32),
        ]
        + solve_scratch()
        + [pltpu.SemaphoreType.DMA]
        + ([pltpu.VMEM((rows, LANES), F32) for rows in (LIVE, PITCHED)] if part == 2 else []),
        compiler_params=PARAMS,
        cost_estimate=cost,
        name="solve_part",
    )(*operands)


def near_shards(row_total, col_total, orbitals, pair_list, pair_count):
    row_swap = lambda values, flip: swap(values, "row", row_total, flip)
    col_swap = lambda values, flip: swap(values, "col", col_total, flip)
    both = lambda a, b: jnp.concatenate([a, b], axis=0)

    def corner_swap(values):
        places = list(itertools.product(range(row_total), range(col_total)))
        at = lambda row, col: row * col_total + col
        pairs = [(at(row, col), at(row ^ 3, col)) for row, col in places]
        return lax.ppermute(values, ("row", "col"), pairs)

    counts = list_counts(pair_list, pair_count)
    own = add_counts(pack_band(orbitals), col_total, counts, col_swap(counts, 1))
    in_order = lambda *values: lax.optimization_barrier(values)
    mate, x, y, z, w = in_order(
        col_swap(own, 1), col_swap(own, 2), row_swap(own, 1), row_swap(own, 2), row_swap(own, 4)
    )
    w_z, w_x, w_y = in_order(both(w, z), both(w, x), both(w, y))
    over_x, over_y, over_z = col_swap(w_z, 2), row_swap(w_x, 1), row_swap(w_y, 2)
    tables = [jnp.asarray(table) for table in solve_tables()]
    blocks = [own, w, z, y, x]
    *waves, sum0, sum1 = near_part(row_total, col_total, 0, [*blocks, mate, *tables])
    w_z, sum0 = in_order(w_z, sum0)
    other, sum0, sum1, over_x, over_y, over_z = in_order(
        col_swap(w_z, 1), sum0, sum1, over_x, over_y, over_z
    )
    last = (
        col_swap(over_z, 2),
        row_swap(over_x[:1], 1),
        row_swap(over_y[:1], 2),
        corner_swap(over_x[:1]),
    )
    for part, arrived in enumerate(((over_x, over_y, over_z, other), last), 1):
        blocks += arrived
        operands = [*blocks, mate, *tables, *waves, sum0, sum1]
        sum0, sum1 = near_part(row_total, col_total, part, operands)
    return finish(flatten(sum0), col_swap(sum1, 1))


def far_shards(row_total, col_total, orbitals, pair_list, pair_count):
    counts = count_pairs(pair_list, pair_count, row_total, col_total)
    own = pack_band(orbitals)
    axes = ("row", "col")
    table = lax.all_gather(counts.reshape(-1), axes)
    table = table.reshape(row_total, col_total, col_total, row_total)
    wide = col_total // 2
    column = lax.all_gather(own[0], "row")
    columns = [column] + [swap(column, "col", col_total, 2 * x) for x in range(1, wide)]
    bands = jnp.concatenate(columns, axis=0)
    row = lax.axis_index("row")
    col = lax.axis_index("col")
    mine = jnp.stack([col, col ^ 1])
    other_col = ((col // 2) ^ lax.iota(jnp.int32, wide)) * 2 + col % 2
    other_row = lax.iota(jnp.int32, row_total)
    direct = table[row][other_col][:, mine]
    direct = jnp.transpose(direct, (1, 2, 0))
    mirror = table[:, :, :, row][:, mine][:, :, other_col]
    mirror = jnp.transpose(mirror, (1, 0, 2))
    same = (mine[:, None, None] == other_col[None, None, :]) & (other_row == row)[None, :, None]
    weights = (direct + jnp.where(same, 0.0, mirror)).astype(jnp.int32).reshape(-1)
    index = lax.iota(jnp.int32, weights.shape[0])
    order = jnp.argsort(jnp.where(weights > 0, 0, 1), stable=True)
    pad = lambda values: jnp.pad(values.astype(jnp.int32), (0, SIDE))
    slots = row_total * wide
    slot = order % slots
    band = (slot % wide) * row_total + slot // wide
    total = jnp.sum((weights > 0).astype(jnp.int32)).reshape(1)
    fields = pl.pallas_call(
        far_kernel,
        out_shape=[wide_of(LIVE), wide_of(FLAT)],
        in_specs=[SMEM_SPEC] * 4 + [ANY_SPEC] + [VMEM_SPEC] * 7,
        out_specs=[VMEM_SPEC] * 2,
        scratch_shapes=[pltpu.VMEM((PACK, LANES), BF16)]
        + [pltpu.VMEM((rows, LANES), F32) for rows in (LIVE, LIVE, LIVE, PITCHED)]
        + solve_scratch(),
        compiler_params=PARAMS,
        name="solve_pairs",
    )(
        total,
        pad(band),
        pad(order // slots),
        pad(weights[order]),
        bands,
        own,
        swap(own, "col", col_total, 1),
        *map(jnp.asarray, solve_tables()),
    )
    return finish(flatten(fields[0]), swap(fields[1], "col", col_total, 1))


def solution(mesh):
    row_total, col_total = mesh.shape["row"], mesh.shape["col"]
    near = (row_total, col_total) == NEAR
    shards = near_shards if near else far_shards
    return jax.shard_map(
        functools.partial(shards, row_total, col_total),
        mesh=mesh,
        in_specs=(P(("row", "col"), None), P(("row", "col"), None, None), P(("row", "col"))),
        out_specs=P(("row", "col"), None),
        check_vma=False,
    )
```

```python
import functools
import itertools

import jax
import jax.numpy as jnp
import ml_dtypes
import numpy as np
from jax import lax
from jax.experimental import pallas as pl
from jax.experimental.pallas import tpu as pltpu
from jax.sharding import PartitionSpec as P

GX = 40
LANES = 128
SIDE = 3
THIRD = GX // SIDE
PART = THIRD * GX
PACK = -(-PART // 16) * 16
LIVE = GX * GX
SPARE = SIDE * GX
LAST = LANES - SPARE
LAST_PARTS = GX // LAST
TABLE = 208
FLAT = LIVE * GX // LANES
CHUNK = PACK // 16
FLAT_ROWS = 512
PITCHED = LIVE // 16 * 17
DUO = 2 * GX
QUAD = 4 * GX
PITCH = GX + 1
VMEM_LIMIT = 16 * 1024 * 1024
screen_width = 0.9
F32 = jnp.float32
BF16 = jnp.bfloat16


def real_basis():
    half = GX // 2
    point = np.arange(GX)
    rows = [np.cos(2 * np.pi * (k * point % GX) / GX) for k in range(half + 1)]
    rows += [np.sin(2 * np.pi * (k * point % GX) / GX) for k in range(1, half)]
    frequency = np.concatenate([np.arange(half + 1), np.arange(1, half)])
    norm = np.where((frequency == 0) | (frequency == half), 1.0, 2.0) / GX
    return np.stack(rows), frequency, norm


def halves(table):
    high = table.astype(ml_dtypes.bfloat16)
    low = (table - high.astype(np.float64)).astype(ml_dtypes.bfloat16)
    return high, low


def left_table(table):
    high, low = halves(np.kron(np.eye(2), table))
    return np.concatenate([high, low, high], axis=1)


def right_table(table):
    wide = np.zeros((LANES, LANES))
    for p in range(SIDE):
        wide[p * GX : (p + 1) * GX, p * GX : (p + 1) * GX] = table
    high, low = halves(wide)
    both = np.concatenate([high, low], axis=1)
    return np.concatenate([both, both], axis=0)


def kernel_table():
    _, frequency, norm = real_basis()
    wave = frequency * (2.0 * np.pi / GX)
    squared = wave * wave
    total = squared[:, None, None] + squared[None, :, None] + squared[None, None, :]
    safe = np.where(total > 0, total, 1.0)
    screened = 4.0 * np.pi * (1.0 - np.exp(-safe / (4.0 * screen_width**2))) / safe
    kernel = np.where(total > 0, screened, np.pi / screen_width**2)
    kernel = kernel * norm[:, None, None] * norm[None, :, None] * norm[None, None, :]
    rows = np.swapaxes(kernel, 0, 1).reshape(LIVE, GX)
    out = np.zeros((LIVE, LANES), np.float32)
    for p in range(SIDE):
        out[:, p * GX : (p + 1) * GX] = rows
    return out


def dot(a, b):
    return jnp.dot(a, b, preferred_element_type=F32)


def split(values):
    high = values.astype(BF16)
    return high, (values - high.astype(F32)).astype(BF16)


def contract_rows(table, values):
    high, low = split(values)
    return dot(table, jnp.concatenate([high, high, low], axis=0))


def contract_lanes(values, table):
    both = dot(jnp.concatenate(split(values), axis=1), table)
    return both[:, :LANES] + both[:, LANES:]


def contract_lanes_by_two(values, table):
    count = values[0].shape[0]
    out = []
    for at in range(0, len(values), 2):
        both = contract_lanes(jnp.concatenate(values[at : at + 2], axis=0), table)
        out += [both[:count], both[count:]]
    return out


def fold(values):
    return jnp.concatenate([values[:DUO], values[DUO:]], axis=1)


def unfold(values):
    return jnp.concatenate([values[:, :LANES], values[:, LANES:]], axis=0)


def quad(step):
    return pl.ds(step * QUAD, QUAD)


def joined(planes):
    left = jnp.concatenate(planes[:2], axis=0)
    return jnp.concatenate([left, jnp.concatenate(planes[2:], axis=0)], axis=1)


def parted(values):
    return [
        values[i % 2 * GX : i % 2 * GX + GX, i // 2 * LANES : (i // 2 + 1) * LANES] for i in range(4)
    ]


def load_planes(ref, step):
    return joined([ref[pl.ds(step * 4 + i, GX, stride=PITCH), :] for i in range(4)])


def store_planes(ref, step, values):
    for i, plane in enumerate(parted(values)):
        ref[pl.ds(step * 4 + i, GX, stride=PITCH), :] = plane


def load_x_planes(ref, step):
    return joined([ref[pl.ds((step * 4 + i) * PITCH, GX), :] for i in range(4)])


def store_x_planes(ref, step, values):
    for i, plane in enumerate(parted(values)):
        ref[pl.ds((step * 4 + i) * PITCH, GX), :] = plane


def count_vector(pairs, live):
    slots = pairs.shape[1]
    row = lax.broadcasted_iota(jnp.int32, (16, slots), 0)
    lane = lax.broadcasted_iota(jnp.int32, (LANES, slots), 0) - SPARE
    first = (pairs[0:1] == row) & (lax.broadcasted_iota(jnp.int32, (16, slots), 1) < live)
    second = jnp.where(pairs[1:2] == lane, 1.0, 0.0)
    contract = (((1,), (1,)), ((), ()))
    return lax.dot_general(jnp.where(first, 1.0, 0.0), second, contract, preferred_element_type=F32)


def unroll_rows(copy):
    for k in range(FLAT):
        copy(k, slice(k * LANES, (k + 1) * LANES))


def pack_kernel(band_ref, out_ref, flat_ref, wide_ref, last_ref):
    def to_rows(k, lanes):
        flat_ref[k : k + 1, :] = band_ref[0:1, lanes].astype(F32)

    unroll_rows(to_rows)
    unused = FLAT_ROWS - FLAT
    flat_ref[FLAT:FLAT_ROWS, :] = jnp.zeros((unused, LANES), F32)
    lane = lax.broadcasted_iota(jnp.int32, (1, LANES), 1)

    def rows_of(first, count, target):
        group, q = divmod(first, 16)
        row, offset = divmod(q * GX, LANES)
        start = group * 5 + row
        values = flat_ref[pl.ds(start, count, stride=5), :]
        if offset + GX > LANES:
            after = flat_ref[pl.ds(start + 1, count, stride=5), :]
            values = jnp.where(lane >= offset, values, after)
        shift = (target - offset) % LANES
        return pltpu.roll(values, shift, 1) if shift else values

    for q in range(16):
        packed = jnp.zeros((CHUNK, LANES), F32)
        for third in range(SIDE):
            values = rows_of(third * PART + q, CHUNK, third * GX)
            packed = jnp.where(lane // GX == third, values, packed)
        wide_ref[pl.ds(q, CHUNK, stride=16), :] = packed
        last_ref[pl.ds(q, 3, stride=16), :] = rows_of(SIDE * PART + q, 3, 0)
    for part in range(LAST_PARTS):
        rows = slice(part * GX, (part + 1) * GX)
        values = pltpu.roll(last_ref[0:GX, :], SPARE - part * LAST, 1)
        wide_ref[rows, :] = jnp.where(lane >= SPARE, values, wide_ref[rows, :])
    out_ref[0] = wide_ref[...].astype(BF16)


def list_kernel(pairs_ref, live_ref, out_ref):
    out_ref[...] = count_vector(pairs_ref[0], live_ref[...])


def count_kernel(col_total, packed_ref, own_ref, mate_ref, out_ref):
    out_ref[...] = packed_ref[...]
    counts = own_ref[...] + pltpu.roll(mate_ref[...], col_total, 0)
    rows = slice(TABLE, TABLE + 16)
    out_ref[0, rows, :] = (packed_ref[0, rows, :].astype(F32) + counts).astype(BF16)


def spread(load, out_ref):
    lane = lax.broadcasted_iota(jnp.int32, (1, LANES), 1)
    for start in range(0, PACK, DUO):
        count = min(DUO, PACK - start)
        bands = [load(p, slice(start, start + count)).astype(F32) for p in range(SIDE)]
        count = min(count, PART - start)
        for third in range(SIDE):
            wide = jnp.zeros((count, LANES), F32)
            for p, values in enumerate(bands):
                shift = (p - third) * GX % LANES
                values = values[:count]
                values = pltpu.roll(values, shift, 1) if shift else values
                wide = jnp.where(lane // GX == p, values, wide)
            out_ref[third * PART + start : third * PART + start + count, :] = wide
    wide = jnp.zeros((GX, LANES), F32)
    for p in range(SIDE):
        band = load(p, slice(0, TABLE)).astype(F32)
        for part in range(LAST_PARTS):
            lanes = p * GX + part * LAST
            values = pltpu.roll(band[part * GX : (part + 1) * GX], (lanes - SPARE) % LANES, 1)
            wide = jnp.where((lane >= lanes) & (lane < lanes + LAST), values, wide)
    out_ref[SIDE * PART : LIVE, :] = wide


def spread_waves(band_refs, wave_refs):
    for (ref, at), wave_ref in zip(band_refs, wave_refs):
        spread(lambda p, rows: ref[at, rows, :], wave_ref)


def clear(sum_refs):
    for sum_ref in sum_refs:
        sum_ref[...] = jnp.zeros_like(sum_ref)


def lane_side():
    return lax.broadcasted_iota(jnp.int32, (1, LANES), 1) // GX


def solve_trios(first, count, lists, load_band, tables, wave_refs, sum_refs, scratch):
    z_ref, z_back_ref, row_ref, row_back_ref, kernel_ref = tables
    trio_ref, partner_ref, work_ref, work2_ref = scratch
    slot_list, band_list, weight_list = lists
    side = lane_side()

    def by_side(values):
        row = jnp.zeros((1, LANES), F32)
        for p in range(SIDE):
            row = jnp.where(side == p, values[p].astype(F32), row)
        return row

    def trio(at, carry):
        places = [first + at * SIDE + p for p in range(SIDE)]
        for p, place in enumerate(places):
            load_band(slot_list[place], trio_ref, p)
        bands = [band_list[place] for place in places]
        weights = [weight_list[place] for place in places]
        is_mate = by_side(bands) > 0.5
        scales = [
            by_side([jnp.where(bands[p] == which, weights[p], 0) for p in range(SIDE)])
            for which in range(2)
        ]
        spread(lambda p, rows: trio_ref[p, rows, :], partner_ref)

        steps = range(GX // 4)

        def forward():
            values = []
            for step in steps:
                wave = jnp.where(is_mate, wave_refs[1][quad(step), :], wave_refs[0][quad(step), :])
                values.append(partner_ref[quad(step), :] * wave)
            values = contract_lanes_by_two(values, z_ref[...])
            values = [contract_rows(row_ref[...], fold(v)) for v in values]
            for step, v in zip(steps, values):
                store_x_planes(work_ref, step, v)

        def across():
            values = [load_planes(work_ref, step) for step in steps]
            values = [contract_rows(row_ref[...], v) for v in values]
            values = [v * fold(kernel_ref[quad(step), :]) for step, v in zip(steps, values)]
            values = [contract_rows(row_back_ref[...], v) for v in values]
            for step, v in zip(steps, values):
                store_planes(work2_ref, step, v)

        def back():
            values = [load_x_planes(work2_ref, step) for step in steps]
            values = [unfold(contract_rows(row_back_ref[...], v)) for v in values]
            values = contract_lanes_by_two(values, z_back_ref[...])
            for step, v in zip(steps, values):
                v = v * partner_ref[quad(step), :]
                for sum_ref, scale in zip(sum_refs, scales):
                    sum_ref[quad(step), :] = sum_ref[quad(step), :] + v * scale

        for phase in (forward, across, back):
            phase()
        return carry

    lax.fori_loop(0, count, trio, 0)


def flat_field(sum_ref, out_ref, pitched_ref):
    lane = lax.broadcasted_iota(jnp.int32, (1, LANES), 1)
    rows = LIVE // 16
    for group in range(rows):
        pitched_ref[group * 17 : group * 17 + 16, :] = sum_ref[group * 16 : group * 16 + 16, :]
    flat = [jnp.zeros((rows, LANES), F32)] * 5
    for q in range(16):
        row, offset = divmod(q * GX, LANES)
        values = pitched_ref[pl.ds(q, rows, stride=17), :]
        moved = jnp.zeros((rows, LANES), F32)
        for p in range(SIDE):
            shift = (offset - p * GX) % LANES
            moved = moved + (pltpu.roll(values, shift, 1) if shift else values)
        flat[row] = jnp.where(lane >= offset, moved, flat[row])
        if offset + GX > LANES:
            flat[row + 1] = jnp.where(lane < offset + GX - LANES, moved, flat[row + 1])
    for row in range(5):
        out_ref[pl.ds(row, rows, stride=5), :] = flat[row]


def near_kernel(row_total, col_total, part, *refs):
    stages = STAGES[: part + 1]
    blocks = [block for stage in stages for block in stage]
    band_refs, refs = refs[: len(blocks)], refs[len(blocks) :]
    bands = [(ref, at) for ref, block in zip(band_refs, blocks) for at in range(len(block))]
    flips = [flip for block in blocks for flip in block]
    mate_ref, tables, refs = refs[0], refs[1:6], refs[6:]
    if part:
        wave_refs, given_refs, out_refs, refs = refs[:2], refs[2:4], refs[4:6], refs[6:]
    else:
        wave_refs, out_refs, refs = refs[:2], refs[2:4], refs[4:]
    (count_vmem, count_smem, slot_list, band_list, weight_list), refs = refs[:5], refs[5:]
    scratch, sem = refs[:4], refs[4]
    sum_refs = (out_refs[0], refs[5]) if part == 2 else out_refs

    lane = lax.broadcasted_iota(jnp.int32, (8, LANES), 1)
    counts = jnp.zeros((8, LANES), F32)
    for s, (ref, at) in enumerate(bands):
        spare = ref[at, TABLE : TABLE + 16, :].astype(F32)[0:8]
        shift = (s * row_total - SPARE) % LANES
        moved = pltpu.roll(spare, shift, 1) if shift else spare
        counts = jnp.where(lane // row_total == s, moved, counts)
    count_vmem[...] = counts.astype(jnp.int32)
    copy = pltpu.make_async_copy(count_vmem, count_smem, sem)
    copy.start()
    if part:
        for sum_ref, given_ref in zip(sum_refs, given_refs):
            sum_ref[...] = given_ref[...]
    else:
        clear(sum_refs)
        spread_waves(((band_refs[0], 0), (mate_ref, 0)), wave_refs)
    copy.wait()
    row = lax.axis_index("row")
    col = lax.axis_index("col")
    total = jnp.int32(0)
    done = jnp.int32(0)
    place = 0
    for step, stage in enumerate(stages):
        here = range(place, place + sum(len(block) for block in stage))
        place = here.stop
        for which, at in itertools.product(range(2), here):
            row_flip, col_flip = flips[at]
            row_place = flips.index((0, col_flip)) * row_total
            col_place = flips.index((row_flip, 0)) * row_total
            weight = count_smem[col ^ which, row_place + (row ^ row_flip)]
            if at or which:
                mirror = which * col_total + (col ^ col_flip)
                weight = weight + count_smem[mirror, col_place + row]
            slot_list[total] = at
            band_list[total] = which
            weight_list[total] = weight
            total = total + jnp.where(weight > 0, 1, 0)
        trios = (total - done + SIDE - 1) // SIDE
        if step < 2:
            trios = jnp.minimum(trios, CAPS[step])
        if step < part:
            done = jnp.minimum(done + trios * SIDE, total)
    for p in range(SIDE - 1):
        slot_list[total + p] = 0
        band_list[total + p] = 0
        weight_list[total + p] = 0

    def load_band(wanted, target, p):
        for place, (ref, at) in enumerate(bands):

            @pl.when(wanted == place)
            def _():
                target[p] = ref[at]

    lists = (slot_list, band_list, weight_list)
    solve_trios(done, trios, lists, load_band, tables, wave_refs, sum_refs, scratch)
    if part == 2:
        flat_field(sum_refs[1], out_refs[1], refs[6])


def far_kernel(total_ref, slot_list, band_list, weight_list, bands_ref, own_ref, mate_ref, *refs):
    tables, out_refs, refs = refs[:5], refs[5:7], refs[7:]
    buffer, wave_refs, sum_refs = refs[0], refs[1:3], (out_refs[0], refs[3])
    pitched_ref, scratch = refs[4], refs[5:]
    spread_waves(((own_ref, 0), (mate_ref, 0)), wave_refs)
    clear(sum_refs)

    def load_band(place, target, p):
        pltpu.sync_copy(bands_ref.at[place], buffer)
        target[p] = buffer[...]

    lists = (slot_list, band_list, weight_list)
    trios = (total_ref[0] + SIDE - 1) // SIDE
    solve_trios(0, trios, lists, load_band, tables, wave_refs, sum_refs, scratch)
    flat_field(sum_refs[1], out_refs[1], pitched_ref)


def flat_kernel(sum_ref, out_ref, pitched_ref):
    flat_field(sum_ref, out_ref, pitched_ref)


def finish_kernel(own_ref, part_ref, out_ref):
    def to_lanes(k, lanes):
        out_ref[0:1, lanes] = own_ref[k : k + 1, :] + part_ref[k : k + 1, :]

    unroll_rows(to_lanes)


VMEM_SPEC = pl.BlockSpec(memory_space=pltpu.VMEM)
SMEM_SPEC = pl.BlockSpec(memory_space=pltpu.SMEM)
ANY_SPEC = pl.BlockSpec(memory_space=pl.ANY)
PARAMS = pltpu.CompilerParams(vmem_limit_bytes=VMEM_LIMIT)


def solve_tables():
    basis, _, _ = real_basis()
    return [
        right_table(basis.T),
        right_table(basis),
        left_table(basis),
        left_table(basis.T),
        kernel_table(),
    ]


def solve_scratch():
    wide = [pltpu.VMEM((rows, LANES), F32) for rows in (LIVE, GX * PITCH, GX * PITCH)]
    return [pltpu.VMEM((SIDE, PACK, LANES), BF16)] + wide


def wide_of(rows):
    return jax.ShapeDtypeStruct((rows, LANES), F32)


def swap(values, axis, size, flip):
    return lax.ppermute(values, axis, [(i, i ^ flip) for i in range(size)])


def count_pairs(pair_list, pair_count, row_total, col_total):
    slots = pair_list.shape[1]
    live = lax.iota(jnp.int32, slots) < pair_count[0]
    first = pair_list[0, :, 0][:, None, None] == lax.iota(jnp.int32, col_total)[None, :, None]
    second = pair_list[0, :, 1][:, None, None] == lax.iota(jnp.int32, row_total)[None, None, :]
    return jnp.sum((first & second & live[:, None, None]).astype(F32), axis=0)


def pack_band(orbitals):
    return pl.pallas_call(
        pack_kernel,
        out_shape=jax.ShapeDtypeStruct((1, PACK, LANES), BF16),
        in_specs=[VMEM_SPEC],
        out_specs=VMEM_SPEC,
        scratch_shapes=[pltpu.VMEM((rows, LANES), F32) for rows in (FLAT_ROWS, PACK, 48)],
        compiler_params=PARAMS,
        name="pack_band",
    )(orbitals)


def list_counts(pair_list, pair_count):
    return pl.pallas_call(
        list_kernel,
        out_shape=jax.ShapeDtypeStruct((16, LANES), F32),
        in_specs=[VMEM_SPEC] * 2,
        out_specs=VMEM_SPEC,
        compiler_params=PARAMS,
        name="list_counts",
    )(jnp.swapaxes(pair_list, 1, 2), pair_count.reshape(1, 1))


def add_counts(packed, col_total, counts, mate_counts):
    return pl.pallas_call(
        functools.partial(count_kernel, col_total),
        out_shape=jax.ShapeDtypeStruct(packed.shape, BF16),
        in_specs=[VMEM_SPEC] * 3,
        out_specs=VMEM_SPEC,
        compiler_params=PARAMS,
        name="add_counts",
    )(packed, counts, mate_counts)


def flatten(sums):
    return pl.pallas_call(
        flat_kernel,
        out_shape=wide_of(FLAT),
        in_specs=[VMEM_SPEC],
        out_specs=VMEM_SPEC,
        scratch_shapes=[pltpu.VMEM((PITCHED, LANES), F32)],
        compiler_params=PARAMS,
        name="flatten",
    )(sums)


def finish(own, part):
    return pl.pallas_call(
        finish_kernel,
        out_shape=jax.ShapeDtypeStruct((1, LIVE * GX), F32),
        in_specs=[VMEM_SPEC] * 2,
        out_specs=VMEM_SPEC,
        compiler_params=PARAMS,
        name="add_parts",
    )(own, part)


NEAR = (8, 4)
STAGES = (
    (((0, 0),), ((4, 0),), ((2, 0),), ((1, 0),), ((0, 2),)),
    (((4, 2), (2, 2)), ((5, 0), (1, 2)), ((6, 0), (3, 0))),
    (((6, 2), (3, 2)), ((5, 2),), ((7, 0),), ((7, 2),)),
)
CAPS = (1, 2)


def near_part(row_total, col_total, part, operands):
    places = 2 * row_total * (col_total // 2) + SIDE
    out_shape = [wide_of(LIVE)] * 2
    if part == 0:
        out_shape = out_shape * 2
    if part == 2:
        out_shape = [wide_of(LIVE), wide_of(FLAT)]
    operands = list(operands)
    cost = pl.CostEstimate(flops=4 * 10**9, bytes_accessed=2 * 10**7, transcendentals=0)
    return pl.pallas_call(
        functools.partial(near_kernel, row_total, col_total, part),
        out_shape=out_shape,
        in_specs=[VMEM_SPEC] * len(operands),
        out_specs=[VMEM_SPEC] * len(out_shape),
        scratch_shapes=[
            pltpu.VMEM((8, LANES), jnp.int32),
            pltpu.SMEM((8, LANES), jnp.int32),
            pltpu.SMEM((places,), jnp.int32),
            pltpu.SMEM((places,), jnp.int32),
            pltpu.SMEM((places,), jnp.int32),
        ]
        + solve_scratch()
        + [pltpu.SemaphoreType.DMA]
        + ([pltpu.VMEM((rows, LANES), F32) for rows in (LIVE, PITCHED)] if part == 2 else []),
        compiler_params=PARAMS,
        cost_estimate=cost,
        name="solve_part",
    )(*operands)


def near_shards(row_total, col_total, orbitals, pair_list, pair_count):
    row_swap = lambda values, flip: swap(values, "row", row_total, flip)
    col_swap = lambda values, flip: swap(values, "col", col_total, flip)
    both = lambda a, b: jnp.concatenate([a, b], axis=0)

    def corner_swap(values):
        places = list(itertools.product(range(row_total), range(col_total)))
        at = lambda row, col: row * col_total + col
        pairs = [(at(row, col), at(row ^ 3, col)) for row, col in places]
        return lax.ppermute(values, ("row", "col"), pairs)

    counts = list_counts(pair_list, pair_count)
    own = add_counts(pack_band(orbitals), col_total, counts, col_swap(counts, 1))
    in_order = lambda *values: lax.optimization_barrier(values)
    mate, x, y, z, w = in_order(
        col_swap(own, 1), col_swap(own, 2), row_swap(own, 1), row_swap(own, 2), row_swap(own, 4)
    )
    w_z, w_x, w_y = in_order(both(w, z), both(w, x), both(w, y))
    over_x, over_y, over_z = col_swap(w_z, 2), row_swap(w_x, 1), row_swap(w_y, 2)
    tables = [jnp.asarray(table) for table in solve_tables()]
    blocks = [own, w, z, y, x]
    *waves, sum0, sum1 = near_part(row_total, col_total, 0, [*blocks, mate, *tables])
    sum0, sum1, over_x, over_y, over_z = in_order(sum0, sum1, over_x, over_y, over_z)
    last = (
        col_swap(over_z, 2),
        row_swap(over_x[:1], 1),
        row_swap(over_y[:1], 2),
        corner_swap(over_x[:1]),
    )
    for part, arrived in enumerate(((over_x, over_y, over_z), last), 1):
        blocks += arrived
        operands = [*blocks, mate, *tables, *waves, sum0, sum1]
        sum0, sum1 = near_part(row_total, col_total, part, operands)
    return finish(flatten(sum0), col_swap(sum1, 1))


def far_shards(row_total, col_total, orbitals, pair_list, pair_count):
    counts = count_pairs(pair_list, pair_count, row_total, col_total)
    own = pack_band(orbitals)
    axes = ("row", "col")
    table = lax.all_gather(counts.reshape(-1), axes)
    table = table.reshape(row_total, col_total, col_total, row_total)
    wide = col_total // 2
    column = lax.all_gather(own[0], "row")
    columns = [column] + [swap(column, "col", col_total, 2 * x) for x in range(1, wide)]
    bands = jnp.concatenate(columns, axis=0)
    row = lax.axis_index("row")
    col = lax.axis_index("col")
    mine = jnp.stack([col, col ^ 1])
    other_col = ((col // 2) ^ lax.iota(jnp.int32, wide)) * 2 + col % 2
    other_row = lax.iota(jnp.int32, row_total)
    direct = table[row][other_col][:, mine]
    direct = jnp.transpose(direct, (1, 2, 0))
    mirror = table[:, :, :, row][:, mine][:, :, other_col]
    mirror = jnp.transpose(mirror, (1, 0, 2))
    same = (mine[:, None, None] == other_col[None, None, :]) & (other_row == row)[None, :, None]
    weights = (direct + jnp.where(same, 0.0, mirror)).astype(jnp.int32).reshape(-1)
    index = lax.iota(jnp.int32, weights.shape[0])
    order = jnp.argsort(jnp.where(weights > 0, 0, 1), stable=True)
    pad = lambda values: jnp.pad(values.astype(jnp.int32), (0, SIDE))
    slots = row_total * wide
    slot = order % slots
    band = (slot % wide) * row_total + slot // wide
    total = jnp.sum((weights > 0).astype(jnp.int32)).reshape(1)
    fields = pl.pallas_call(
        far_kernel,
        out_shape=[wide_of(LIVE), wide_of(FLAT)],
        in_specs=[SMEM_SPEC] * 4 + [ANY_SPEC] + [VMEM_SPEC] * 7,
        out_specs=[VMEM_SPEC] * 2,
        scratch_shapes=[pltpu.VMEM((PACK, LANES), BF16)]
        + [pltpu.VMEM((rows, LANES), F32) for rows in (LIVE, LIVE, LIVE, PITCHED)]
        + solve_scratch(),
        compiler_params=PARAMS,
        name="solve_pairs",
    )(
        total,
        pad(band),
        pad(order // slots),
        pad(weights[order]),
        bands,
        own,
        swap(own, "col", col_total, 1),
        *map(jnp.asarray, solve_tables()),
    )
    return finish(flatten(fields[0]), swap(fields[1], "col", col_total, 1))


def solution(mesh):
    row_total, col_total = mesh.shape["row"], mesh.shape["col"]
    near = (row_total, col_total) == NEAR
    shards = near_shards if near else far_shards
    return jax.shard_map(
        functools.partial(shards, row_total, col_total),
        mesh=mesh,
        in_specs=(P(("row", "col"), None), P(("row", "col"), None, None), P(("row", "col"))),
        out_specs=P(("row", "col"), None),
        check_vma=False,
    )
```
